32 devices in a mesh: dp: 8 (over z, core), tensor: 4 (over y, x).
Axes of the slice: x: 2, y: 2, z: 4, core: 2. Of those that a mesh axis runs over, the one named last changes fastest.
Arguments:
- tokens: bfloat16 [4096, 2048], P(('dp', 'tensor')), may hold values from -6 to 6
- lengths: int32 [8, 8], P('dp'), may hold values from 1 to 128, 512 in all within a row
- group_prefix: int32 [8], replicated, may hold values from 0 to 7, as said below
- prefix_cache: bfloat16 [32768, 512], P(('dp', 'tensor')), may hold values from -340 to 340
- query_weight: bfloat16 [2048, 1024], P(None, 'tensor'), may hold values from -0.125 to 0.125
- key_weight: bfloat16 [2048, 256], replicated, may hold values from -0.375 to 0.375
- value_weight: bfloat16 [2048, 256], replicated, may hold values from -0.125 to 0.125
- out_weight: bfloat16 [1024, 2048], P('tensor'), may hold values from -0.1875 to 0.1875
- gate_up_weight: bfloat16 [2, 2048, 5120], P(None, None, 'tensor'), may hold values from -0.125 to 0.125
- down_weight: bfloat16 [5120, 2048], P('tensor'), may hold values from -0.078125 to 0.078125
Outputs:
- layer_out: bfloat16 [4096, 2048], P(('dp', 'tensor'))
The draws below stay inside these ranges and needn't reach their ends.
Inputs may be any that keep to these rules, and one draw needn't show every extreme that they name: The 8 lengths of a group sum to 512, and one of them is exactly 128. `group_prefix`: several groups may continue the same slot.
All inputs are finite; a program needn't handle non-finite values.
Results may differ from the reference program's by a relative error of at most 0.023.
Values may be sent and summed in bfloat16 or wider, within the bound.
A program may use at most 128 MiB of HBM per device.

```python
import math
import jax
import jax.numpy as jnp
import numpy as np
from jax import lax

D = 2048
QH = 16
KVH = 4
HD = 64
FF = 5120
REQS = 8
TOK_G = 512
PLEN = 4096
MOSTLEN = 128
TOKENS = 4096
QW = 1024
KW = 256
N_DP = 8
N_TENSOR = 4


def draw_group_prefix(key, part):
    key_slots, key_order = jax.random.split(key)
    slots = jax.random.randint(key_slots, (N_DP,), 0, N_DP)
    order = jax.random.permutation(key_order, N_DP)
    slots = slots.at[order[0]].set(0)
    slots = slots.at[order[1]].set(N_DP - 1)
    slots = slots.at[order[2]].set((order[2] + N_DP - 1) % N_DP)
    slots = slots.at[order[3]].set((order[3] + 1) % N_DP)
    return slots.astype(jnp.int32)


def draw_prefix_cache(key, part):
    row_total = N_DP * PLEN
    kv_total = KVH * HD
    key_noise = jax.random.fold_in(key, 0)
    key_vals = jax.random.fold_in(key, 3)
    keys_part = jnp.clip(3.0 * jax.random.normal(key_noise, (row_total, kv_total), jnp.float32), -18.0, 18.0)
    values_part = jnp.clip(jax.random.normal(key_vals, (row_total, kv_total), jnp.float32), -6.0, 6.0)
    return jnp.concatenate([keys_part, values_part], axis=1).astype(jnp.bfloat16)


def block_levels(key, dims, shards, least, top_value):
    def one(position, parts):
        draws = jax.random.uniform(jax.random.fold_in(jax.random.fold_in(key, 6), position), (parts,), jnp.float32, least / len(shards), top_value / len(shards))
        return jnp.repeat(jnp.exp(draws), dims[position] // parts).reshape((-1,) + (1,) * (len(dims) - position - 1))

    loudness = one(*shards[0])
    for cut in shards[1:]:
        loudness = loudness * one(*cut)
    return loudness


def length_profile(count, total, limit, skew):
    loads = [(1 << 20) // math.isqrt(standing ** skew) + 1 for standing in range(2, count + 1)]
    spare, counts = total - limit - (count - 1), [1] * (count - 1)
    while spare > 0:
        movable = [i for i in range(count - 1) if counts[i] < limit]
        whole, left = sum([loads[i] for i in movable]), spare
        for i in movable:
            addition = min(limit - counts[i], max(1, left * loads[i] // whole), spare)
            counts[i] = counts[i] + addition
            spare = spare - addition
    return np.array([limit] + counts)


def ragged_sizes(key, number_of, total, reach, skew):
    if number_of == 2:
        one = jax.random.randint(key, (), max(1, total - reach), min(reach, total - 1) + 1)
        return jnp.stack([one, total - one])
    sizes = jnp.asarray(length_profile(number_of, total, reach, skew), jnp.int32)
    pairs = (number_of - 1) // 2
    source_of, taker = sizes[1:1 + 2 * pairs:2], sizes[2:2 + 2 * pairs:2]
    margin = jnp.minimum(source_of - 1, reach - taker)
    passed = jax.random.randint(jax.random.fold_in(key, 1), (pairs,), 0, 1 << 20) % (margin + 1)
    sizes = sizes.at[1:1 + 2 * pairs:2].set(source_of - passed).at[2:2 + 2 * pairs:2].set(taker + passed)
    return sizes[jax.random.permutation(jax.random.fold_in(key, 2), number_of)]


def noise(own_key, dims, width, limit, cuts=(), held_as=jnp.bfloat16):
    result = width * jax.random.normal(own_key, dims, jnp.float32)
    if cuts:
        result = result * block_levels(own_key, dims, cuts, -0.22, 0.18)
    return jnp.clip(result, -limit, limit).astype(held_as)


def setup_inputs(seed: int = 0) -> dict:
    seeds = jax.random.split(jax.random.key(seed), 11)
    tokens = noise(seeds[0], (TOKENS, D), 1.0, 6.0, ((0, 32),))
    lengths = jax.vmap(lambda own: ragged_sizes(own, REQS, TOK_G, MOSTLEN, 2))(jax.random.split(seeds[1], N_DP)).reshape((N_DP, REQS)).astype(jnp.int32)
    group_prefix = draw_group_prefix(jax.random.fold_in(seeds[10], 71), 0)
    prefix_cache = draw_prefix_cache(jax.random.fold_in(seeds[10], 71), 0)
    query_weight = noise(seeds[4], (D, QW), D ** -0.5, 0.125, ((1, 4),))
    key_weight = noise(seeds[5], (D, KW), (D // 9) ** -0.5, 0.375)
    value_weight = noise(seeds[6], (D, KW), D ** -0.5, 0.125)
    out_weight = noise(seeds[7], (QW, D), QW ** -0.5, 0.1875, ((0, 4),))
    gate_up_weight = noise(seeds[8], (2, D, FF), D ** -0.5, 0.125, ((2, 4),))
    down_weight = noise(seeds[9], (FF, D), FF ** -0.5, 0.078125, ((0, 4),))
    return {"tokens": tokens, "lengths": lengths, "group_prefix": group_prefix, "prefix_cache": prefix_cache, "query_weight": query_weight, "key_weight": key_weight, "value_weight": value_weight, "out_weight": out_weight, "gate_up_weight": gate_up_weight, "down_weight": down_weight}


NEG_FILL = -1e+30

def token_layout(lengths, total_rows):
    ends_at = jnp.cumsum(lengths).astype(jnp.int32)
    starts_at = (ends_at - lengths).astype(jnp.int32)
    indices = jnp.arange(total_rows, dtype=jnp.int32)
    request = lax.optimization_barrier(jnp.sum((indices[:, None] >= ends_at[None, :]).astype(jnp.int32), axis=1)).astype(jnp.int32)
    begins = lax.optimization_barrier(jnp.max(jnp.where(starts_at[None, :] <= indices[:, None], starts_at[None, :], 0), axis=1)).astype(jnp.int32)
    return ((PLEN + indices - begins).astype(jnp.float32), request)

def rope_tables(positions):
    halves = HD // 2
    steps_float = jnp.arange(halves, dtype=jnp.float32)
    inverse = jnp.exp(steps_float * (-2.0 * math.log(10000.0) / HD))
    angles = positions[:, None] * inverse[None, :]
    return (jnp.cos(angles), jnp.sin(angles))

def rotate(values, cos_table, sin_table):
    halves = values.shape[-1] // 2
    former = values[..., :halves]
    latter = values[..., halves:]
    cos_rows = cos_table[:, None, :]
    sin_rows = sin_table[:, None, :]
    return jnp.concatenate([former * cos_rows - latter * sin_rows, latter * cos_rows + former * sin_rows], axis=-1)

def norm_rows(inputs):
    floats = inputs.astype(jnp.float32)
    return (floats * lax.rsqrt(lax.optimization_barrier(jnp.mean(floats * floats, axis=-1, keepdims=True)) + 1e-05)).astype(jnp.bfloat16)

def reference(tokens, lengths, group_prefix, prefix_cache, query_weight, key_weight, value_weight, out_weight, gate_up_weight, down_weight):
    scaling = 1.0 / math.sqrt(HD)
    head_ratio = QH // KVH
    token_groups = tokens.reshape(N_DP, TOK_G, D)

    def one_group(inputs):
        group_tokens, group_lengths, slot = inputs
        positions, request = token_layout(group_lengths, TOK_G)
        cos_table, sin_table = rope_tables(positions)
        normed = norm_rows(group_tokens)
        queries = jnp.dot(normed, query_weight, preferred_element_type=jnp.float32).reshape(TOK_G, QH, HD)
        queries = rotate(queries, cos_table, sin_table).astype(jnp.bfloat16)
        new_keys = jnp.dot(normed, key_weight, preferred_element_type=jnp.float32).reshape(TOK_G, KVH, HD)
        new_keys = rotate(new_keys, cos_table, sin_table).astype(jnp.bfloat16)
        new_values = jnp.dot(normed, value_weight, preferred_element_type=jnp.float32).astype(jnp.bfloat16).reshape(TOK_G, KVH, HD)
        cached = lax.dynamic_slice_in_dim(prefix_cache, (slot * PLEN).astype(jnp.int32), PLEN, 0)
        all_keys = jnp.concatenate([cached[:, :KW].reshape(PLEN, KVH, HD), new_keys], axis=0)
        all_values = jnp.concatenate([cached[:, KW:].reshape(PLEN, KVH, HD), new_values], axis=0)
        indices = jnp.arange(TOK_G, dtype=jnp.int32)
        own_seen = (request[:, None] == request[None, :]) & (indices[None, :] <= indices[:, None])
        allowed = jnp.concatenate([jnp.ones((TOK_G, PLEN), dtype=bool), own_seen], axis=1)

        def one_head(head):
            kv_index = (head // head_ratio).astype(jnp.int32)
            query_head = lax.dynamic_index_in_dim(queries, head, axis=1, keepdims=False)
            key_head = lax.dynamic_index_in_dim(all_keys, kv_index, axis=1, keepdims=False)
            value_head = lax.dynamic_index_in_dim(all_values, kv_index, axis=1, keepdims=False)
            scores = jnp.dot(query_head, key_head.T, preferred_element_type=jnp.float32) * scaling
            scores = jnp.where(allowed, scores, NEG_FILL)
            top_score = lax.optimization_barrier(jnp.max(scores, axis=1, keepdims=True))
            exponent = jnp.exp(scores - top_score)
            total_weight = lax.optimization_barrier(jnp.sum(exponent, axis=1, keepdims=True))
            blended = jnp.dot(exponent.astype(jnp.bfloat16), value_head, preferred_element_type=jnp.float32)
            return (blended / total_weight).astype(jnp.bfloat16)
        heads_out = lax.map(one_head, jnp.arange(QH, dtype=jnp.int32))
        attended = jnp.transpose(heads_out, (1, 0, 2)).reshape(TOK_G, QW)
        grouped = attended.reshape(TOK_G, N_TENSOR, QW // N_TENSOR).astype(jnp.float32)
        out_groups = out_weight.reshape(N_TENSOR, QW // N_TENSOR, D).astype(jnp.float32)
        partials = jnp.einsum('tgk,gkd->gtd', grouped, out_groups).astype(jnp.bfloat16)
        partials = lax.optimization_barrier(partials)
        attn_sum = lax.optimization_barrier(jnp.sum(partials.astype(jnp.float32), axis=0))
        middle = (group_tokens.astype(jnp.float32) + attn_sum).astype(jnp.bfloat16)
        middle_normed = norm_rows(middle)
        gate_value = jnp.dot(middle_normed, gate_up_weight[0], preferred_element_type=jnp.float32)
        upward = jnp.dot(middle_normed, gate_up_weight[1], preferred_element_type=jnp.float32)
        hidden = (jax.nn.silu(gate_value) * upward).astype(jnp.bfloat16)
        hidden_groups = hidden.reshape(TOK_G, N_TENSOR, FF // N_TENSOR).astype(jnp.float32)
        down_groups = down_weight.reshape(N_TENSOR, FF // N_TENSOR, D).astype(jnp.float32)
        ffn_parts = jnp.einsum('tgk,gkd->gtd', hidden_groups, down_groups).astype(jnp.bfloat16)
        ffn_parts = lax.optimization_barrier(ffn_parts)
        ffn_sum = lax.optimization_barrier(jnp.sum(ffn_parts.astype(jnp.float32), axis=0))
        return (middle.astype(jnp.float32) + ffn_sum).astype(jnp.bfloat16)
    outputs = lax.map(one_group, (token_groups, lengths, group_prefix))
    return outputs.reshape(TOKENS, D)
```

```python
import functools
import math

import jax
import jax.numpy as jnp
from jax import lax
from jax.experimental import pallas as pl
from jax.experimental.pallas import tpu as pltpu
from jax.sharding import PartitionSpec as P

QH = 16
KVH = 4
HD = 64
PLEN = 4096
LANES = 128
NEG_FILL = -1e30
VMEM = pl.BlockSpec(memory_space=pltpu.VMEM)
SMEM = pl.BlockSpec(memory_space=pltpu.SMEM)
ANY = pl.BlockSpec(memory_space=pl.ANY)
MESH = pl.DeviceIdType.MESH
BF16 = jnp.bfloat16
F32 = jnp.float32
MIB = 1 << 20


def norm_rows(inputs):
    floats = inputs.astype(F32)
    mean = jnp.mean(floats * floats, axis=-1, keepdims=True)
    return (floats * lax.rsqrt(mean + 1e-05)).astype(BF16)


def token_layout(lengths, total_rows):
    ends_at = jnp.cumsum(lengths)
    starts_at = ends_at - lengths
    indices = jnp.arange(total_rows, dtype=jnp.int32)
    begins = jnp.max(
        jnp.where(starts_at[None, :] <= indices[:, None], starts_at[None, :], 0), axis=1
    )
    return ((PLEN + indices - begins).astype(F32), begins)


def rope_tables(positions):
    halves = HD // 2
    steps_float = jnp.arange(halves, dtype=F32)
    inverse = jnp.exp(steps_float * (-2.0 * math.log(10000.0) / HD))
    angles = positions[:, None] * inverse[None, :]
    return (jnp.cos(angles), jnp.sin(angles))


def route_tables(group_prefix, chips):
    slots = jnp.arange(2 * chips, dtype=jnp.int32)
    chip = jnp.arange(chips, dtype=jnp.int32)
    wanted = group_prefix[None, :] == slots[:, None]
    group_chip = slots // 2
    beyond = group_chip[None, None, :] > chip[:, None, None]
    before = group_chip[None, None, :] < chip[:, None, None]
    right = jnp.any(wanted[None] & beyond, axis=2) & (group_chip[None, :] <= chip[:, None])
    left = jnp.any(wanted[None] & before, axis=2) & (group_chip[None, :] >= chip[:, None])
    earlier = slots[None, :] < slots[:, None]

    def ranks(need):
        return jnp.sum((need[:, None, :] & earlier[None]).astype(jnp.int32), axis=2)

    most = jnp.maximum(
        jnp.max(jnp.sum(right.astype(jnp.int32), axis=1)),
        jnp.max(jnp.sum(left.astype(jnp.int32), axis=1)),
    )
    return right, ranks(right), left, ranks(left), most


def route_choice(group_prefix, tables, group, chips, width):
    right, right_rank, left, left_rank, _ = tables
    chip, core = group // 2, group % 2
    slots = jnp.arange(2 * chips, dtype=jnp.int32)
    own = slots // 2 == chip
    from_left = 2 + right_rank[jnp.maximum(chip - 1, 0)]
    from_right = 2 + left_rank[jnp.minimum(chip + 1, chips - 1)]
    held_right = jnp.where(own, slots % 2, from_left)
    held_left = jnp.where(own, slots % 2, from_right)
    final = jnp.where(
        own, slots % 2, jnp.where(slots < 2 * chip, from_left, 2 * width + from_right)
    )
    wanted = slots == group_prefix[group]
    choices = [jnp.sum(jnp.where(wanted, final, 0))]
    places = jnp.arange(width, dtype=jnp.int32) * 2 + core
    for need, rank, held in (
        (right[chip], right_rank[chip], held_right),
        (left[chip], left_rank[chip], held_left),
    ):
        hit = need[None, :] & (rank[None, :] == places[:, None])
        choices.append(jnp.sum(jnp.where(hit, held[None, :], 0), axis=1))
    return jnp.concatenate([choices[0][None], choices[1], choices[2]]).astype(jnp.int32)


def pick(number, candidates):
    result = candidates[0]
    for i in range(1, len(candidates)):
        result = jnp.where(number == i, candidates[i], result)
    return result


def gather_kernel(
    parts, chips, width, sub,
    choice, tokens, prefix, segment, kv_out,
    packed, own, held_l, held_r, stage_r, stage_l, ag,
    ag_send, ag_recv, a2a_send, a2a_recv, own_send, own_recv,
    r_send, r_recv, l_send, l_recv, rf_send, rf_recv, lf_send, lf_recv,
):
    me = lax.axis_index("tensor")
    group = lax.axis_index("dp")
    chip, core = group // 2, group % 2
    other = 1 - core
    sibling = chip * 2 + other
    groups = 2 * chips
    chunks = parts * sub
    chunk_rows = prefix.shape[0] // sub

    barrier = pltpu.get_barrier_semaphore()
    for d in range(1, parts):
        pl.semaphore_signal(
            barrier, inc=1, device_id={"tensor": lax.rem(me + d, parts)}, device_id_type=MESH
        )
    near = (sibling, lax.rem(group + 2, groups), lax.rem(group + groups - 2, groups))
    for to in near:
        pl.semaphore_signal(barrier, inc=1, device_id={"dp": to}, device_id_type=MESH)

    rows_i = lax.broadcasted_iota(jnp.int32, (2 * KVH * HD, LANES), 0)
    cols_i = lax.broadcasted_iota(jnp.int32, (2 * KVH * HD, LANES), 1)
    source = cols_i + jnp.where(cols_i >= HD, KVH * HD - HD, 0)
    for h in range(KVH):
        take = (rows_i == source + h * HD).astype(F32).astype(BF16)
        packed[h] = (
            jnp.dot(prefix[...], take, preferred_element_type=F32)
            .astype(BF16)
            .reshape(sub, chunk_rows, LANES)
        )
    pl.semaphore_wait(barrier, parts - 1 + 3)

    copies = []
    for d in range(parts - 1, 0, -1):
        to = lax.rem(me + d, parts)
        copy = pltpu.make_async_remote_copy(
            src_ref=packed.at[to * KVH // parts],
            dst_ref=own.at[core, pl.ds((parts - d) * sub, sub)],
            send_sem=a2a_send.at[parts - d],
            recv_sem=a2a_recv.at[parts - d],
            device_id={"tensor": to},
            device_id_type=MESH,
        )
        copy.start()
        copies.append(copy)
    own[core, 0:sub] = packed[me * KVH // parts]

    ag[0] = norm_rows(tokens[...])
    ag_copies = []
    for d in range(1, parts):
        copy = pltpu.make_async_remote_copy(
            src_ref=ag.at[0],
            dst_ref=ag.at[d],
            send_sem=ag_send.at[d],
            recv_sem=ag_recv.at[d],
            device_id={"tensor": lax.rem(me + d, parts)},
            device_id_type=MESH,
        )
        copy.start()
        ag_copies.append(copy)

    def lane_copy(src, dst, send_sem, recv_sem, to):
        return pltpu.make_async_remote_copy(
            src_ref=src, dst_ref=dst, send_sem=send_sem, recv_sem=recv_sem,
            device_id={"dp": to}, device_id_type=MESH,
        )

    def own_copy(m):
        block = own.at[core, pl.ds(m * sub, sub)]
        return lane_copy(block, block, own_send.at[m], own_recv.at[m], sibling)

    def flow(k, has_from, has_to, to, base, held, stage, send, recv, f_send, f_recv):
        def hop(w):
            return lane_copy(
                stage.at[w, k], held.at[w * 2 + core, k], send.at[w, k], recv.at[w, k], to
            )

        def forward(w):
            ref = held.at[w * 2 + core, k]
            return lane_copy(ref, ref, f_send.at[w, k], f_recv.at[w, k], sibling)

        @pl.when(has_from)
        def _():
            for w in range(width):
                hop(w).wait_recv()
                forward(w).start()
            for w in range(width):
                forward(w).wait_recv()

        @pl.when(has_to)
        def _():
            for w in range(width):
                stage[w, k] = pick(
                    choice[base + w],
                    [own[0, k], own[1, k]] + [held[i, k] for i in range(2 * width)],
                )
                hop(w).start()

    last = chips - 1

    def step(s, carry):
        m = s // sub

        @pl.when((m < parts) & (s % sub == 0))
        def _():
            @pl.when(m > 0)
            def _():
                pltpu.make_async_remote_copy(
                    src_ref=packed.at[0],
                    dst_ref=own.at[core, pl.ds(m * sub, sub)],
                    send_sem=a2a_send.at[m],
                    recv_sem=a2a_recv.at[m],
                    device_id={"tensor": lax.rem(me + 1, parts)},
                    device_id_type=MESH,
                ).wait_recv()

            own_copy(m).start()
            own_copy(m).wait_recv()

        k = s - chip

        @pl.when((k >= 0) & (k < chunks))
        def _():
            flow(
                k, chip > 0, chip < last, lax.rem(group + 2, groups), 1,
                held_l, stage_r, r_send, r_recv, rf_send, rf_recv,
            )

        j = s - (last - chip)

        @pl.when((j >= 0) & (j < chunks))
        def _():
            flow(
                j, chip < last, chip > 0, lax.rem(group + groups - 2, groups), 1 + width,
                held_r, stage_l, l_send, l_recv, lf_send, lf_recv,
            )

        return carry

    for edge in ((chip == 0, held_l), (chip == last, held_r)):
        def clear(ref=edge[1]):
            ref[...] = jnp.zeros_like(ref)
        pl.when(edge[0])(clear)

    lax.fori_loop(0, chunks + last, step, 0)

    def finish(k, carry):
        kv_out[k] = pick(
            choice[0],
            [own[0, k], own[1, k]]
            + [held_l[i, k] for i in range(2 * width)]
            + [held_r[i, k] for i in range(2 * width)],
        )
        return carry

    lax.fori_loop(0, chunks, finish, 0)

    def drain(k, carry):
        def one(sem, has):
            @pl.when(has)
            def _():
                for w in range(width):
                    lane_copy(
                        stage_r.at[w, k], stage_r.at[w, k], sem.at[w, k], sem.at[w, k], sibling
                    ).wait_send()

        one(r_send, chip < last)
        one(l_send, chip > 0)
        one(rf_send, chip > 0)
        one(lf_send, chip < last)
        return carry

    lax.fori_loop(0, chunks, drain, 0)
    for m in range(parts):
        own_copy(m).wait_send()
    for copy in copies:
        copy.wait_send()
    segment[pl.ds(me, 1)] = ag[0:1]
    for d in range(1, parts):
        ag_copies[d - 1].wait_recv()
        segment[pl.ds(lax.rem(me + parts - d, parts), 1)] = ag[d : d + 1]
    for copy in ag_copies:
        copy.wait_send()


def gather(choice, tokens, prefix, parts, chips, width, identity):
    rows, model = tokens.shape
    shard = prefix.shape[0]
    sub = 2 if shard >= 512 else 1
    chunks = parts * sub
    piece = (chunks, shard // sub, LANES)
    dma = pltpu.SemaphoreType.DMA
    lane = [dma((width, chunks))] * 8
    segment, kv = pl.pallas_call(
        functools.partial(gather_kernel, parts, chips, width, sub),
        out_shape=(
            jax.ShapeDtypeStruct((parts, rows, model), BF16),
            jax.ShapeDtypeStruct(piece, BF16),
        ),
        in_specs=[SMEM, VMEM, VMEM],
        out_specs=(VMEM, VMEM),
        scratch_shapes=[
            pltpu.VMEM((KVH, sub, shard // sub, LANES), BF16),
            pltpu.VMEM((2,) + piece, BF16),
            pltpu.VMEM((2 * width,) + piece, BF16),
            pltpu.VMEM((2 * width,) + piece, BF16),
            pltpu.VMEM((width,) + piece, BF16),
            pltpu.VMEM((width,) + piece, BF16),
            pltpu.VMEM((parts, rows, model), BF16),
        ]
        + [dma((parts,))] * 6
        + lane,
        compiler_params=pltpu.CompilerParams(
            collective_id=identity, has_side_effects=True, vmem_limit_bytes=52 * MIB
        ),
        name="gather",
    )(choice, tokens, prefix)
    return segment.reshape(parts * rows, model), kv.reshape(PLEN, LANES)


def attention_kernel(heads, x_ref, wq_ref, wkv_ref, cos_ref, sin_ref, begin_ref, kv_ref,
                     out_ref, queries, keys, values, scores):
    rows = x_ref.shape[0]
    lane = lax.broadcasted_iota(jnp.int32, (1, LANES), 1)
    former = (lane % HD) < HD // 2
    low = lane < HD

    def rotated(tile, cos_table, sin_table):
        swapped = jnp.where(
            former, -pltpu.roll(tile, LANES - HD // 2, 1), pltpu.roll(tile, HD // 2, 1)
        )
        return tile * cos_table + swapped * sin_table

    x = x_ref[...]
    mapped = jnp.dot(x, wq_ref[...], preferred_element_type=F32)
    cos_table, sin_table = cos_ref[...], sin_ref[...]
    for h in range(heads):
        if h % 2 == 0:
            tile = mapped[:, (h // 2) * LANES : (h // 2 + 1) * LANES]
            tile = rotated(tile, cos_table, sin_table).astype(BF16).astype(F32) * 0.125
            head = tile
        else:
            head = pltpu.roll(tile, HD, 1)
        queries[h] = jnp.where(low, head, 0.0).astype(BF16)
    pair = jnp.dot(x, wkv_ref[...], preferred_element_type=F32)
    pair = jnp.where(low, rotated(pair, cos_table, sin_table), pair)
    keys[0:PLEN, :] = kv_ref[...]
    keys[PLEN:, :] = pair.astype(BF16)
    values[...] = jnp.where(low, 1.0, keys[...].astype(F32)).astype(BF16)

    block = 256 if rows % 256 == 0 else rows
    step = 512
    total = PLEN + rows
    per_head = rows // block

    def one(i, carry):
        h, b = i // per_head, i % per_head
        start = pl.multiple_of(b * block, block)
        query = queries[h, pl.ds(start, block), :]
        top = jnp.full((block, LANES), NEG_FILL, F32)
        for n in range(total // step):
            part = lax.dot_general(
                query, keys[n * step : (n + 1) * step, :], (((1,), (1,)), ((), ())),
                preferred_element_type=F32,
            )
            if n * step >= PLEN:
                place = lax.broadcasted_iota(jnp.int32, (block, step), 1) + (n * step - PLEN)
                row = lax.broadcasted_iota(jnp.int32, (block, step), 0) + start
                seen = (place >= begin_ref[pl.ds(start, block), 0:1]) & (place <= row)
                part = jnp.where(seen, part, NEG_FILL)
            scores[:, n * step : (n + 1) * step] = part
            for q in range(step // LANES):
                top = jnp.maximum(top, part[:, q * LANES : (q + 1) * LANES])
        top = jnp.max(top, axis=1, keepdims=True)
        blended = jnp.zeros((block, LANES), F32)
        for n in range(total // step):
            weight = jnp.exp(scores[:, n * step : (n + 1) * step] - top).astype(BF16)
            blended += jnp.dot(
                weight, values[n * step : (n + 1) * step, :], preferred_element_type=F32
            )
        result = jnp.where(low, 0.0, blended / pltpu.roll(blended, HD, 1))
        out_ref[h, pl.ds(start, block), :] = result.astype(BF16)
        return carry

    lax.fori_loop(0, heads * per_head, one, 0)


def attention(x, wq, wkv, cos_table, sin_table, begins, kv, heads):
    rows = x.shape[0]
    total = PLEN + rows
    block = 256 if rows % 256 == 0 else rows
    out = pl.pallas_call(
        functools.partial(attention_kernel, heads),
        out_shape=jax.ShapeDtypeStruct((heads, rows, LANES), BF16),
        in_specs=[VMEM] * 7,
        out_specs=VMEM,
        scratch_shapes=[
            pltpu.VMEM((heads, rows, LANES), BF16),
            pltpu.VMEM((total, LANES), BF16),
            pltpu.VMEM((total, LANES), BF16),
            pltpu.VMEM((block, total), F32),
        ],
        compiler_params=pltpu.CompilerParams(vmem_limit_bytes=52 * MIB),
        name="attention",
    )(x, wq, wkv, cos_table, sin_table, begins, kv)
    return out


def mlp_kernel(
    parts, att, out_w, tokens, gate_up, down, result,
    gu_v, dn_v, a_send, a_recv, rows_v, f_send, f_recv, hidden,
    w_sem, as_sem, ar_sem, gs_sem, gr_sem, fs_sem, fr_sem,
):
    me = lax.axis_index("tensor")
    rows = tokens.shape[0]
    model = tokens.shape[1]
    units = hidden.shape[1]
    heads = att.shape[0]
    loads = [
        pltpu.make_async_copy(gate_up, gu_v, w_sem.at[0]),
        pltpu.make_async_copy(down, dn_v, w_sem.at[1]),
    ]
    for load in loads:
        load.start()
    barrier = pltpu.get_barrier_semaphore()
    for d in range(1, parts):
        pl.semaphore_signal(
            barrier, inc=1, device_id={"tensor": lax.rem(me + d, parts)}, device_id_type=MESH
        )

    def send(src, dst, send_sem, recv_sem, to):
        return pltpu.make_async_remote_copy(
            src_ref=src, dst_ref=dst, send_sem=send_sem, recv_sem=recv_sem,
            device_id={"tensor": to}, device_id_type=MESH,
        )

    def partial_out(owner):
        start = pl.multiple_of(owner * rows, rows)
        total = jnp.zeros((rows, model), F32)
        for h in range(heads):
            total += jnp.dot(
                att[h, pl.ds(start, rows), :], out_w[h], preferred_element_type=F32
            )
        return total.astype(BF16)

    copies = []
    for d in range(1, parts):
        to = lax.rem(me + d, parts)
        a_send[d] = partial_out(to)
        if d == 1:
            pl.semaphore_wait(barrier, parts - 1)
        copy = send(a_send.at[d], a_recv.at[d], as_sem.at[d], ar_sem.at[d], to)
        copy.start()
        copies.append(copy)
    total = partial_out(me).astype(F32)
    for d in range(1, parts):
        copies[d - 1].wait_recv()
        total += a_recv[d].astype(F32)
    middle = (tokens[...].astype(F32) + total).astype(BF16)
    a_send[0] = middle
    rows_v[0] = norm_rows(middle)
    sends = []
    for d in range(1, parts):
        copy = send(
            rows_v.at[0], rows_v.at[d], gs_sem.at[d], gr_sem.at[d], lax.rem(me + d, parts)
        )
        copy.start()
        sends.append(copy)
    for load in loads:
        load.wait()

    tile = 256 if units % 256 == 0 else units
    out_tile = 512
    backs = []
    for d in range(parts):
        if d > 0:
            sends[d - 1].wait_recv()

        def up(i, carry, d=d):
            if tile == units:
                at = slice(None)
            else:
                at = pl.ds(pl.multiple_of(i * tile, tile), tile)
            x = rows_v[d]
            gate = jnp.dot(x, gu_v[0, :, at], preferred_element_type=F32)
            raised = jnp.dot(x, gu_v[1, :, at], preferred_element_type=F32)
            hidden[:, at] = (gate / (1.0 + jnp.exp(-gate)) * raised).astype(BF16)
            return carry

        lax.fori_loop(0, units // tile, up, 0)

        def lower(i, carry, d=d):
            at = pl.ds(pl.multiple_of(i * out_tile, out_tile), out_tile)
            f_send[d, :, at] = jnp.dot(
                hidden[...], dn_v[:, at], preferred_element_type=F32
            ).astype(BF16)
            return carry

        lax.fori_loop(0, model // out_tile, lower, 0)
        if d > 0:
            owner = lax.rem(me + parts - d, parts)
            copy = send(f_send.at[d], f_recv.at[d], fs_sem.at[d], fr_sem.at[d], owner)
            copy.start()
            backs.append(copy)
    total = f_send[0].astype(F32)
    for d in range(1, parts):
        backs[d - 1].wait_recv()
        total += f_recv[d].astype(F32)
    result[...] = (a_send[0].astype(F32) + total).astype(BF16)
    for copy in copies + sends + backs:
        copy.wait_send()


def mlp(att, out_w, tokens, gate_up, down, parts, identity):
    rows, model = tokens.shape
    dma = pltpu.SemaphoreType.DMA
    full = pltpu.VMEM((parts, rows, model), BF16)
    return pl.pallas_call(
        functools.partial(mlp_kernel, parts),
        out_shape=jax.ShapeDtypeStruct((rows, model), BF16),
        in_specs=[VMEM, VMEM, VMEM, ANY, ANY],
        out_specs=VMEM,
        scratch_shapes=[
            pltpu.VMEM(gate_up.shape, BF16),
            pltpu.VMEM(down.shape, BF16),
            full, full, full, full, full,
            pltpu.VMEM((rows, down.shape[0]), BF16),
            dma((2,)),
        ]
        + [dma((parts,))] * 6,
        compiler_params=pltpu.CompilerParams(
            collective_id=identity, has_side_effects=True, vmem_limit_bytes=52 * MIB
        ),
        name="mlp",
    )(att, out_w, tokens, gate_up, down)


def on_device(
    tokens,
    lengths,
    group_prefix,
    prefix_cache,
    query_weight,
    key_weight,
    value_weight,
    out_weight,
    gate_up_weight,
    down_weight,
):
    parts = lax.axis_size("tensor")
    chips = lax.axis_size("dp") // 2
    rank = lax.axis_index("tensor")
    group = lax.axis_index("dp")
    rows = tokens.shape[0] * parts
    heads = query_weight.shape[1] // HD
    kv_head = rank * heads // (QH // KVH)

    tables = route_tables(group_prefix, chips)
    most = tables[-1]

    def routed(width, identity):
        def run(prefix, rows_in):
            choice = route_choice(group_prefix, tables, group, chips, width)
            return gather(choice, rows_in, prefix, parts, chips, width, identity)
        return run

    segment, kv = lax.cond(
        most <= 2, routed(1, 0), routed(chips // 2, 1), prefix_cache, tokens
    )

    positions, begins = token_layout(lengths[0], rows)
    cos_half, sin_half = rope_tables(positions)
    cos_table = jnp.concatenate([cos_half] * 4, axis=1)
    sin_table = jnp.concatenate([sin_half] * 4, axis=1)
    wkv = jnp.concatenate(
        [
            lax.dynamic_slice_in_dim(key_weight, kv_head * HD, HD, 1),
            lax.dynamic_slice_in_dim(value_weight, kv_head * HD, HD, 1),
        ],
        axis=1,
    )
    wq = query_weight
    if heads % 2:
        wq = jnp.pad(wq, ((0, 0), (0, HD)))
    att = attention(
        segment, wq, wkv, cos_table, sin_table, begins[:, None], kv, heads
    )
    out_w = jnp.pad(
        out_weight.reshape(heads, HD, out_weight.shape[1]), ((0, 0), (HD, 0), (0, 0))
    )
    return mlp(att, out_w, tokens, gate_up_weight, down_weight, parts, 2)


def solution(mesh):
    return jax.shard_map(
        on_device,
        mesh=mesh,
        in_specs=(
            P(("dp", "tensor"), None),
            P("dp", None),
            P(),
            P(("dp", "tensor"), None),
            P(None, "tensor"),
            P(),
            P(),
            P("tensor", None),
            P(None, None, "tensor"),
            P("tensor", None),
        ),
        out_specs=P(("dp", "tensor"), None),
        check_vma=False,
    )
```

```python
import functools
import math

import jax
import jax.numpy as jnp
from jax import lax
from jax.experimental import pallas as pl
from jax.experimental.pallas import tpu as pltpu
from jax.sharding import PartitionSpec as P

QH = 16
KVH = 4
HD = 64
PLEN = 4096
LANES = 128
NEG_FILL = -1e30
VMEM = pl.BlockSpec(memory_space=pltpu.VMEM)
SMEM = pl.BlockSpec(memory_space=pltpu.SMEM)
ANY = pl.BlockSpec(memory_space=pl.ANY)
MESH = pl.DeviceIdType.MESH
BF16 = jnp.bfloat16
F32 = jnp.float32
MIB = 1 << 20


def norm_rows(inputs):
    floats = inputs.astype(F32)
    mean = jnp.mean(floats * floats, axis=-1, keepdims=True)
    return (floats * lax.rsqrt(mean + 1e-05)).astype(BF16)


def token_layout(lengths, total_rows):
    ends_at = jnp.cumsum(lengths)
    starts_at = ends_at - lengths
    indices = jnp.arange(total_rows, dtype=jnp.int32)
    begins = jnp.max(
        jnp.where(starts_at[None, :] <= indices[:, None], starts_at[None, :], 0), axis=1
    )
    return ((PLEN + indices - begins).astype(F32), begins)


def rope_tables(positions):
    halves = HD // 2
    steps_float = jnp.arange(halves, dtype=F32)
    inverse = jnp.exp(steps_float * (-2.0 * math.log(10000.0) / HD))
    angles = positions[:, None] * inverse[None, :]
    return (jnp.cos(angles), jnp.sin(angles))


def most_crossing(group_prefix, chips):
    slots = jnp.arange(2 * chips, dtype=jnp.int32)
    wanted = group_prefix[None, :] == slots[:, None]
    final = jnp.max(jnp.where(wanted, slots[None, :], -1), axis=1)
    first = jnp.min(jnp.where(wanted, slots[None, :], 2 * chips), axis=1)
    edge = 2 * jnp.arange(1, chips, dtype=jnp.int32)[:, None]
    right = (slots[None, :] < edge) & (final[None, :] >= edge)
    left = (slots[None, :] >= edge) & (first[None, :] < edge)
    counts = jnp.sum(jnp.stack([right, left]).astype(jnp.int32), axis=2)
    return jnp.max(counts)


def route_choice(slot_ref, group, chips, width):
    number = 2 * chips
    chip, core = group // 2, group % 2
    held = [slot_ref[g] for g in range(number)]
    final, first = [], []
    for s in range(number):
        top, low = jnp.int32(-1), jnp.int32(number)
        for g in range(number):
            top = jnp.where(held[g] == s, g, top)
        for g in reversed(range(number)):
            low = jnp.where(held[g] == s, g, low)
        final.append(top)
        first.append(low)

    def ranks(needs):
        result, count = [], jnp.int32(0)
        for need in needs:
            result.append(count)
            count = count + need.astype(jnp.int32)
        return result

    def right(z):
        return [(s // 2 <= z) & (final[s] >= 2 * (z + 1)) for s in range(number)]

    def left(z):
        return [(s // 2 >= z) & (first[s] < 2 * z) for s in range(number)]

    from_left, from_right = ranks(right(chip - 1)), ranks(left(chip + 1))
    mine = slot_ref[group]
    keep = jnp.int32(0)
    sides = []
    for s in range(number):
        own = chip == s // 2
        value = jnp.where(
            own, s % 2, jnp.where(chip > s // 2, 2 + from_left[s], 2 + 2 * width + from_right[s])
        )
        keep = jnp.where(mine == s, value, keep)
    for needs, source in ((right(chip), from_left), (left(chip), from_right)):
        rank = ranks(needs)
        chosen = []
        for w in range(width):
            place = 2 * w + core
            value = jnp.int32(0)
            for s in range(number):
                value = jnp.where(
                    needs[s] & (rank[s] == place),
                    jnp.where(chip == s // 2, s % 2, 2 + source[s]),
                    value,
                )
            chosen.append(value)
        sides.append(chosen)
    return [keep] + sides[0] + sides[1]


def pick(number, candidates):
    result = candidates[0]
    for i in range(1, len(candidates)):
        result = jnp.where(number == i, candidates[i], result)
    return result


def gather_kernel(
    parts, chips, width, sub,
    slot_ref, tokens, prefix, segment, kv_out,
    packed, own, held_l, held_r, stage_r, stage_l, ag,
    ag_send, ag_recv, a2a_send, a2a_recv, own_send, own_recv,
    r_send, r_recv, l_send, l_recv, rf_send, rf_recv, lf_send, lf_recv,
):
    me = lax.axis_index("tensor")
    group = lax.axis_index("dp")
    chip, core = group // 2, group % 2
    other = 1 - core
    sibling = chip * 2 + other
    groups = 2 * chips
    chunks = parts * sub
    chunk_rows = prefix.shape[0] // sub

    barrier = pltpu.get_barrier_semaphore()
    for d in range(1, parts):
        pl.semaphore_signal(
            barrier, inc=1, device_id={"tensor": lax.rem(me + d, parts)}, device_id_type=MESH
        )
    near = (sibling, lax.rem(group + 2, groups), lax.rem(group + groups - 2, groups))
    for to in near:
        pl.semaphore_signal(barrier, inc=1, device_id={"dp": to}, device_id_type=MESH)

    choice = route_choice(slot_ref, group, chips, width)
    rows_i = lax.broadcasted_iota(jnp.int32, (2 * KVH * HD, LANES), 0)
    cols_i = lax.broadcasted_iota(jnp.int32, (2 * KVH * HD, LANES), 1)
    source = cols_i + jnp.where(cols_i >= HD, KVH * HD - HD, 0)
    for h in range(KVH):
        take = (rows_i == source + h * HD).astype(F32).astype(BF16)
        packed[h] = (
            jnp.dot(prefix[...], take, preferred_element_type=F32)
            .astype(BF16)
            .reshape(sub, chunk_rows, LANES)
        )
    pl.semaphore_wait(barrier, parts - 1 + 3)

    copies = []
    for d in range(parts - 1, 0, -1):
        to = lax.rem(me + d, parts)
        copy = pltpu.make_async_remote_copy(
            src_ref=packed.at[to * KVH // parts],
            dst_ref=own.at[core, pl.ds((parts - d) * sub, sub)],
            send_sem=a2a_send.at[parts - d],
            recv_sem=a2a_recv.at[parts - d],
            device_id={"tensor": to},
            device_id_type=MESH,
        )
        copy.start()
        copies.append(copy)
    own[core, 0:sub] = packed[me * KVH // parts]

    ag[0] = norm_rows(tokens[...])
    def ag_copy(d):
        return pltpu.make_async_remote_copy(
            src_ref=ag.at[0],
            dst_ref=ag.at[d],
            send_sem=ag_send.at[d],
            recv_sem=ag_recv.at[d],
            device_id={"tensor": lax.rem(me + d, parts)},
            device_id_type=MESH,
        )

    def half_copy(slot, place, half, to):
        rows = tokens.shape[0] // 2
        at = pl.ds(half * rows, rows)
        return pltpu.make_async_remote_copy(
            src_ref=ag.at[slot, at],
            dst_ref=ag.at[place, at],
            send_sem=ag_send.at[2 * place + half - 2],
            recv_sem=ag_recv.at[2 * place + half - 2],
            device_id={"tensor": to},
            device_id_type=MESH,
        )

    near_x, near_y = me + 1 - 2 * (me % 2), lax.rem(me + 2, parts)

    def ag_start():
        if parts == 4:
            half_copy(0, 1, 0, near_x).start()
            half_copy(0, 2, 1, near_y).start()
            half_copy(0, 1, 1, near_x).start()
            half_copy(0, 2, 0, near_y).start()
        else:
            for d in range(1, parts):
                ag_copy(d).start()

    def ag_forward():
        if parts == 4:
            half_copy(0, 1, 0, near_x).wait_recv()
            half_copy(1, 3, 0, near_y).start()
            half_copy(0, 2, 1, near_y).wait_recv()
            half_copy(2, 3, 1, near_x).start()

    def ag_finish():
        segment[pl.ds(me, 1)] = ag[0:1]
        if parts == 4:
            half_copy(0, 1, 1, near_x).wait_recv()
            segment[pl.ds(near_x, 1)] = ag[1:2]
            half_copy(0, 2, 0, near_y).wait_recv()
            segment[pl.ds(near_y, 1)] = ag[2:3]
            half_copy(1, 3, 0, near_y).wait_recv()
            half_copy(2, 3, 1, near_x).wait_recv()
            segment[pl.ds(parts - 1 - me, 1)] = ag[3:4]
            for place, half in ((1, 0), (1, 1), (2, 0), (2, 1), (3, 0), (3, 1)):
                half_copy(0, place, half, near_x).wait_send()
        else:
            for d in range(1, parts):
                ag_copy(d).wait_recv()
                segment[pl.ds(lax.rem(me + parts - d, parts), 1)] = ag[d : d + 1]
            for d in range(1, parts):
                ag_copy(d).wait_send()

    def lane_copy(src, dst, send_sem, recv_sem, to):
        return pltpu.make_async_remote_copy(
            src_ref=src, dst_ref=dst, send_sem=send_sem, recv_sem=recv_sem,
            device_id={"dp": to}, device_id_type=MESH,
        )

    def own_copy(m):
        block = own.at[core, pl.ds(m * sub, sub)]
        return lane_copy(block, block, own_send.at[m], own_recv.at[m], sibling)

    def flow(k, has_from, has_to, to, base, held, stage, send, recv, f_send, f_recv):
        def hop(w):
            return lane_copy(
                stage.at[w, k], held.at[w * 2 + core, k], send.at[w, k], recv.at[w, k], to
            )

        def forward(w):
            ref = held.at[w * 2 + core, k]
            return lane_copy(ref, ref, f_send.at[w, k], f_recv.at[w, k], sibling)

        @pl.when(has_from)
        def _():
            for w in range(width):
                hop(w).wait_recv()
                forward(w).start()
            for w in range(width):
                forward(w).wait_recv()

        @pl.when(has_to)
        def _():
            for w in range(width):
                stage[w, k] = pick(
                    choice[base + w],
                    [own[0, k], own[1, k]] + [held[i, k] for i in range(2 * width)],
                )
                hop(w).start()

    last = chips - 1

    def step(s, carry):
        m = s // sub

        @pl.when((m < parts) & (s % sub == 0))
        def _():
            @pl.when(m > 0)
            def _():
                pltpu.make_async_remote_copy(
                    src_ref=packed.at[0],
                    dst_ref=own.at[core, pl.ds(m * sub, sub)],
                    send_sem=a2a_send.at[m],
                    recv_sem=a2a_recv.at[m],
                    device_id={"tensor": lax.rem(me + 1, parts)},
                    device_id_type=MESH,
                ).wait_recv()

            own_copy(m).start()
            own_copy(m).wait_recv()
            pl.when(m == parts - 1)(ag_start)

        k = s - chip

        @pl.when((k >= 0) & (k < chunks))
        def _():
            flow(
                k, chip > 0, chip < last, lax.rem(group + 2, groups), 1,
                held_l, stage_r, r_send, r_recv, rf_send, rf_recv,
            )

        j = s - (last - chip)

        @pl.when((j >= 0) & (j < chunks))
        def _():
            flow(
                j, chip < last, chip > 0, lax.rem(group + groups - 2, groups), 1 + width,
                held_r, stage_l, l_send, l_recv, lf_send, lf_recv,
            )

        pl.when(s == chunks + last - 2)(ag_forward)
        return carry

    for edge in ((chip == 0, held_l), (chip == last, held_r)):
        def clear(ref=edge[1]):
            ref[...] = jnp.zeros_like(ref)
        pl.when(edge[0])(clear)

    lax.fori_loop(0, chunks + last, step, 0)

    def finish(k, carry):
        kv_out[k] = pick(
            choice[0],
            [own[0, k], own[1, k]]
            + [held_l[i, k] for i in range(2 * width)]
            + [held_r[i, k] for i in range(2 * width)],
        )
        return carry

    lax.fori_loop(0, chunks, finish, 0)

    def drain(k, carry):
        def one(sem, has):
            @pl.when(has)
            def _():
                for w in range(width):
                    lane_copy(
                        stage_r.at[w, k], stage_r.at[w, k], sem.at[w, k], sem.at[w, k], sibling
                    ).wait_send()

        one(r_send, chip < last)
        one(l_send, chip > 0)
        one(rf_send, chip > 0)
        one(lf_send, chip < last)
        return carry

    lax.fori_loop(0, chunks, drain, 0)
    for m in range(parts):
        own_copy(m).wait_send()
    for copy in copies:
        copy.wait_send()
    ag_finish()


def gather(slots, tokens, prefix, parts, chips, width, identity):
    rows, model = tokens.shape
    shard = prefix.shape[0]
    sub = 2 if shard >= 512 else 1
    chunks = parts * sub
    piece = (chunks, shard // sub, LANES)
    dma = pltpu.SemaphoreType.DMA
    lane = [dma((width, chunks))] * 8
    segment, kv = pl.pallas_call(
        functools.partial(gather_kernel, parts, chips, width, sub),
        out_shape=(
            jax.ShapeDtypeStruct((parts, rows, model), BF16),
            jax.ShapeDtypeStruct(piece, BF16),
        ),
        in_specs=[SMEM, VMEM, VMEM],
        out_specs=(VMEM, VMEM),
        scratch_shapes=[
            pltpu.VMEM((KVH, sub, shard // sub, LANES), BF16),
            pltpu.VMEM((2,) + piece, BF16),
            pltpu.VMEM((2 * width,) + piece, BF16),
            pltpu.VMEM((2 * width,) + piece, BF16),
            pltpu.VMEM((width,) + piece, BF16),
            pltpu.VMEM((width,) + piece, BF16),
            pltpu.VMEM((parts, rows, model), BF16),
        ]
        + [dma((max(parts, 6),))] * 2
        + [dma((parts,))] * 4
        + lane,
        compiler_params=pltpu.CompilerParams(
            collective_id=identity, has_side_effects=True, vmem_limit_bytes=52 * MIB
        ),
        name="gather",
    )(slots, tokens, prefix)
    return segment.reshape(parts * rows, model), kv.reshape(PLEN, LANES)


def attention_kernel(heads, parts, *refs):
    (x_ref, wq_ref, wkv_ref, cos_ref, sin_ref, begin_ref, kv_ref) = refs[:7]
    if parts == 4:
        ow, out_ref, ow_all, queries, keys, values, scores, w_send, w_recv, s_send, s_recv = refs[7:]
        me = lax.axis_index("tensor")
        group = lax.axis_index("dp")
        core = group % 2
        sibling = group + 1 - 2 * core
        near_x, near_y = me + 1 - 2 * (me % 2), lax.rem(me + 2, parts)
        quarter = ow.shape[0] // 4

        def piece(src, place, half, to):
            at = pl.ds((2 * core + half) * quarter, quarter)
            return pltpu.make_async_remote_copy(
                src_ref=ow.at[at] if src == 0 else ow_all.at[src, at],
                dst_ref=ow_all.at[place, at],
                send_sem=w_send.at[2 * place + half - 2],
                recv_sem=w_recv.at[2 * place + half - 2],
                device_id={"tensor": to},
                device_id_type=MESH,
            )

        def share(place):
            ref = ow_all.at[place, pl.ds(2 * core * quarter, 2 * quarter)]
            return pltpu.make_async_remote_copy(
                src_ref=ref, dst_ref=ref, send_sem=s_send.at[place - 1],
                recv_sem=s_recv.at[place - 1], device_id={"dp": sibling}, device_id_type=MESH,
            )

        barrier = pltpu.get_barrier_semaphore()
        for to in ({"tensor": near_x}, {"tensor": near_y}, {"dp": sibling}):
            pl.semaphore_signal(barrier, inc=1, device_id=to, device_id_type=MESH)
        pl.semaphore_wait(barrier, 3)
        piece(0, 1, 0, near_x).start()
        piece(0, 2, 1, near_y).start()
        piece(0, 1, 1, near_x).start()
        piece(0, 2, 0, near_y).start()
        ow_all[0] = ow[...]
    else:
        out_ref, queries, keys, values, scores = refs[7:]
    rows = x_ref.shape[0]
    lane = lax.broadcasted_iota(jnp.int32, (1, LANES), 1)
    former = (lane % HD) < HD // 2
    low = lane < HD

    def rotated(tile, cos_table, sin_table):
        swapped = jnp.where(
            former, -pltpu.roll(tile, LANES - HD // 2, 1), pltpu.roll(tile, HD // 2, 1)
        )
        return tile * cos_table + swapped * sin_table

    x = x_ref[...]
    mapped = jnp.dot(x, wq_ref[...], preferred_element_type=F32)
    cos_table, sin_table = cos_ref[...], sin_ref[...]
    for h in range(heads):
        if h % 2 == 0:
            tile = mapped[:, (h // 2) * LANES : (h // 2 + 1) * LANES]
            tile = rotated(tile, cos_table, sin_table).astype(BF16).astype(F32) * 0.125
            head = tile
        else:
            head = pltpu.roll(tile, HD, 1)
        queries[h] = jnp.where(low, head, 0.0).astype(BF16)
    pair = jnp.dot(x, wkv_ref[...], preferred_element_type=F32)
    pair = jnp.where(low, rotated(pair, cos_table, sin_table), pair)
    keys[0:PLEN, :] = kv_ref[...]
    keys[PLEN:, :] = pair.astype(BF16)
    values[...] = jnp.where(low, 1.0, keys[...].astype(F32)).astype(BF16)

    block = 256 if rows % 256 == 0 else rows
    step = 512
    total = PLEN + rows
    per_head = rows // block
    pairs = (heads + 1) // 2

    def one_head(h, start, slot):
        query = queries[h, pl.ds(start, block), :]
        top = jnp.full((block, LANES), NEG_FILL, F32)
        for n in range(total // step):
            part = lax.dot_general(
                query, keys[n * step : (n + 1) * step, :], (((1,), (1,)), ((), ())),
                preferred_element_type=F32,
            )
            if n * step >= PLEN:
                place = lax.broadcasted_iota(jnp.int32, (block, step), 1) + (n * step - PLEN)
                row = lax.broadcasted_iota(jnp.int32, (block, step), 0) + start
                seen = (place >= begin_ref[pl.ds(start, block), 0:1]) & (place <= row)
                part = jnp.where(seen, part, NEG_FILL)
            scores[slot, :, n * step : (n + 1) * step] = part
            for q in range(step // LANES):
                top = jnp.maximum(top, part[:, q * LANES : (q + 1) * LANES])
        top = jnp.max(top, axis=1, keepdims=True)
        blended = jnp.zeros((block, LANES), F32)
        for n in range(total // step):
            weight = jnp.exp(scores[slot, :, n * step : (n + 1) * step] - top).astype(BF16)
            blended += jnp.dot(
                weight, values[n * step : (n + 1) * step, :], preferred_element_type=F32
            )
        return blended

    def one(i, carry):
        if parts == 4:
            @pl.when(i == 1)
            def _():
                piece(0, 1, 0, near_x).wait_recv()
                piece(1, 3, 0, near_y).start()
                piece(0, 2, 1, near_y).wait_recv()
                piece(2, 3, 1, near_x).start()

            @pl.when(i == pairs * per_head - 1)
            def _():
                piece(0, 1, 1, near_x).wait_recv()
                share(1).start()
                piece(0, 2, 0, near_y).wait_recv()
                share(2).start()

        p, b = i // per_head, i % per_head
        start = pl.multiple_of(b * block, block)
        even = one_head(2 * p, start, 0)
        even = pltpu.roll(even, HD, 1) / even
        if heads > 1:
            odd = one_head(2 * p + 1, start, 1)
            odd = odd / pltpu.roll(odd, HD, 1)
        else:
            odd = jnp.zeros_like(even)
        at = pl.ds(pl.multiple_of(p * LANES, LANES), LANES)
        out_ref[pl.ds(start, block), at] = jnp.where(low, even, odd).astype(BF16)
        return carry

    lax.fori_loop(0, pairs * per_head, one, 0)
    if parts == 4:
        piece(1, 3, 0, near_y).wait_recv()
        piece(2, 3, 1, near_x).wait_recv()
        share(3).start()
        for place in (1, 2, 3):
            share(place).wait_recv()
        for place in (1, 2, 3):
            share(place).wait_send()
            for half in range(2):
                piece(0, place, half, near_x).wait_send()


def attention(x, wq, wkv, cos_table, sin_table, begins, kv, out_w, heads, parts, identity):
    rows = x.shape[0]
    total = PLEN + rows
    block = 256 if rows % 256 == 0 else rows
    width = (heads + 1) // 2 * LANES
    exchange = parts == 4
    shapes = [jax.ShapeDtypeStruct((rows, width), BF16)]
    operands = [x, wq, wkv, cos_table, sin_table, begins, kv]
    scratch = [
        pltpu.VMEM((heads, rows, LANES), BF16),
        pltpu.VMEM((total, LANES), BF16),
        pltpu.VMEM((total, LANES), BF16),
        pltpu.VMEM((2, block, total), F32),
    ]
    params = dict(vmem_limit_bytes=52 * MIB)
    if exchange:
        operands.append(out_w)
        shapes.append(jax.ShapeDtypeStruct((parts,) + out_w.shape, BF16))
        scratch += [pltpu.SemaphoreType.DMA((6,))] * 2 + [pltpu.SemaphoreType.DMA((3,))] * 2
        params.update(collective_id=identity, has_side_effects=True)
    return pl.pallas_call(
        functools.partial(attention_kernel, heads, parts),
        out_shape=shapes,
        in_specs=[VMEM] * len(operands),
        out_specs=[VMEM] * len(shapes),
        scratch_shapes=scratch,
        compiler_params=pltpu.CompilerParams(**params),
        name="attention",
    )(*operands)


def mlp_kernel(
    parts, att, out_w, tokens, gate_up, down, result,
    gu_v, dn_v, a_send, a_recv, rows_v, f_send, f_recv, hidden,
    w_sem, as_sem, ar_sem, gs_sem, gr_sem, fs_sem, fr_sem,
):
    me = lax.axis_index("tensor")
    rows = tokens.shape[0]
    model = tokens.shape[1]
    units = hidden.shape[1]
    loads = [
        pltpu.make_async_copy(gate_up, gu_v, w_sem.at[0]),
        pltpu.make_async_copy(down, dn_v, w_sem.at[1]),
    ]
    for load in loads:
        load.start()
    barrier = pltpu.get_barrier_semaphore()
    for d in range(1, parts):
        pl.semaphore_signal(
            barrier, inc=1, device_id={"tensor": lax.rem(me + d, parts)}, device_id_type=MESH
        )

    def send(src, dst, send_sem, recv_sem, to):
        return pltpu.make_async_remote_copy(
            src_ref=src, dst_ref=dst, send_sem=send_sem, recv_sem=recv_sem,
            device_id={"tensor": to}, device_id_type=MESH,
        )

    def partial_out(owner):
        start = pl.multiple_of(owner * rows, rows)
        return jnp.dot(
            att[pl.ds(start, rows), :], out_w[...], preferred_element_type=F32
        ).astype(BF16)

    copies = []
    for d in range(1, parts):
        to = lax.rem(me + d, parts)
        a_send[d] = partial_out(to)
        if d == 1:
            pl.semaphore_wait(barrier, parts - 1)
        copy = send(a_send.at[d], a_recv.at[d], as_sem.at[d], ar_sem.at[d], to)
        copy.start()
        copies.append(copy)
    total = partial_out(me).astype(F32)
    for d in range(1, parts):
        copies[d - 1].wait_recv()
        total += a_recv[d].astype(F32)
    middle = (tokens[...].astype(F32) + total).astype(BF16)
    a_send[0] = middle
    rows_v[0] = norm_rows(middle)
    sends = []
    for d in range(1, parts):
        copy = send(
            rows_v.at[0], rows_v.at[d], gs_sem.at[d], gr_sem.at[d], lax.rem(me + d, parts)
        )
        copy.start()
        sends.append(copy)
    for load in loads:
        load.wait()

    tile = 256 if units % 256 == 0 else units
    out_tile = 512
    backs = []
    for d in range(parts):
        if d > 0:
            sends[d - 1].wait_recv()

        def up(i, carry, d=d):
            if tile == units:
                at = slice(None)
            else:
                at = pl.ds(pl.multiple_of(i * tile, tile), tile)
            x = rows_v[d]
            gate = jnp.dot(x, gu_v[0, :, at], preferred_element_type=F32)
            raised = jnp.dot(x, gu_v[1, :, at], preferred_element_type=F32)
            hidden[:, at] = (gate / (1.0 + jnp.exp(-gate)) * raised).astype(BF16)
            return carry

        lax.fori_loop(0, units // tile, up, 0)

        def lower(i, carry, d=d):
            at = pl.ds(pl.multiple_of(i * out_tile, out_tile), out_tile)
            f_send[d, :, at] = jnp.dot(
                hidden[...], dn_v[:, at], preferred_element_type=F32
            ).astype(BF16)
            return carry

        lax.fori_loop(0, model // out_tile, lower, 0)
        if d > 0:
            owner = lax.rem(me + parts - d, parts)
            copy = send(f_send.at[d], f_recv.at[d], fs_sem.at[d], fr_sem.at[d], owner)
            copy.start()
            backs.append(copy)
    total = f_send[0].astype(F32)
    for d in range(1, parts):
        backs[d - 1].wait_recv()
        total += f_recv[d].astype(F32)
    result[...] = (a_send[0].astype(F32) + total).astype(BF16)
    for copy in copies + sends + backs:
        copy.wait_send()


def mlp_square_kernel(
    att, out_w, tokens, gate_up, down, result,
    gu_v, dn_v, att_v, mid_v, rows_v, f_v, f_in, hidden,
    w_sem, as_sem, ar_sem, gs_sem, gr_sem, fs_sem, fr_sem,
):
    parts = 4
    me = lax.axis_index("tensor")
    near_x, near_y, far = me + 1 - 2 * (me % 2), lax.rem(me + 2, parts), parts - 1 - me
    rows, model = tokens.shape
    half_rows = rows // 2
    units = hidden.shape[1]
    loads = [
        pltpu.make_async_copy(gate_up, gu_v, w_sem.at[0]),
        pltpu.make_async_copy(down, dn_v, w_sem.at[1]),
    ]
    for load in loads:
        load.start()
    barrier = pltpu.get_barrier_semaphore()
    for to in (near_x, near_y, far):
        pl.semaphore_signal(barrier, inc=1, device_id={"tensor": to}, device_id_type=MESH)
    pl.semaphore_wait(barrier, parts - 1)

    def send(src, dst, send_sem, recv_sem, to):
        return pltpu.make_async_remote_copy(
            src_ref=src, dst_ref=dst, send_sem=send_sem, recv_sem=recv_sem,
            device_id={"tensor": to}, device_id_type=MESH,
        )

    def cut(half):
        return pl.ds(half * half_rows, half_rows)

    def block_of(owner):
        return att.at[pl.ds(pl.multiple_of(owner * rows, rows), rows)]

    swaps = [
        send(block_of(to), att_v.at[slot], as_sem.at[slot], ar_sem.at[slot], to)
        for slot, to in ((3, far), (1, near_x), (2, near_y))
    ]
    for copy in swaps:
        copy.start()

    def group_term(block, slot):
        term = jnp.dot(block, out_w[slot], preferred_element_type=F32)
        return term.astype(BF16).astype(F32)

    total = group_term(att[pl.ds(pl.multiple_of(me * rows, rows), rows), :], 0)
    for copy, slot in zip(swaps[1:] + swaps[:1], (1, 2, 3)):
        copy.wait_recv()
        total += group_term(att_v[slot], slot)
    middle = (tokens[...].astype(F32) + total).astype(BF16)
    mid_v[...] = middle
    rows_v[0] = norm_rows(middle)

    def piece(src, place, half, to):
        at = 2 * place + half - 2
        return send(
            rows_v.at[src, cut(half)], rows_v.at[place, cut(half)],
            gs_sem.at[at], gr_sem.at[at], to,
        )

    piece(0, 1, 0, near_x).start()
    piece(0, 2, 1, near_y).start()
    piece(0, 1, 1, near_x).start()
    piece(0, 2, 0, near_y).start()
    for load in loads:
        load.wait()

    tile = 256 if units % 256 == 0 else units
    out_tile = 512

    def feed(first, count):
        many = count * rows

        def up(i, carry):
            at = pl.ds(pl.multiple_of(i * tile, tile), tile)
            x = rows_v[first : first + count].reshape(many, model)
            gate = jnp.dot(x, gu_v[0, :, at], preferred_element_type=F32)
            raised = jnp.dot(x, gu_v[1, :, at], preferred_element_type=F32)
            hidden[0:many, at] = (gate / (1.0 + jnp.exp(-gate)) * raised).astype(BF16)
            return carry

        lax.fori_loop(0, units // tile, up, 0)

        def lower(i, carry):
            at = pl.ds(pl.multiple_of(i * out_tile, out_tile), out_tile)
            f_v[first : first + count, :, at] = (
                jnp.dot(hidden[0:many, :], dn_v[:, at], preferred_element_type=F32)
                .astype(BF16)
                .reshape(count, rows, out_tile)
            )
            return carry

        lax.fori_loop(0, model // out_tile, lower, 0)

    def back(slot, half, place, to):
        at = 2 * place + half
        return send(
            f_v.at[slot, cut(half)], f_in.at[place, cut(half)], fs_sem.at[at], fr_sem.at[at], to
        )

    feed(0, 1)
    piece(0, 1, 0, near_x).wait_recv()
    piece(1, 3, 0, near_y).start()
    piece(0, 2, 1, near_y).wait_recv()
    piece(2, 3, 1, near_x).start()
    piece(0, 1, 1, near_x).wait_recv()
    piece(0, 2, 0, near_y).wait_recv()
    feed(1, 2)
    back(1, 0, 0, near_x).start()
    back(2, 1, 1, near_y).start()
    piece(1, 3, 0, near_y).wait_recv()
    piece(2, 3, 1, near_x).wait_recv()
    feed(3, 1)
    back(3, 0, 2, near_x).start()
    back(3, 1, 2, near_y).start()
    for half, slot, place, to in ((0, 2, 1, near_y), (1, 1, 0, near_x)):
        back(3, half, 2, to).wait_recv()
        f_v[slot, cut(half)] = (
            f_v[slot, cut(half)].astype(F32) + f_in[2, cut(half)].astype(F32)
        ).astype(BF16)
        back(slot, half, place, to).start()
    order = ((1, 0, 0, near_x), (2, 1, 1, near_y), (2, 0, 1, near_y), (1, 1, 0, near_x))
    for slot, half, place, to in order:
        back(slot, half, place, to).wait_recv()
    total = f_v[0].astype(F32) + f_in[0].astype(F32) + f_in[1].astype(F32)
    result[...] = (mid_v[...].astype(F32) + total).astype(BF16)
    for copy in swaps:
        copy.wait_send()
    for place in (1, 2, 3):
        for half in range(2):
            piece(0, place, half, near_x).wait_send()
            back(1, half, place - 1, near_x).wait_send()


def mlp_square(att, out_w, tokens, gate_up, down, identity):
    rows, model = tokens.shape
    parts = 4
    dma = pltpu.SemaphoreType.DMA
    full = pltpu.VMEM((parts, rows, model), BF16)
    return pl.pallas_call(
        mlp_square_kernel,
        out_shape=jax.ShapeDtypeStruct((rows, model), BF16),
        in_specs=[VMEM, VMEM, VMEM, ANY, ANY],
        out_specs=VMEM,
        scratch_shapes=[
            pltpu.VMEM(gate_up.shape, BF16),
            pltpu.VMEM(down.shape, BF16),
            pltpu.VMEM((parts, rows, att.shape[1]), BF16),
            pltpu.VMEM((rows, model), BF16),
            full, full,
            pltpu.VMEM((3, rows, model), BF16),
            pltpu.VMEM((2 * rows, down.shape[0]), BF16),
            dma((2,)), dma((parts,)), dma((parts,)),
        ]
        + [dma((6,))] * 4,
        compiler_params=pltpu.CompilerParams(
            collective_id=identity, has_side_effects=True, vmem_limit_bytes=52 * MIB
        ),
        name="mlp",
    )(att, out_w, tokens, gate_up, down)


def mlp(att, out_w, tokens, gate_up, down, parts, identity):
    rows, model = tokens.shape
    dma = pltpu.SemaphoreType.DMA
    full = pltpu.VMEM((parts, rows, model), BF16)
    return pl.pallas_call(
        functools.partial(mlp_kernel, parts),
        out_shape=jax.ShapeDtypeStruct((rows, model), BF16),
        in_specs=[VMEM, VMEM, VMEM, ANY, ANY],
        out_specs=VMEM,
        scratch_shapes=[
            pltpu.VMEM(gate_up.shape, BF16),
            pltpu.VMEM(down.shape, BF16),
            full, full, full, full, full,
            pltpu.VMEM((rows, down.shape[0]), BF16),
            dma((2,)),
        ]
        + [dma((parts,))] * 6,
        compiler_params=pltpu.CompilerParams(
            collective_id=identity, has_side_effects=True, vmem_limit_bytes=52 * MIB
        ),
        name="mlp",
    )(att, out_w, tokens, gate_up, down)


def on_device(
    tokens,
    lengths,
    group_prefix,
    prefix_cache,
    query_weight,
    key_weight,
    value_weight,
    out_weight,
    gate_up_weight,
    down_weight,
):
    parts = lax.axis_size("tensor")
    chips = lax.axis_size("dp") // 2
    rank = lax.axis_index("tensor")
    rows = tokens.shape[0] * parts
    heads = query_weight.shape[1] // HD
    kv_head = rank * heads // (QH // KVH)

    most = most_crossing(group_prefix, chips)

    def routed(width, identity):
        def run(prefix, rows_in):
            return gather(group_prefix, rows_in, prefix, parts, chips, width, identity)
        return run

    segment, kv = lax.cond(
        most <= 2, routed(1, 0), routed(chips // 2, 1), prefix_cache, tokens
    )

    positions, begins = token_layout(lengths[0], rows)
    cos_half, sin_half = rope_tables(positions)
    cos_table = jnp.concatenate([cos_half] * 4, axis=1)
    sin_table = jnp.concatenate([sin_half] * 4, axis=1)
    wkv = jnp.concatenate(
        [
            lax.dynamic_slice_in_dim(key_weight, kv_head * HD, HD, 1),
            lax.dynamic_slice_in_dim(value_weight, kv_head * HD, HD, 1),
        ],
        axis=1,
    )
    wq = query_weight
    if heads % 2:
        wq = jnp.pad(wq, ((0, 0), (0, HD)))
    outputs = attention(
        segment, wq, wkv, cos_table, sin_table, begins[:, None], kv, out_weight, heads, parts, 3
    )
    if parts == 4:
        return mlp_square(*outputs, tokens, gate_up_weight, down_weight, 2)
    out_w = out_weight
    if heads % 2:
        out_w = jnp.pad(out_w, ((0, HD), (0, 0)))
    return mlp(outputs[0], out_w, tokens, gate_up_weight, down_weight, parts, 2)


def solution(mesh):
    return jax.shard_map(
        on_device,
        mesh=mesh,
        in_specs=(
            P(("dp", "tensor"), None),
            P("dp", None),
            P(),
            P(("dp", "tensor"), None),
            P(None, "tensor"),
            P(),
            P(),
            P("tensor", None),
            P(None, None, "tensor"),
            P("tensor", None),
        ),
        out_specs=P(("dp", "tensor"), None),
        check_vma=False,
    )
```

```python
import functools
import math

import jax
import jax.numpy as jnp
from jax import lax
from jax.experimental import pallas as pl
from jax.experimental.pallas import tpu as pltpu
from jax.sharding import PartitionSpec as P

QH = 16
KVH = 4
HD = 64
PLEN = 4096
LANES = 128
SKEW = 3
NEG_FILL = -1e30
VMEM = pl.BlockSpec(memory_space=pltpu.VMEM)
SMEM = pl.BlockSpec(memory_space=pltpu.SMEM)
ANY = pl.BlockSpec(memory_space=pl.ANY)
MESH = pl.DeviceIdType.MESH
BF16 = jnp.bfloat16
F32 = jnp.float32
MIB = 1 << 20


def norm_rows(inputs):
    floats = inputs.astype(F32)
    mean = jnp.mean(floats * floats, axis=-1, keepdims=True)
    return (floats * lax.rsqrt(mean + 1e-05)).astype(BF16)


def token_layout(lengths, total_rows):
    ends_at = jnp.cumsum(lengths)
    starts_at = ends_at - lengths
    indices = jnp.arange(total_rows, dtype=jnp.int32)
    begins = jnp.max(
        jnp.where(starts_at[None, :] <= indices[:, None], starts_at[None, :], 0), axis=1
    )
    return ((PLEN + indices - begins).astype(F32), begins)


def rope_tables(positions):
    halves = HD // 2
    steps_float = jnp.arange(halves, dtype=F32)
    inverse = jnp.exp(steps_float * (-2.0 * math.log(10000.0) / HD))
    angles = positions[:, None] * inverse[None, :]
    return (jnp.cos(angles), jnp.sin(angles))


def most_crossing(group_prefix, chips):
    slots = jnp.arange(2 * chips, dtype=jnp.int32)
    wanted = group_prefix[None, :] == slots[:, None]
    final = jnp.max(jnp.where(wanted, slots[None, :], -1), axis=1)
    first = jnp.min(jnp.where(wanted, slots[None, :], 2 * chips), axis=1)
    edge = 2 * jnp.arange(1, chips, dtype=jnp.int32)[:, None]
    right = (slots[None, :] < edge) & (final[None, :] >= edge)
    left = (slots[None, :] >= edge) & (first[None, :] < edge)
    counts = jnp.sum(jnp.stack([right, left]).astype(jnp.int32), axis=2)
    return jnp.max(counts)


def route_choice(slot_ref, group, chips, width):
    number = 2 * chips
    chip, core = group // 2, group % 2
    held = [slot_ref[g] for g in range(number)]
    final, first = [], []
    for s in range(number):
        top, low = jnp.int32(-1), jnp.int32(number)
        for g in range(number):
            top = jnp.where(held[g] == s, g, top)
        for g in reversed(range(number)):
            low = jnp.where(held[g] == s, g, low)
        final.append(top)
        first.append(low)

    def ranks(needs):
        result, count = [], jnp.int32(0)
        for need in needs:
            result.append(count)
            count = count + need.astype(jnp.int32)
        return result

    def right(z):
        return [(s // 2 <= z) & (final[s] >= 2 * (z + 1)) for s in range(number)]

    def left(z):
        return [(s // 2 >= z) & (first[s] < 2 * z) for s in range(number)]

    from_left, from_right = ranks(right(chip - 1)), ranks(left(chip + 1))
    mine = slot_ref[group]
    keep = jnp.int32(0)
    sides = []
    for s in range(number):
        own = chip == s // 2
        value = jnp.where(
            own, s % 2, jnp.where(chip > s // 2, 2 + from_left[s], 2 + 2 * width + from_right[s])
        )
        keep = jnp.where(mine == s, value, keep)
    for needs, source in ((right(chip), from_left), (left(chip), from_right)):
        rank = ranks(needs)
        chosen = []
        for w in range(width):
            place = 2 * w + core
            value = jnp.int32(0)
            for s in range(number):
                value = jnp.where(
                    needs[s] & (rank[s] == place),
                    jnp.where(chip == s // 2, s % 2, 2 + source[s]),
                    value,
                )
            chosen.append(value)
        sides.append(chosen)
    return [keep] + sides[0] + sides[1]


def pick(number, candidates):
    result = candidates[0]
    for i in range(1, len(candidates)):
        result = jnp.where(number == i, candidates[i], result)
    return result


def gather_kernel(
    parts, chips, width, sub,
    slot_ref, tokens, prefix, segment, kv_out,
    packed, own, held_l, held_r, stage_r, stage_l, ag,
    ag_send, ag_recv, a2a_send, a2a_recv, own_send, own_recv,
    r_send, r_recv, l_send, l_recv, rf_send, rf_recv, lf_send, lf_recv,
):
    me = lax.axis_index("tensor")
    group = lax.axis_index("dp")
    chip, core = group // 2, group % 2
    other = 1 - core
    sibling = chip * 2 + other
    groups = 2 * chips
    chunks = parts * sub
    chunk_rows = prefix.shape[0] // sub

    for ref in (held_l, held_r):
        ref[...] = jnp.zeros_like(ref)
    barrier = pltpu.get_barrier_semaphore()
    for d in range(1, parts):
        pl.semaphore_signal(
            barrier, inc=1, device_id={"tensor": lax.rem(me + d, parts)}, device_id_type=MESH
        )
    near = (sibling, lax.rem(group + 2, groups), lax.rem(group + groups - 2, groups))
    for to in near:
        pl.semaphore_signal(barrier, inc=1, device_id={"dp": to}, device_id_type=MESH)

    choice = route_choice(slot_ref, group, chips, width)
    rows_i = lax.broadcasted_iota(jnp.int32, (2 * KVH * HD, LANES), 0)
    cols_i = lax.broadcasted_iota(jnp.int32, (2 * KVH * HD, LANES), 1)
    source = cols_i + jnp.where(cols_i >= HD, KVH * HD - HD, 0)
    for h in range(KVH):
        take = (rows_i == source + h * HD).astype(F32).astype(BF16)
        packed[h] = (
            jnp.dot(prefix[...], take, preferred_element_type=F32)
            .astype(BF16)
            .reshape(sub, chunk_rows, LANES)
        )
    pl.semaphore_wait(barrier, parts - 1 + 3)

    copies = []
    for d in range(parts - 1, 0, -1):
        to = lax.rem(me + d, parts)
        copy = pltpu.make_async_remote_copy(
            src_ref=packed.at[to * KVH // parts],
            dst_ref=own.at[core, pl.ds((parts - d) * sub, sub)],
            send_sem=a2a_send.at[parts - d],
            recv_sem=a2a_recv.at[parts - d],
            device_id={"tensor": to},
            device_id_type=MESH,
        )
        copy.start()
        copies.append(copy)
    own[core, 0:sub] = packed[me * KVH // parts]

    ag[0] = norm_rows(tokens[...])
    def ag_copy(d):
        return pltpu.make_async_remote_copy(
            src_ref=ag.at[0],
            dst_ref=ag.at[d],
            send_sem=ag_send.at[d],
            recv_sem=ag_recv.at[d],
            device_id={"tensor": lax.rem(me + d, parts)},
            device_id_type=MESH,
        )

    def half_copy(slot, place, half, to):
        rows = tokens.shape[0] // 2
        at = pl.ds(half * rows, rows)
        return pltpu.make_async_remote_copy(
            src_ref=ag.at[slot, at],
            dst_ref=ag.at[place, at],
            send_sem=ag_send.at[2 * place + half - 2],
            recv_sem=ag_recv.at[2 * place + half - 2],
            device_id={"tensor": to},
            device_id_type=MESH,
        )

    near_x, near_y = me + 1 - 2 * (me % 2), lax.rem(me + 2, parts)

    def ag_start():
        if parts == 4:
            half_copy(0, 1, 0, near_x).start()
            half_copy(0, 2, 1, near_y).start()
            half_copy(0, 1, 1, near_x).start()
            half_copy(0, 2, 0, near_y).start()
        else:
            for d in range(1, parts):
                ag_copy(d).start()

    def ag_forward():
        if parts == 4:
            half_copy(0, 1, 0, near_x).wait_recv()
            half_copy(1, 3, 0, near_y).start()
            half_copy(0, 2, 1, near_y).wait_recv()
            half_copy(2, 3, 1, near_x).start()

    def ag_finish():
        segment[pl.ds(me, 1)] = ag[0:1]
        if parts == 4:
            half_copy(0, 1, 1, near_x).wait_recv()
            segment[pl.ds(near_x, 1)] = ag[1:2]
            half_copy(0, 2, 0, near_y).wait_recv()
            segment[pl.ds(near_y, 1)] = ag[2:3]
            half_copy(1, 3, 0, near_y).wait_recv()
            half_copy(2, 3, 1, near_x).wait_recv()
            segment[pl.ds(parts - 1 - me, 1)] = ag[3:4]
            for place, half in ((1, 0), (1, 1), (2, 0), (2, 1), (3, 0), (3, 1)):
                half_copy(0, place, half, near_x).wait_send()
        else:
            for d in range(1, parts):
                ag_copy(d).wait_recv()
                segment[pl.ds(lax.rem(me + parts - d, parts), 1)] = ag[d : d + 1]
            for d in range(1, parts):
                ag_copy(d).wait_send()

    def lane_copy(src, dst, send_sem, recv_sem, to):
        return pltpu.make_async_remote_copy(
            src_ref=src, dst_ref=dst, send_sem=send_sem, recv_sem=recv_sem,
            device_id={"dp": to}, device_id_type=MESH,
        )

    def own_copy(m):
        block = own.at[core, pl.ds(m * sub, sub)]
        return lane_copy(block, block, own_send.at[m], own_recv.at[m], sibling)

    last = chips - 1

    def flow(place, to, base, held, stage, send, recv, f_send, f_recv):
        def hop(w, k):
            return lane_copy(
                stage.at[w, k], held.at[w * 2 + core, k], send.at[w, k], recv.at[w, k], to
            )

        def forward(w, k):
            ref = held.at[w * 2 + core, k]
            return lane_copy(ref, ref, f_send.at[w, k], f_recv.at[w, k], sibling)

        def comes(w):
            return (place > w) & (place <= last - w)

        def goes(w):
            return (place >= w) & (place < last - w)

        def receive(s):
            k = s - SKEW * place
            for w in range(width):
                @pl.when((k >= 0) & (k < chunks) & comes(w))
                def _(w=w):
                    hop(w, k).wait_recv()
                    forward(w, k).start()

        def pass_on(s):
            k = s - 1 - SKEW * place
            for w in range(width):
                @pl.when((k >= 0) & (k < chunks) & comes(w))
                def _(w=w):
                    forward(w, k).wait_recv()
            for w in range(width):
                @pl.when((k >= 0) & (k < chunks) & goes(w))
                def _(w=w):
                    stage[w, k] = pick(
                        choice[base + w],
                        [own[0, k], own[1, k]] + [held[i, k] for i in range(2 * width)],
                    )
                    hop(w, k).start()

        def drain(k):
            for w in range(width):
                @pl.when(goes(w))
                def _(w=w):
                    hop(w, k).wait_send()
                @pl.when(comes(w))
                def _(w=w):
                    forward(w, k).wait_send()

        return receive, pass_on, drain

    flows = (
        flow(chip, lax.rem(group + 2, groups), 1,
             held_l, stage_r, r_send, r_recv, rf_send, rf_recv),
        flow(last - chip, lax.rem(group + groups - 2, groups), 1 + width,
             held_r, stage_l, l_send, l_recv, lf_send, lf_recv),
    )

    def step(s, carry):
        m = s // sub

        @pl.when((m < parts) & (s % sub == 0))
        def _():
            @pl.when(m > 0)
            def _():
                pltpu.make_async_remote_copy(
                    src_ref=packed.at[0],
                    dst_ref=own.at[core, pl.ds(m * sub, sub)],
                    send_sem=a2a_send.at[m],
                    recv_sem=a2a_recv.at[m],
                    device_id={"tensor": lax.rem(me + 1, parts)},
                    device_id_type=MESH,
                ).wait_recv()

            own_copy(m).start()
            pl.when(m == parts // 2)(ag_start)

        for receive, _, _ in flows:
            receive(s)
        before = s - 1

        @pl.when((before >= 0) & (before // sub < parts) & (before % sub == 0))
        def _():
            own_copy(before // sub).wait_recv()

        for _, pass_on, _ in flows:
            pass_on(s)
        pl.when(s == parts * sub - 1)(ag_forward)
        return carry

    lax.fori_loop(0, chunks + SKEW * last + 1, step, 0)

    def finish(k, carry):
        kv_out[k] = pick(
            choice[0],
            [own[0, k], own[1, k]]
            + [held_l[i, k] for i in range(2 * width)]
            + [held_r[i, k] for i in range(2 * width)],
        )
        return carry

    lax.fori_loop(0, chunks, finish, 0)

    def drain(k, carry):
        for _, _, end in flows:
            end(k)
        return carry

    lax.fori_loop(0, chunks, drain, 0)
    for m in range(parts):
        own_copy(m).wait_send()
    for copy in copies:
        copy.wait_send()
    ag_finish()


def gather(slots, tokens, prefix, parts, chips, width, identity):
    rows, model = tokens.shape
    shard = prefix.shape[0]
    sub = 4 if shard >= 1024 else 2
    chunks = parts * sub
    piece = (chunks, shard // sub, LANES)
    dma = pltpu.SemaphoreType.DMA
    lane = [dma((width, chunks))] * 8
    segment, kv = pl.pallas_call(
        functools.partial(gather_kernel, parts, chips, width, sub),
        out_shape=(
            jax.ShapeDtypeStruct((parts, rows, model), BF16),
            jax.ShapeDtypeStruct(piece, BF16),
        ),
        in_specs=[SMEM, VMEM, VMEM],
        out_specs=(VMEM, VMEM),
        scratch_shapes=[
            pltpu.VMEM((KVH, sub, shard // sub, LANES), BF16),
            pltpu.VMEM((2,) + piece, BF16),
            pltpu.VMEM((2 * width,) + piece, BF16),
            pltpu.VMEM((2 * width,) + piece, BF16),
            pltpu.VMEM((width,) + piece, BF16),
            pltpu.VMEM((width,) + piece, BF16),
            pltpu.VMEM((parts, rows, model), BF16),
        ]
        + [dma((max(parts, 6),))] * 2
        + [dma((parts,))] * 4
        + lane,
        compiler_params=pltpu.CompilerParams(
            collective_id=identity, has_side_effects=True, vmem_limit_bytes=52 * MIB
        ),
        name="gather",
    )(slots, tokens, prefix)
    return segment.reshape(parts * rows, model), kv.reshape(PLEN, LANES)


def attention_kernel(heads, parts, *refs):
    (x_ref, wq_ref, wkv_ref, cos_ref, sin_ref, begin_ref, kv_ref) = refs[:7]
    if parts == 4:
        ow, out_ref, ow_all, queries, keys, values, scores, w_send, w_recv, s_send, s_recv = refs[7:]
        me = lax.axis_index("tensor")
        group = lax.axis_index("dp")
        core = group % 2
        sibling = group + 1 - 2 * core
        near_x, near_y = me + 1 - 2 * (me % 2), lax.rem(me + 2, parts)
        quarter = ow.shape[0] // 4

        def piece(src, place, half, to):
            at = pl.ds((2 * core + half) * quarter, quarter)
            return pltpu.make_async_remote_copy(
                src_ref=ow.at[at] if src == 0 else ow_all.at[src, at],
                dst_ref=ow_all.at[place, at],
                send_sem=w_send.at[2 * place + half - 2],
                recv_sem=w_recv.at[2 * place + half - 2],
                device_id={"tensor": to},
                device_id_type=MESH,
            )

        def share(place):
            ref = ow_all.at[place, pl.ds(2 * core * quarter, 2 * quarter)]
            return pltpu.make_async_remote_copy(
                src_ref=ref, dst_ref=ref, send_sem=s_send.at[place - 1],
                recv_sem=s_recv.at[place - 1], device_id={"dp": sibling}, device_id_type=MESH,
            )

        barrier = pltpu.get_barrier_semaphore()
        for to in ({"tensor": near_x}, {"tensor": near_y}, {"dp": sibling}):
            pl.semaphore_signal(barrier, inc=1, device_id=to, device_id_type=MESH)
        pl.semaphore_wait(barrier, 3)
        piece(0, 1, 0, near_x).start()
        piece(0, 2, 1, near_y).start()
        piece(0, 1, 1, near_x).start()
        piece(0, 2, 0, near_y).start()
        ow_all[0] = ow[...]
    else:
        out_ref, queries, keys, values, scores = refs[7:]
    rows = x_ref.shape[0]
    lane = lax.broadcasted_iota(jnp.int32, (1, LANES), 1)
    former = (lane % HD) < HD // 2
    low = lane < HD

    def rotated(tile, cos_table, sin_table):
        swapped = jnp.where(
            former, -pltpu.roll(tile, LANES - HD // 2, 1), pltpu.roll(tile, HD // 2, 1)
        )
        return tile * cos_table + swapped * sin_table

    x = x_ref[...]
    mapped = jnp.dot(x, wq_ref[...], preferred_element_type=F32)
    cos_table, sin_table = cos_ref[...], sin_ref[...]
    for h in range(heads):
        if h % 2 == 0:
            tile = mapped[:, (h // 2) * LANES : (h // 2 + 1) * LANES]
            tile = rotated(tile, cos_table, sin_table).astype(BF16).astype(F32) * 0.125
            head = tile
        else:
            head = pltpu.roll(tile, HD, 1)
        queries[h] = jnp.where(low, head, 0.0).astype(BF16)
    pair = jnp.dot(x, wkv_ref[...], preferred_element_type=F32)
    pair = jnp.where(low, rotated(pair, cos_table, sin_table), pair)
    keys[0:PLEN, :] = kv_ref[...]
    keys[PLEN:, :] = pair.astype(BF16)
    values[...] = jnp.where(low, 1.0, keys[...].astype(F32)).astype(BF16)

    block = 256 if rows % 256 == 0 else rows
    step = 512
    total = PLEN + rows
    per_head = rows // block
    pairs = (heads + 1) // 2

    def one_head(h, start, slot):
        query = queries[h, pl.ds(start, block), :]
        top = jnp.full((block, LANES), NEG_FILL, F32)
        for n in range(total // step):
            part = lax.dot_general(
                query, keys[n * step : (n + 1) * step, :], (((1,), (1,)), ((), ())),
                preferred_element_type=F32,
            )
            if n * step >= PLEN:
                place = lax.broadcasted_iota(jnp.int32, (block, step), 1) + (n * step - PLEN)
                row = lax.broadcasted_iota(jnp.int32, (block, step), 0) + start
                seen = (place >= begin_ref[pl.ds(start, block), 0:1]) & (place <= row)
                part = jnp.where(seen, part, NEG_FILL)
            scores[slot, :, n * step : (n + 1) * step] = part
            for q in range(step // LANES):
                top = jnp.maximum(top, part[:, q * LANES : (q + 1) * LANES])
        top = jnp.max(top, axis=1, keepdims=True)
        blended = jnp.zeros((block, LANES), F32)
        for n in range(total // step):
            weight = jnp.exp(scores[slot, :, n * step : (n + 1) * step] - top).astype(BF16)
            blended += jnp.dot(
                weight, values[n * step : (n + 1) * step, :], preferred_element_type=F32
            )
        return blended

    def one(i, carry):
        if parts == 4:
            @pl.when(i == 1)
            def _():
                piece(0, 1, 0, near_x).wait_recv()
                piece(1, 3, 0, near_y).start()
                piece(0, 2, 1, near_y).wait_recv()
                piece(2, 3, 1, near_x).start()

            @pl.when(i == pairs * per_head - 1)
            def _():
                piece(0, 1, 1, near_x).wait_recv()
                share(1).start()
                piece(0, 2, 0, near_y).wait_recv()
                share(2).start()

        p, b = i // per_head, i % per_head
        start = pl.multiple_of(b * block, block)
        even = one_head(2 * p, start, 0)
        even = pltpu.roll(even, HD, 1) / even
        if heads > 1:
            odd = one_head(2 * p + 1, start, 1)
            odd = odd / pltpu.roll(odd, HD, 1)
        else:
            odd = jnp.zeros_like(even)
        at = pl.ds(pl.multiple_of(p * LANES, LANES), LANES)
        out_ref[pl.ds(start, block), at] = jnp.where(low, even, odd).astype(BF16)
        return carry

    lax.fori_loop(0, pairs * per_head, one, 0)
    if parts == 4:
        piece(1, 3, 0, near_y).wait_recv()
        piece(2, 3, 1, near_x).wait_recv()
        share(3).start()
        for place in (1, 2, 3):
            share(place).wait_recv()
        for place in (1, 2, 3):
            share(place).wait_send()
            for half in range(2):
                piece(0, place, half, near_x).wait_send()


def attention(x, wq, wkv, cos_table, sin_table, begins, kv, out_w, heads, parts, identity):
    rows = x.shape[0]
    total = PLEN + rows
    block = 256 if rows % 256 == 0 else rows
    width = (heads + 1) // 2 * LANES
    exchange = parts == 4
    shapes = [jax.ShapeDtypeStruct((rows, width), BF16)]
    operands = [x, wq, wkv, cos_table, sin_table, begins, kv]
    scratch = [
        pltpu.VMEM((heads, rows, LANES), BF16),
        pltpu.VMEM((total, LANES), BF16),
        pltpu.VMEM((total, LANES), BF16),
        pltpu.VMEM((2, block, total), F32),
    ]
    params = dict(vmem_limit_bytes=52 * MIB)
    if exchange:
        operands.append(out_w)
        shapes.append(jax.ShapeDtypeStruct((parts,) + out_w.shape, BF16))
        scratch += [pltpu.SemaphoreType.DMA((6,))] * 2 + [pltpu.SemaphoreType.DMA((3,))] * 2
        params.update(collective_id=identity, has_side_effects=True)
    return pl.pallas_call(
        functools.partial(attention_kernel, heads, parts),
        out_shape=shapes,
        in_specs=[VMEM] * len(operands),
        out_specs=[VMEM] * len(shapes),
        scratch_shapes=scratch,
        compiler_params=pltpu.CompilerParams(**params),
        name="attention",
    )(*operands)


def mlp_kernel(
    parts, att, out_w, tokens, gate_up, down, result,
    gu_v, dn_v, a_send, a_recv, rows_v, f_send, f_recv, hidden,
    w_sem, as_sem, ar_sem, gs_sem, gr_sem, fs_sem, fr_sem,
):
    me = lax.axis_index("tensor")
    rows = tokens.shape[0]
    model = tokens.shape[1]
    units = hidden.shape[1]
    loads = [
        pltpu.make_async_copy(gate_up, gu_v, w_sem.at[0]),
        pltpu.make_async_copy(down, dn_v, w_sem.at[1]),
    ]
    for load in loads:
        load.start()
    barrier = pltpu.get_barrier_semaphore()
    for d in range(1, parts):
        pl.semaphore_signal(
            barrier, inc=1, device_id={"tensor": lax.rem(me + d, parts)}, device_id_type=MESH
        )

    def send(src, dst, send_sem, recv_sem, to):
        return pltpu.make_async_remote_copy(
            src_ref=src, dst_ref=dst, send_sem=send_sem, recv_sem=recv_sem,
            device_id={"tensor": to}, device_id_type=MESH,
        )

    def partial_out(owner):
        start = pl.multiple_of(owner * rows, rows)
        return jnp.dot(
            att[pl.ds(start, rows), :], out_w[...], preferred_element_type=F32
        ).astype(BF16)

    copies = []
    for d in range(1, parts):
        to = lax.rem(me + d, parts)
        a_send[d] = partial_out(to)
        if d == 1:
            pl.semaphore_wait(barrier, parts - 1)
        copy = send(a_send.at[d], a_recv.at[d], as_sem.at[d], ar_sem.at[d], to)
        copy.start()
        copies.append(copy)
    total = partial_out(me).astype(F32)
    for d in range(1, parts):
        copies[d - 1].wait_recv()
        total += a_recv[d].astype(F32)
    middle = (tokens[...].astype(F32) + total).astype(BF16)
    a_send[0] = middle
    rows_v[0] = norm_rows(middle)
    sends = []
    for d in range(1, parts):
        copy = send(
            rows_v.at[0], rows_v.at[d], gs_sem.at[d], gr_sem.at[d], lax.rem(me + d, parts)
        )
        copy.start()
        sends.append(copy)
    for load in loads:
        load.wait()

    tile = 256 if units % 256 == 0 else units
    out_tile = 512
    backs = []
    for d in range(parts):
        if d > 0:
            sends[d - 1].wait_recv()

        def up(i, carry, d=d):
            if tile == units:
                at = slice(None)
            else:
                at = pl.ds(pl.multiple_of(i * tile, tile), tile)
            x = rows_v[d]
            gate = jnp.dot(x, gu_v[0, :, at], preferred_element_type=F32)
            raised = jnp.dot(x, gu_v[1, :, at], preferred_element_type=F32)
            hidden[:, at] = (gate / (1.0 + jnp.exp(-gate)) * raised).astype(BF16)
            return carry

        lax.fori_loop(0, units // tile, up, 0)

        def lower(i, carry, d=d):
            at = pl.ds(pl.multiple_of(i * out_tile, out_tile), out_tile)
            f_send[d, :, at] = jnp.dot(
                hidden[...], dn_v[:, at], preferred_element_type=F32
            ).astype(BF16)
            return carry

        lax.fori_loop(0, model // out_tile, lower, 0)
        if d > 0:
            owner = lax.rem(me + parts - d, parts)
            copy = send(f_send.at[d], f_recv.at[d], fs_sem.at[d], fr_sem.at[d], owner)
            copy.start()
            backs.append(copy)
    total = f_send[0].astype(F32)
    for d in range(1, parts):
        backs[d - 1].wait_recv()
        total += f_recv[d].astype(F32)
    result[...] = (a_send[0].astype(F32) + total).astype(BF16)
    for copy in copies + sends + backs:
        copy.wait_send()


def mlp_square_kernel(
    att, out_w, tokens, gate_up, down, result,
    gu_v, dn_v, att_v, mid_v, rows_v, f_v, f_in, hidden,
    w_sem, as_sem, ar_sem, gs_sem, gr_sem, fs_sem, fr_sem,
):
    parts = 4
    me = lax.axis_index("tensor")
    near_x, near_y, far = me + 1 - 2 * (me % 2), lax.rem(me + 2, parts), parts - 1 - me
    rows, model = tokens.shape
    half_rows = rows // 2
    units = hidden.shape[1]
    loads = [
        pltpu.make_async_copy(gate_up, gu_v, w_sem.at[0]),
        pltpu.make_async_copy(down, dn_v, w_sem.at[1]),
    ]
    for load in loads:
        load.start()
    barrier = pltpu.get_barrier_semaphore()
    for to in (near_x, near_y, far):
        pl.semaphore_signal(barrier, inc=1, device_id={"tensor": to}, device_id_type=MESH)
    pl.semaphore_wait(barrier, parts - 1)

    def send(src, dst, send_sem, recv_sem, to):
        return pltpu.make_async_remote_copy(
            src_ref=src, dst_ref=dst, send_sem=send_sem, recv_sem=recv_sem,
            device_id={"tensor": to}, device_id_type=MESH,
        )

    def cut(half):
        return pl.ds(half * half_rows, half_rows)

    def block_of(owner):
        return att.at[pl.ds(pl.multiple_of(owner * rows, rows), rows)]

    swaps = [
        send(block_of(to), att_v.at[slot], as_sem.at[slot], ar_sem.at[slot], to)
        for slot, to in ((3, far), (1, near_x), (2, near_y))
    ]
    for copy in swaps:
        copy.start()

    def group_term(block, slot):
        term = jnp.dot(block, out_w[slot], preferred_element_type=F32)
        return term.astype(BF16).astype(F32)

    total = group_term(att[pl.ds(pl.multiple_of(me * rows, rows), rows), :], 0)
    for copy, slot in zip(swaps[1:] + swaps[:1], (1, 2, 3)):
        copy.wait_recv()
        total += group_term(att_v[slot], slot)
    middle = (tokens[...].astype(F32) + total).astype(BF16)
    mid_v[...] = middle
    rows_v[0] = norm_rows(middle)

    def piece(src, place, half, to):
        at = 2 * place + half - 2
        return send(
            rows_v.at[src, cut(half)], rows_v.at[place, cut(half)],
            gs_sem.at[at], gr_sem.at[at], to,
        )

    piece(0, 1, 0, near_x).start()
    piece(0, 2, 1, near_y).start()
    piece(0, 1, 1, near_x).start()
    piece(0, 2, 0, near_y).start()
    for load in loads:
        load.wait()

    tile = 256 if units % 256 == 0 else units
    out_tile = 512

    def feed(first, count):
        many = count * rows

        def up(i, carry):
            at = pl.ds(pl.multiple_of(i * tile, tile), tile)
            x = rows_v[first : first + count].reshape(many, model)
            gate = jnp.dot(x, gu_v[0, :, at], preferred_element_type=F32)
            raised = jnp.dot(x, gu_v[1, :, at], preferred_element_type=F32)
            hidden[0:many, at] = (gate / (1.0 + jnp.exp(-gate)) * raised).astype(BF16)
            return carry

        lax.fori_loop(0, units // tile, up, 0)

        def lower(i, carry):
            at = pl.ds(pl.multiple_of(i * out_tile, out_tile), out_tile)
            f_v[first : first + count, :, at] = (
                jnp.dot(hidden[0:many, :], dn_v[:, at], preferred_element_type=F32)
                .astype(BF16)
                .reshape(count, rows, out_tile)
            )
            return carry

        lax.fori_loop(0, model // out_tile, lower, 0)

    def back(slot, half, place, to):
        at = 2 * place + half
        return send(
            f_v.at[slot, cut(half)], f_in.at[place, cut(half)], fs_sem.at[at], fr_sem.at[at], to
        )

    feed(0, 1)
    piece(0, 1, 0, near_x).wait_recv()
    piece(1, 3, 0, near_y).start()
    piece(0, 2, 1, near_y).wait_recv()
    piece(2, 3, 1, near_x).start()
    piece(0, 1, 1, near_x).wait_recv()
    piece(0, 2, 0, near_y).wait_recv()
    feed(1, 2)
    back(1, 0, 0, near_x).start()
    back(2, 1, 1, near_y).start()
    piece(1, 3, 0, near_y).wait_recv()
    piece(2, 3, 1, near_x).wait_recv()
    feed(3, 1)
    back(3, 0, 2, near_x).start()
    back(3, 1, 2, near_y).start()
    for half, slot, place, to in ((0, 2, 1, near_y), (1, 1, 0, near_x)):
        back(3, half, 2, to).wait_recv()
        f_v[slot, cut(half)] = (
            f_v[slot, cut(half)].astype(F32) + f_in[2, cut(half)].astype(F32)
        ).astype(BF16)
        back(slot, half, place, to).start()
    order = ((1, 0, 0, near_x), (2, 1, 1, near_y), (2, 0, 1, near_y), (1, 1, 0, near_x))
    for slot, half, place, to in order:
        back(slot, half, place, to).wait_recv()
    total = f_v[0].astype(F32) + f_in[0].astype(F32) + f_in[1].astype(F32)
    result[...] = (mid_v[...].astype(F32) + total).astype(BF16)
    for copy in swaps:
        copy.wait_send()
    for place in (1, 2, 3):
        for half in range(2):
            piece(0, place, half, near_x).wait_send()
            back(1, half, place - 1, near_x).wait_send()


def mlp_square(att, out_w, tokens, gate_up, down, identity):
    rows, model = tokens.shape
    parts = 4
    dma = pltpu.SemaphoreType.DMA
    full = pltpu.VMEM((parts, rows, model), BF16)
    return pl.pallas_call(
        mlp_square_kernel,
        out_shape=jax.ShapeDtypeStruct((rows, model), BF16),
        in_specs=[VMEM, VMEM, VMEM, ANY, ANY],
        out_specs=VMEM,
        scratch_shapes=[
            pltpu.VMEM(gate_up.shape, BF16),
            pltpu.VMEM(down.shape, BF16),
            pltpu.VMEM((parts, rows, att.shape[1]), BF16),
            pltpu.VMEM((rows, model), BF16),
            full, full,
            pltpu.VMEM((3, rows, model), BF16),
            pltpu.VMEM((2 * rows, down.shape[0]), BF16),
            dma((2,)), dma((parts,)), dma((parts,)),
        ]
        + [dma((6,))] * 4,
        compiler_params=pltpu.CompilerParams(
            collective_id=identity, has_side_effects=True, vmem_limit_bytes=52 * MIB
        ),
        name="mlp",
    )(att, out_w, tokens, gate_up, down)


def mlp(att, out_w, tokens, gate_up, down, parts, identity):
    rows, model = tokens.shape
    dma = pltpu.SemaphoreType.DMA
    full = pltpu.VMEM((parts, rows, model), BF16)
    return pl.pallas_call(
        functools.partial(mlp_kernel, parts),
        out_shape=jax.ShapeDtypeStruct((rows, model), BF16),
        in_specs=[VMEM, VMEM, VMEM, ANY, ANY],
        out_specs=VMEM,
        scratch_shapes=[
            pltpu.VMEM(gate_up.shape, BF16),
            pltpu.VMEM(down.shape, BF16),
            full, full, full, full, full,
            pltpu.VMEM((rows, down.shape[0]), BF16),
            dma((2,)),
        ]
        + [dma((parts,))] * 6,
        compiler_params=pltpu.CompilerParams(
            collective_id=identity, has_side_effects=True, vmem_limit_bytes=52 * MIB
        ),
        name="mlp",
    )(att, out_w, tokens, gate_up, down)


def on_device(
    tokens,
    lengths,
    group_prefix,
    prefix_cache,
    query_weight,
    key_weight,
    value_weight,
    out_weight,
    gate_up_weight,
    down_weight,
):
    parts = lax.axis_size("tensor")
    chips = lax.axis_size("dp") // 2
    rank = lax.axis_index("tensor")
    rows = tokens.shape[0] * parts
    heads = query_weight.shape[1] // HD
    kv_head = rank * heads // (QH // KVH)

    most = most_crossing(group_prefix, chips)

    def routed(width, identity):
        def run(prefix, rows_in):
            return gather(group_prefix, rows_in, prefix, parts, chips, width, identity)
        return run

    segment, kv = lax.cond(
        most <= 2, routed(1, 0), routed(chips // 2, 1), prefix_cache, tokens
    )

    positions, begins = token_layout(lengths[0], rows)
    cos_half, sin_half = rope_tables(positions)
    cos_table = jnp.concatenate([cos_half] * 4, axis=1)
    sin_table = jnp.concatenate([sin_half] * 4, axis=1)
    wkv = jnp.concatenate(
        [
            lax.dynamic_slice_in_dim(key_weight, kv_head * HD, HD, 1),
            lax.dynamic_slice_in_dim(value_weight, kv_head * HD, HD, 1),
        ],
        axis=1,
    )
    wq = query_weight
    if heads % 2:
        wq = jnp.pad(wq, ((0, 0), (0, HD)))
    outputs = attention(
        segment, wq, wkv, cos_table, sin_table, begins[:, None], kv, out_weight, heads, parts, 3
    )
    if parts == 4:
        return mlp_square(*outputs, tokens, gate_up_weight, down_weight, 2)
    out_w = out_weight
    if heads % 2:
        out_w = jnp.pad(out_w, ((0, HD), (0, 0)))
    return mlp(outputs[0], out_w, tokens, gate_up_weight, down_weight, parts, 2)


def solution(mesh):
    return jax.shard_map(
        on_device,
        mesh=mesh,
        in_specs=(
            P(("dp", "tensor"), None),
            P("dp", None),
            P(),
            P(("dp", "tensor"), None),
            P(None, "tensor"),
            P(),
            P(),
            P("tensor", None),
            P(None, None, "tensor"),
            P("tensor", None),
        ),
        out_specs=P(("dp", "tensor"), None),
        check_vma=False,
    )
```

```python
import functools
import math

import jax
import jax.numpy as jnp
from jax import lax
from jax.experimental import pallas as pl
from jax.experimental.pallas import tpu as pltpu
from jax.sharding import PartitionSpec as P

QH = 16
KVH = 4
HD = 64
PLEN = 4096
LANES = 128
SKEW = 3
NEG_FILL = -1e30
VMEM = pl.BlockSpec(memory_space=pltpu.VMEM)
SMEM = pl.BlockSpec(memory_space=pltpu.SMEM)
ANY = pl.BlockSpec(memory_space=pl.ANY)
MESH = pl.DeviceIdType.MESH
BF16 = jnp.bfloat16
F32 = jnp.float32
MIB = 1 << 20


def norm_rows(inputs):
    floats = inputs.astype(F32)
    mean = jnp.mean(floats * floats, axis=-1, keepdims=True)
    return (floats * lax.rsqrt(mean + 1e-05)).astype(BF16)


def most_crossing(group_prefix, chips):
    slots = jnp.arange(2 * chips, dtype=jnp.int32)
    wanted = group_prefix[None, :] == slots[:, None]
    final = jnp.max(jnp.where(wanted, slots[None, :], -1), axis=1)
    first = jnp.min(jnp.where(wanted, slots[None, :], 2 * chips), axis=1)
    edge = 2 * jnp.arange(1, chips, dtype=jnp.int32)[:, None]
    right = (slots[None, :] < edge) & (final[None, :] >= edge)
    left = (slots[None, :] >= edge) & (first[None, :] < edge)
    counts = jnp.sum(jnp.stack([right, left]).astype(jnp.int32), axis=2)
    return jnp.max(counts)


def route_choice(slot_ref, group, chips, width):
    number = 2 * chips
    chip, core = group // 2, group % 2
    held = [slot_ref[g] for g in range(number)]
    final, first = [], []
    for s in range(number):
        top, low = jnp.int32(-1), jnp.int32(number)
        for g in range(number):
            top = jnp.where(held[g] == s, g, top)
        for g in reversed(range(number)):
            low = jnp.where(held[g] == s, g, low)
        final.append(top)
        first.append(low)

    def ranks(needs):
        result, count = [], jnp.int32(0)
        for need in needs:
            result.append(count)
            count = count + need.astype(jnp.int32)
        return result

    def right(z):
        return [(s // 2 <= z) & (final[s] >= 2 * (z + 1)) for s in range(number)]

    def left(z):
        return [(s // 2 >= z) & (first[s] < 2 * z) for s in range(number)]

    from_left, from_right = ranks(right(chip - 1)), ranks(left(chip + 1))
    mine = slot_ref[group]
    keep = jnp.int32(0)
    sides = []
    for s in range(number):
        own = chip == s // 2
        value = jnp.where(
            own, s % 2, jnp.where(chip > s // 2, 2 + from_left[s], 2 + 2 * width + from_right[s])
        )
        keep = jnp.where(mine == s, value, keep)
    for needs, source in ((right(chip), from_left), (left(chip), from_right)):
        rank = ranks(needs)
        chosen = []
        for w in range(width):
            place = 2 * w + core
            value = jnp.int32(0)
            for s in range(number):
                value = jnp.where(
                    needs[s] & (rank[s] == place),
                    jnp.where(chip == s // 2, s % 2, 2 + source[s]),
                    value,
                )
            chosen.append(value)
        sides.append(chosen)
    return [keep] + sides[0] + sides[1]


def pick(number, candidates):
    result = candidates[0]
    for i in range(1, len(candidates)):
        result = jnp.where(number == i, candidates[i], result)
    return result


def gather_kernel(parts, chips, width, sub, *refs):
    if parts == 4:
        ow, ow_all, w_send, w_recv, share_send, share_recv = refs[3], refs[6], *refs[-4:]
        refs = refs[:3] + refs[4:6] + refs[7:-4]
    (
    slot_ref, tokens, prefix, segment, kv_out,
    packed, own, held_l, held_r, stage_r, stage_l, ag,
    ag_send, ag_recv, a2a_send, a2a_recv, own_send, own_recv,
    r_send, r_recv, l_send, l_recv, rf_send, rf_recv, lf_send, lf_recv,
    ) = refs
    me = lax.axis_index("tensor")
    group = lax.axis_index("dp")
    chip, core = group // 2, group % 2
    other = 1 - core
    sibling = chip * 2 + other
    groups = 2 * chips
    chunks = parts * sub
    chunk_rows = prefix.shape[0] // sub

    for ref in (held_l, held_r):
        ref[...] = jnp.zeros_like(ref)
    barrier = pltpu.get_barrier_semaphore()
    for d in range(1, parts):
        pl.semaphore_signal(
            barrier, inc=1, device_id={"tensor": lax.rem(me + d, parts)}, device_id_type=MESH
        )
    near = (sibling, lax.rem(group + 2, groups), lax.rem(group + groups - 2, groups))
    for to in near:
        pl.semaphore_signal(barrier, inc=1, device_id={"dp": to}, device_id_type=MESH)

    choice = route_choice(slot_ref, group, chips, width)
    rows_i = lax.broadcasted_iota(jnp.int32, (2 * KVH * HD, LANES), 0)
    cols_i = lax.broadcasted_iota(jnp.int32, (2 * KVH * HD, LANES), 1)
    source = cols_i + jnp.where(cols_i >= HD, KVH * HD - HD, 0)
    for h in range(KVH):
        take = (rows_i == source + h * HD).astype(F32).astype(BF16)
        packed[h] = (
            jnp.dot(prefix[...], take, preferred_element_type=F32)
            .astype(BF16)
            .reshape(sub, chunk_rows, LANES)
        )
    pl.semaphore_wait(barrier, parts - 1 + 3)

    copies = []
    for d in range(parts - 1, 0, -1):
        to = lax.rem(me + d, parts)
        copy = pltpu.make_async_remote_copy(
            src_ref=packed.at[to * KVH // parts],
            dst_ref=own.at[core, pl.ds((parts - d) * sub, sub)],
            send_sem=a2a_send.at[parts - d],
            recv_sem=a2a_recv.at[parts - d],
            device_id={"tensor": to},
            device_id_type=MESH,
        )
        copy.start()
        copies.append(copy)
    own[core, 0:sub] = packed[me * KVH // parts]

    ag[0] = norm_rows(tokens[...])
    def ag_copy(d):
        return pltpu.make_async_remote_copy(
            src_ref=ag.at[0],
            dst_ref=ag.at[d],
            send_sem=ag_send.at[d],
            recv_sem=ag_recv.at[d],
            device_id={"tensor": lax.rem(me + d, parts)},
            device_id_type=MESH,
        )

    def half_copy(slot, place, half, to):
        rows = tokens.shape[0] // 2
        at = pl.ds(half * rows, rows)
        return pltpu.make_async_remote_copy(
            src_ref=ag.at[slot, at],
            dst_ref=ag.at[place, at],
            send_sem=ag_send.at[2 * place + half - 2],
            recv_sem=ag_recv.at[2 * place + half - 2],
            device_id={"tensor": to},
            device_id_type=MESH,
        )

    near_x, near_y = me + 1 - 2 * (me % 2), lax.rem(me + 2, parts)

    def ag_start():
        if parts == 4:
            half_copy(0, 1, 0, near_x).start()
            half_copy(0, 2, 1, near_y).start()
            half_copy(0, 1, 1, near_x).start()
            half_copy(0, 2, 0, near_y).start()
        else:
            for d in range(1, parts):
                ag_copy(d).start()

    def ag_forward():
        if parts == 4:
            half_copy(0, 1, 0, near_x).wait_recv()
            half_copy(1, 3, 0, near_y).start()
            half_copy(0, 2, 1, near_y).wait_recv()
            half_copy(2, 3, 1, near_x).start()

    def ag_finish():
        segment[pl.ds(me, 1)] = ag[0:1]
        if parts == 4:
            half_copy(0, 1, 1, near_x).wait_recv()
            segment[pl.ds(near_x, 1)] = ag[1:2]
            half_copy(0, 2, 0, near_y).wait_recv()
            segment[pl.ds(near_y, 1)] = ag[2:3]
            half_copy(1, 3, 0, near_y).wait_recv()
            half_copy(2, 3, 1, near_x).wait_recv()
            segment[pl.ds(parts - 1 - me, 1)] = ag[3:4]
            for place, half in ((1, 0), (1, 1), (2, 0), (2, 1), (3, 0), (3, 1)):
                half_copy(0, place, half, near_x).wait_send()
        else:
            for d in range(1, parts):
                ag_copy(d).wait_recv()
                segment[pl.ds(lax.rem(me + parts - d, parts), 1)] = ag[d : d + 1]
            for d in range(1, parts):
                ag_copy(d).wait_send()

    def weight_piece(src, place, half, to):
        quarter = ow.shape[0] // 4
        at = pl.ds((2 * core + half) * quarter, quarter)
        return pltpu.make_async_remote_copy(
            src_ref=ow.at[at] if src == 0 else ow_all.at[src, at],
            dst_ref=ow_all.at[place, at],
            send_sem=w_send.at[2 * place + half - 2],
            recv_sem=w_recv.at[2 * place + half - 2],
            device_id={"tensor": to},
            device_id_type=MESH,
        )

    def share(place):
        quarter = ow.shape[0] // 4
        ref = ow_all.at[place, pl.ds(2 * core * quarter, 2 * quarter)]
        return pltpu.make_async_remote_copy(
            src_ref=ref, dst_ref=ref, send_sem=share_send.at[place - 1],
            recv_sem=share_recv.at[place - 1], device_id={"dp": sibling}, device_id_type=MESH,
        )

    def weight_start():
        weight_piece(0, 1, 0, near_x).start()
        weight_piece(0, 2, 1, near_y).start()
        weight_piece(0, 1, 1, near_x).start()
        weight_piece(0, 2, 0, near_y).start()
        ow_all[0] = ow[...]

    def weight_forward():
        weight_piece(0, 1, 0, near_x).wait_recv()
        weight_piece(1, 3, 0, near_y).start()
        weight_piece(0, 2, 1, near_y).wait_recv()
        weight_piece(2, 3, 1, near_x).start()

    def weight_share():
        weight_piece(0, 1, 1, near_x).wait_recv()
        share(1).start()
        weight_piece(0, 2, 0, near_y).wait_recv()
        share(2).start()

    def weight_finish():
        weight_piece(1, 3, 0, near_y).wait_recv()
        weight_piece(2, 3, 1, near_x).wait_recv()
        share(3).start()

    def weight_end():
        for place in (1, 2, 3):
            share(place).wait_recv()
        for place in (1, 2, 3):
            share(place).wait_send()
            for half in range(2):
                weight_piece(0, place, half, near_x).wait_send()

    def lane_copy(src, dst, send_sem, recv_sem, to):
        return pltpu.make_async_remote_copy(
            src_ref=src, dst_ref=dst, send_sem=send_sem, recv_sem=recv_sem,
            device_id={"dp": to}, device_id_type=MESH,
        )

    def own_copy(m):
        block = own.at[core, pl.ds(m * sub, sub)]
        return lane_copy(block, block, own_send.at[m], own_recv.at[m], sibling)

    last = chips - 1

    def flow(place, to, base, held, stage, send, recv, f_send, f_recv):
        def hop(w, k):
            return lane_copy(
                stage.at[w, k], held.at[w * 2 + core, k], send.at[w, k], recv.at[w, k], to
            )

        def forward(w, k):
            ref = held.at[w * 2 + core, k]
            return lane_copy(ref, ref, f_send.at[w, k], f_recv.at[w, k], sibling)

        def comes(w):
            return (place > w) & (place <= last - w)

        def goes(w):
            return (place >= w) & (place < last - w)

        def receive(s):
            k = s - SKEW * place
            for w in range(width):
                @pl.when((k >= 0) & (k < chunks) & comes(w))
                def _(w=w):
                    hop(w, k).wait_recv()
                    forward(w, k).start()

        def pass_on(s):
            k = s - 1 - SKEW * place
            for w in range(width):
                @pl.when((k >= 0) & (k < chunks) & comes(w))
                def _(w=w):
                    forward(w, k).wait_recv()
            for w in range(width):
                @pl.when((k >= 0) & (k < chunks) & goes(w))
                def _(w=w):
                    stage[w, k] = pick(
                        choice[base + w],
                        [own[0, k], own[1, k]] + [held[i, k] for i in range(2 * width)],
                    )
                    hop(w, k).start()

        def drain(k):
            for w in range(width):
                @pl.when(goes(w))
                def _(w=w):
                    hop(w, k).wait_send()
                @pl.when(comes(w))
                def _(w=w):
                    forward(w, k).wait_send()

        return receive, pass_on, drain

    flows = (
        flow(chip, lax.rem(group + 2, groups), 1,
             held_l, stage_r, r_send, r_recv, rf_send, rf_recv),
        flow(last - chip, lax.rem(group + groups - 2, groups), 1 + width,
             held_r, stage_l, l_send, l_recv, lf_send, lf_recv),
    )

    def step(s, carry):
        m = s // sub

        @pl.when((m < parts) & (s % sub == 0))
        def _():
            @pl.when(m > 0)
            def _():
                pltpu.make_async_remote_copy(
                    src_ref=packed.at[0],
                    dst_ref=own.at[core, pl.ds(m * sub, sub)],
                    send_sem=a2a_send.at[m],
                    recv_sem=a2a_recv.at[m],
                    device_id={"tensor": lax.rem(me + 1, parts)},
                    device_id_type=MESH,
                ).wait_recv()

            own_copy(m).start()
            pl.when(m == 1)(ag_start)

        for receive, _, _ in flows:
            receive(s)
        before = s - 1

        @pl.when((before >= 0) & (before // sub < parts) & (before % sub == 0))
        def _():
            own_copy(before // sub).wait_recv()

        for _, pass_on, _ in flows:
            pass_on(s)
        if parts == 4:
            pl.when(s == 10)(ag_forward)
            pl.when(s == 10)(weight_start)
            pl.when(s == 19)(weight_forward)
            pl.when(s == 23)(weight_share)
        return carry

    lax.fori_loop(0, chunks + SKEW * last + 1, step, 0)

    if parts == 4:
        weight_finish()

    def finish(k, carry):
        kv_out[k] = pick(
            choice[0],
            [own[0, k], own[1, k]]
            + [held_l[i, k] for i in range(2 * width)]
            + [held_r[i, k] for i in range(2 * width)],
        )
        return carry

    lax.fori_loop(0, chunks, finish, 0)

    def drain(k, carry):
        for _, _, end in flows:
            end(k)
        return carry

    lax.fori_loop(0, chunks, drain, 0)
    for m in range(parts):
        own_copy(m).wait_send()
    for copy in copies:
        copy.wait_send()
    ag_finish()
    if parts == 4:
        weight_end()


def gather(slots, tokens, prefix, out_w, parts, chips, width, identity):
    rows, model = tokens.shape
    shard = prefix.shape[0]
    sub = 4 if shard >= 1024 else 2
    chunks = parts * sub
    piece = (chunks, shard // sub, LANES)
    dma = pltpu.SemaphoreType.DMA
    lane = [dma((width, chunks))] * 8
    shapes = [
        jax.ShapeDtypeStruct((parts, rows, model), BF16),
        jax.ShapeDtypeStruct(piece, BF16),
    ]
    operands = [slots, tokens, prefix]
    extra = []
    if parts == 4:
        operands.append(out_w)
        shapes.append(jax.ShapeDtypeStruct((parts,) + out_w.shape, BF16))
        extra = [dma((6,))] * 2 + [dma((3,))] * 2
    segment, kv, *weight = pl.pallas_call(
        functools.partial(gather_kernel, parts, chips, width, sub),
        out_shape=shapes,
        in_specs=[SMEM] + [VMEM] * (len(operands) - 1),
        out_specs=[VMEM] * len(shapes),
        scratch_shapes=[
            pltpu.VMEM((KVH, sub, shard // sub, LANES), BF16),
            pltpu.VMEM((2,) + piece, BF16),
            pltpu.VMEM((2 * width,) + piece, BF16),
            pltpu.VMEM((2 * width,) + piece, BF16),
            pltpu.VMEM((width,) + piece, BF16),
            pltpu.VMEM((width,) + piece, BF16),
            pltpu.VMEM((parts, rows, model), BF16),
        ]
        + [dma((max(parts, 6),))] * 2
        + [dma((parts,))] * 4
        + lane
        + extra,
        compiler_params=pltpu.CompilerParams(
            collective_id=identity, has_side_effects=True, vmem_limit_bytes=52 * MIB
        ),
        name="gather",
    )(*operands)
    return [segment.reshape(parts * rows, model), kv.reshape(PLEN, LANES)] + weight


def attention_kernel(heads, x_ref, wq_ref, wk_ref, wv_ref, lengths, kv_ref,
                     out_ref, queries, keys, values, scores, begin_ref):
    rows = x_ref.shape[0]
    lane = lax.broadcasted_iota(jnp.int32, (1, LANES), 1)
    former = (lane % HD) < HD // 2
    low = lane < HD

    def rotated(tile, cos_table, sin_table):
        swapped = jnp.where(
            former, -pltpu.roll(tile, LANES - HD // 2, 1), pltpu.roll(tile, HD // 2, 1)
        )
        return tile * cos_table + swapped * sin_table

    index = lax.broadcasted_iota(jnp.int32, (rows, LANES), 0)
    begins = jnp.zeros((rows, LANES), jnp.int32)
    start = jnp.int32(0)
    for r in range(lengths.shape[1]):
        begins = jnp.where(index >= start, start, begins)
        start = start + lengths[0, r]
    begin_ref[...] = begins
    steps_float = (lane % (HD // 2)).astype(F32)
    inverse = jnp.exp(steps_float * (-2.0 * math.log(10000.0) / HD))
    angles = (PLEN + index - begins).astype(F32) * inverse
    cos_table, sin_table = jnp.cos(angles), jnp.sin(angles)

    x = x_ref[...]
    mapped = jnp.dot(x, wq_ref[...], preferred_element_type=F32)
    for h in range(heads):
        if h % 2 == 0:
            tile = mapped[:, (h // 2) * LANES : (h // 2 + 1) * LANES]
            tile = rotated(tile, cos_table, sin_table).astype(BF16).astype(F32) * 0.125
            head = tile
        else:
            head = pltpu.roll(tile, HD, 1)
        queries[h] = jnp.where(low, head, 0.0).astype(BF16)
    is_odd = (lax.axis_index("tensor") * heads // (QH // KVH)) % 2 == 1
    new_k = jnp.dot(x, wk_ref[...], preferred_element_type=F32)
    new_v = jnp.dot(x, wv_ref[...], preferred_element_type=F32)
    new_k = rotated(new_k, cos_table, sin_table)
    new_k = jnp.where(is_odd, pltpu.roll(new_k, HD, 1), new_k)
    new_v = jnp.where(is_odd, new_v, pltpu.roll(new_v, HD, 1))
    pair = jnp.where(low, new_k, new_v)
    keys[0:PLEN, :] = kv_ref[...]
    keys[PLEN:, :] = pair.astype(BF16)
    values[...] = jnp.where(low, 1.0, keys[...].astype(F32)).astype(BF16)

    block = 256 if rows % 256 == 0 else rows
    step = 512
    total = PLEN + rows
    per_head = rows // block
    pairs = (heads + 1) // 2

    def one_head(h, start, slot):
        query = queries[h, pl.ds(start, block), :]
        top = jnp.full((block, LANES), NEG_FILL, F32)
        for n in range(total // step):
            part = lax.dot_general(
                query, keys[n * step : (n + 1) * step, :], (((1,), (1,)), ((), ())),
                preferred_element_type=F32,
            )
            if n * step >= PLEN:
                place = lax.broadcasted_iota(jnp.int32, (block, step), 1) + (n * step - PLEN)
                row = lax.broadcasted_iota(jnp.int32, (block, step), 0) + start
                seen = (place >= begin_ref[pl.ds(start, block), 0:1]) & (place <= row)
                part = jnp.where(seen, part, NEG_FILL)
            scores[slot, :, n * step : (n + 1) * step] = part
            for q in range(step // LANES):
                top = jnp.maximum(top, part[:, q * LANES : (q + 1) * LANES])
        top = jnp.max(top, axis=1, keepdims=True)
        blended = jnp.zeros((block, LANES), F32)
        for n in range(total // step):
            weight = jnp.exp(scores[slot, :, n * step : (n + 1) * step] - top).astype(BF16)
            blended += jnp.dot(
                weight, values[n * step : (n + 1) * step, :], preferred_element_type=F32
            )
        return blended

    def one(i, carry):
        p, b = i // per_head, i % per_head
        start = pl.multiple_of(b * block, block)
        even = one_head(2 * p, start, 0)
        even = pltpu.roll(even, HD, 1) / even
        if heads > 1:
            odd = one_head(2 * p + 1, start, 1)
            odd = odd / pltpu.roll(odd, HD, 1)
        else:
            odd = jnp.zeros_like(even)
        at = pl.ds(pl.multiple_of(p * LANES, LANES), LANES)
        out_ref[pl.ds(start, block), at] = jnp.where(low, even, odd).astype(BF16)
        return carry

    lax.fori_loop(0, pairs * per_head, one, 0)


def attention(x, wq, key_weight, value_weight, lengths, kv, heads, tile):
    rows = x.shape[0]
    total = PLEN + rows
    block = 256 if rows % 256 == 0 else rows
    columns = pl.BlockSpec((wq.shape[0], LANES), lambda i: (0, tile()))
    whole = lambda shape: pl.BlockSpec(shape, lambda i: (0,) * len(shape))
    width = (heads + 1) // 2 * LANES
    return pl.pallas_call(
        functools.partial(attention_kernel, heads),
        grid=(1,),
        out_shape=jax.ShapeDtypeStruct((rows, width), BF16),
        in_specs=[whole(x.shape), whole(wq.shape), columns, columns, SMEM, whole(kv.shape)],
        out_specs=whole((rows, width)),
        scratch_shapes=[
            pltpu.VMEM((heads, rows, LANES), BF16),
            pltpu.VMEM((total, LANES), BF16),
            pltpu.VMEM((total, LANES), BF16),
            pltpu.VMEM((2, block, total), F32),
            pltpu.VMEM((rows, LANES), jnp.int32),
        ],
        compiler_params=pltpu.CompilerParams(vmem_limit_bytes=52 * MIB),
        name="attention",
    )(x, wq, key_weight, value_weight, lengths, kv)


def mlp_kernel(
    parts, att, out_w, tokens, gate_up, down, result,
    gu_v, dn_v, a_send, a_recv, rows_v, f_send, f_recv, hidden,
    w_sem, as_sem, ar_sem, gs_sem, gr_sem, fs_sem, fr_sem,
):
    me = lax.axis_index("tensor")
    rows = tokens.shape[0]
    model = tokens.shape[1]
    units = hidden.shape[1]
    loads = [
        pltpu.make_async_copy(gate_up, gu_v, w_sem.at[0]),
        pltpu.make_async_copy(down, dn_v, w_sem.at[1]),
    ]
    for load in loads:
        load.start()
    barrier = pltpu.get_barrier_semaphore()
    for d in range(1, parts):
        pl.semaphore_signal(
            barrier, inc=1, device_id={"tensor": lax.rem(me + d, parts)}, device_id_type=MESH
        )

    def send(src, dst, send_sem, recv_sem, to):
        return pltpu.make_async_remote_copy(
            src_ref=src, dst_ref=dst, send_sem=send_sem, recv_sem=recv_sem,
            device_id={"tensor": to}, device_id_type=MESH,
        )

    def partial_out(owner):
        start = pl.multiple_of(owner * rows, rows)
        return jnp.dot(
            att[pl.ds(start, rows), :], out_w[...], preferred_element_type=F32
        ).astype(BF16)

    copies = []
    for d in range(1, parts):
        to = lax.rem(me + d, parts)
        a_send[d] = partial_out(to)
        if d == 1:
            pl.semaphore_wait(barrier, parts - 1)
        copy = send(a_send.at[d], a_recv.at[d], as_sem.at[d], ar_sem.at[d], to)
        copy.start()
        copies.append(copy)
    total = partial_out(me).astype(F32)
    for d in range(1, parts):
        copies[d - 1].wait_recv()
        total += a_recv[d].astype(F32)
    middle = (tokens[...].astype(F32) + total).astype(BF16)
    a_send[0] = middle
    rows_v[0] = norm_rows(middle)
    sends = []
    for d in range(1, parts):
        copy = send(
            rows_v.at[0], rows_v.at[d], gs_sem.at[d], gr_sem.at[d], lax.rem(me + d, parts)
        )
        copy.start()
        sends.append(copy)
    for load in loads:
        load.wait()

    tile = 256 if units % 256 == 0 else units
    out_tile = 512
    backs = []
    for d in range(parts):
        if d > 0:
            sends[d - 1].wait_recv()

        def up(i, carry, d=d):
            if tile == units:
                at = slice(None)
            else:
                at = pl.ds(pl.multiple_of(i * tile, tile), tile)
            x = rows_v[d]
            gate = jnp.dot(x, gu_v[0, :, at], preferred_element_type=F32)
            raised = jnp.dot(x, gu_v[1, :, at], preferred_element_type=F32)
            hidden[:, at] = (gate / (1.0 + jnp.exp(-gate)) * raised).astype(BF16)
            return carry

        lax.fori_loop(0, units // tile, up, 0)

        def lower(i, carry, d=d):
            at = pl.ds(pl.multiple_of(i * out_tile, out_tile), out_tile)
            f_send[d, :, at] = jnp.dot(
                hidden[...], dn_v[:, at], preferred_element_type=F32
            ).astype(BF16)
            return carry

        lax.fori_loop(0, model // out_tile, lower, 0)
        if d > 0:
            owner = lax.rem(me + parts - d, parts)
            copy = send(f_send.at[d], f_recv.at[d], fs_sem.at[d], fr_sem.at[d], owner)
            copy.start()
            backs.append(copy)
    total = f_send[0].astype(F32)
    for d in range(1, parts):
        backs[d - 1].wait_recv()
        total += f_recv[d].astype(F32)
    result[...] = (a_send[0].astype(F32) + total).astype(BF16)
    for copy in copies + sends + backs:
        copy.wait_send()


def mlp_square_kernel(
    att, out_w, tokens, gate_up, down, result,
    gu_v, dn_v, att_v, mid_v, rows_v, f_v, f_in, hidden,
    w_sem, as_sem, ar_sem, gs_sem, gr_sem, fs_sem, fr_sem,
):
    parts = 4
    me = lax.axis_index("tensor")
    near_x, near_y, far = me + 1 - 2 * (me % 2), lax.rem(me + 2, parts), parts - 1 - me
    rows, model = tokens.shape
    half_rows = rows // 2
    units = hidden.shape[1]
    loads = [
        pltpu.make_async_copy(gate_up, gu_v, w_sem.at[0]),
        pltpu.make_async_copy(down, dn_v, w_sem.at[1]),
    ]
    for load in loads:
        load.start()
    barrier = pltpu.get_barrier_semaphore()
    for to in (near_x, near_y, far):
        pl.semaphore_signal(barrier, inc=1, device_id={"tensor": to}, device_id_type=MESH)
    pl.semaphore_wait(barrier, parts - 1)

    def send(src, dst, send_sem, recv_sem, to):
        return pltpu.make_async_remote_copy(
            src_ref=src, dst_ref=dst, send_sem=send_sem, recv_sem=recv_sem,
            device_id={"tensor": to}, device_id_type=MESH,
        )

    def cut(half):
        return pl.ds(half * half_rows, half_rows)

    def block_of(owner):
        return att.at[pl.ds(pl.multiple_of(owner * rows, rows), rows)]

    swaps = [
        send(block_of(to), att_v.at[slot], as_sem.at[slot], ar_sem.at[slot], to)
        for slot, to in ((3, far), (1, near_x), (2, near_y))
    ]
    for copy in swaps:
        copy.start()

    def group_term(block, slot):
        term = jnp.dot(block, out_w[slot], preferred_element_type=F32)
        return term.astype(BF16).astype(F32)

    total = group_term(att[pl.ds(pl.multiple_of(me * rows, rows), rows), :], 0)
    for copy, slot in zip(swaps[1:] + swaps[:1], (1, 2, 3)):
        copy.wait_recv()
        total += group_term(att_v[slot], slot)
    middle = (tokens[...].astype(F32) + total).astype(BF16)
    mid_v[...] = middle
    rows_v[0] = norm_rows(middle)

    def piece(src, place, half, to):
        at = 2 * place + half - 2
        return send(
            rows_v.at[src, cut(half)], rows_v.at[place, cut(half)],
            gs_sem.at[at], gr_sem.at[at], to,
        )

    piece(0, 1, 0, near_x).start()
    piece(0, 2, 1, near_y).start()
    piece(0, 1, 1, near_x).start()
    piece(0, 2, 0, near_y).start()
    for load in loads:
        load.wait()

    tile = 256 if units % 256 == 0 else units
    out_tile = 512

    def feed(first, count):
        many = count * rows

        def up(i, carry):
            at = pl.ds(pl.multiple_of(i * tile, tile), tile)
            x = rows_v[first : first + count].reshape(many, model)
            gate = jnp.dot(x, gu_v[0, :, at], preferred_element_type=F32)
            raised = jnp.dot(x, gu_v[1, :, at], preferred_element_type=F32)
            hidden[0:many, at] = (gate / (1.0 + jnp.exp(-gate)) * raised).astype(BF16)
            return carry

        lax.fori_loop(0, units // tile, up, 0)

        def lower(i, carry):
            at = pl.ds(pl.multiple_of(i * out_tile, out_tile), out_tile)
            f_v[first : first + count, :, at] = (
                jnp.dot(hidden[0:many, :], dn_v[:, at], preferred_element_type=F32)
                .astype(BF16)
                .reshape(count, rows, out_tile)
            )
            return carry

        lax.fori_loop(0, model // out_tile, lower, 0)

    def back(slot, half, place, to):
        at = 2 * place + half
        return send(
            f_v.at[slot, cut(half)], f_in.at[place, cut(half)], fs_sem.at[at], fr_sem.at[at], to
        )

    feed(0, 1)
    piece(0, 1, 0, near_x).wait_recv()
    piece(1, 3, 0, near_y).start()
    piece(0, 2, 1, near_y).wait_recv()
    piece(2, 3, 1, near_x).start()
    piece(0, 1, 1, near_x).wait_recv()
    piece(0, 2, 0, near_y).wait_recv()
    feed(1, 2)
    back(1, 0, 0, near_x).start()
    back(2, 1, 1, near_y).start()
    piece(1, 3, 0, near_y).wait_recv()
    piece(2, 3, 1, near_x).wait_recv()
    feed(3, 1)
    back(3, 0, 2, near_x).start()
    back(3, 1, 2, near_y).start()
    for half, slot, place, to in ((0, 2, 1, near_y), (1, 1, 0, near_x)):
        back(3, half, 2, to).wait_recv()
        f_v[slot, cut(half)] = (
            f_v[slot, cut(half)].astype(F32) + f_in[2, cut(half)].astype(F32)
        ).astype(BF16)
        back(slot, half, place, to).start()
    order = ((1, 0, 0, near_x), (2, 1, 1, near_y), (2, 0, 1, near_y), (1, 1, 0, near_x))
    for slot, half, place, to in order:
        back(slot, half, place, to).wait_recv()
    total = f_v[0].astype(F32) + f_in[0].astype(F32) + f_in[1].astype(F32)
    result[...] = (mid_v[...].astype(F32) + total).astype(BF16)
    for copy in swaps:
        copy.wait_send()
    for place in (1, 2, 3):
        for half in range(2):
            piece(0, place, half, near_x).wait_send()
            back(1, half, place - 1, near_x).wait_send()


def mlp_square(att, out_w, tokens, gate_up, down, identity):
    rows, model = tokens.shape
    parts = 4
    dma = pltpu.SemaphoreType.DMA
    full = pltpu.VMEM((parts, rows, model), BF16)
    return pl.pallas_call(
        mlp_square_kernel,
        out_shape=jax.ShapeDtypeStruct((rows, model), BF16),
        in_specs=[VMEM, VMEM, VMEM, ANY, ANY],
        out_specs=VMEM,
        scratch_shapes=[
            pltpu.VMEM(gate_up.shape, BF16),
            pltpu.VMEM(down.shape, BF16),
            pltpu.VMEM((parts, rows, att.shape[1]), BF16),
            pltpu.VMEM((rows, model), BF16),
            full, full,
            pltpu.VMEM((3, rows, model), BF16),
            pltpu.VMEM((2 * rows, down.shape[0]), BF16),
            dma((2,)), dma((parts,)), dma((parts,)),
        ]
        + [dma((6,))] * 4,
        compiler_params=pltpu.CompilerParams(
            collective_id=identity, has_side_effects=True, vmem_limit_bytes=52 * MIB
        ),
        name="mlp",
    )(att, out_w, tokens, gate_up, down)


def mlp(att, out_w, tokens, gate_up, down, parts, identity):
    rows, model = tokens.shape
    dma = pltpu.SemaphoreType.DMA
    full = pltpu.VMEM((parts, rows, model), BF16)
    return pl.pallas_call(
        functools.partial(mlp_kernel, parts),
        out_shape=jax.ShapeDtypeStruct((rows, model), BF16),
        in_specs=[VMEM, VMEM, VMEM, ANY, ANY],
        out_specs=VMEM,
        scratch_shapes=[
            pltpu.VMEM(gate_up.shape, BF16),
            pltpu.VMEM(down.shape, BF16),
            full, full, full, full, full,
            pltpu.VMEM((rows, down.shape[0]), BF16),
            dma((2,)),
        ]
        + [dma((parts,))] * 6,
        compiler_params=pltpu.CompilerParams(
            collective_id=identity, has_side_effects=True, vmem_limit_bytes=52 * MIB
        ),
        name="mlp",
    )(att, out_w, tokens, gate_up, down)


def on_device(
    tokens,
    lengths,
    group_prefix,
    prefix_cache,
    query_weight,
    key_weight,
    value_weight,
    out_weight,
    gate_up_weight,
    down_weight,
):
    parts = lax.axis_size("tensor")
    chips = lax.axis_size("dp") // 2
    heads = query_weight.shape[1] // HD

    most = most_crossing(group_prefix, chips)

    def routed(width, identity):
        def run(prefix, rows_in):
            return gather(
                group_prefix, rows_in, prefix, out_weight, parts, chips, width, identity
            )
        return run

    segment, kv, *gathered = lax.cond(
        most <= 2, routed(1, 0), routed(chips // 2, 1), prefix_cache, tokens
    )

    wq = query_weight
    if heads % 2:
        wq = jnp.pad(wq, ((0, 0), (0, HD)))

    def tile():
        return lax.axis_index("tensor") * heads // (QH // KVH) // 2

    att = attention(segment, wq, key_weight, value_weight, lengths, kv, heads, tile)
    if parts == 4:
        return mlp_square(att, gathered[0], tokens, gate_up_weight, down_weight, 2)
    out_w = out_weight
    if heads % 2:
        out_w = jnp.pad(out_w, ((0, HD), (0, 0)))
    return mlp(att, out_w, tokens, gate_up_weight, down_weight, parts, 2)


def solution(mesh):
    return jax.shard_map(
        on_device,
        mesh=mesh,
        in_specs=(
            P(("dp", "tensor"), None),
            P("dp", None),
            P(),
            P(("dp", "tensor"), None),
            P(None, "tensor"),
            P(),
            P(),
            P("tensor", None),
            P(None, None, "tensor"),
            P("tensor", None),
        ),
        out_specs=P(("dp", "tensor"), None),
        check_vma=False,
    )
```

```python
import functools
import math

import jax
import jax.numpy as jnp
from jax import lax
from jax.experimental import pallas as pl
from jax.experimental.pallas import tpu as pltpu
from jax.sharding import PartitionSpec as P

QH = 16
KVH = 4
HD = 64
PLEN = 4096
LANES = 128
SKEW = 3
NEG_FILL = -1e30
VMEM = pl.BlockSpec(memory_space=pltpu.VMEM)
SMEM = pl.BlockSpec(memory_space=pltpu.SMEM)
ANY = pl.BlockSpec(memory_space=pl.ANY)
MESH = pl.DeviceIdType.MESH
BF16 = jnp.bfloat16
F32 = jnp.float32
MIB = 1 << 20


def norm_rows(inputs):
    floats = inputs.astype(F32)
    mean = jnp.mean(floats * floats, axis=-1, keepdims=True)
    return (floats * lax.rsqrt(mean + 1e-05)).astype(BF16)


def most_crossing(group_prefix, chips):
    slots = jnp.arange(2 * chips, dtype=jnp.int32)
    wanted = group_prefix[None, :] == slots[:, None]
    final = jnp.max(jnp.where(wanted, slots[None, :], -1), axis=1)
    first = jnp.min(jnp.where(wanted, slots[None, :], 2 * chips), axis=1)
    edge = 2 * jnp.arange(1, chips, dtype=jnp.int32)[:, None]
    right = (slots[None, :] < edge) & (final[None, :] >= edge)
    left = (slots[None, :] >= edge) & (first[None, :] < edge)
    counts = jnp.sum(jnp.stack([right, left]).astype(jnp.int32), axis=2)
    return jnp.max(counts)


def route_choice(slot_ref, group, chips, width):
    number = 2 * chips
    chip, core = group // 2, group % 2
    held = [slot_ref[g] for g in range(number)]
    final, first = [], []
    for s in range(number):
        top, low = jnp.int32(-1), jnp.int32(number)
        for g in range(number):
            top = jnp.where(held[g] == s, g, top)
        for g in reversed(range(number)):
            low = jnp.where(held[g] == s, g, low)
        final.append(top)
        first.append(low)

    def ranks(needs):
        result, count = [], jnp.int32(0)
        for need in needs:
            result.append(count)
            count = count + need.astype(jnp.int32)
        return result

    def right(z):
        return [(s // 2 <= z) & (final[s] >= 2 * (z + 1)) for s in range(number)]

    def left(z):
        return [(s // 2 >= z) & (first[s] < 2 * z) for s in range(number)]

    from_left, from_right = ranks(right(chip - 1)), ranks(left(chip + 1))
    mine = slot_ref[group]
    keep = jnp.int32(0)
    sides = []
    for s in range(number):
        own = chip == s // 2
        value = jnp.where(
            own, s % 2, jnp.where(chip > s // 2, 2 + from_left[s], 2 + 2 * width + from_right[s])
        )
        keep = jnp.where(mine == s, value, keep)
    for needs, source in ((right(chip), from_left), (left(chip), from_right)):
        rank = ranks(needs)
        chosen = []
        for w in range(width):
            place = 2 * w + core
            value = jnp.int32(0)
            for s in range(number):
                value = jnp.where(
                    needs[s] & (rank[s] == place),
                    jnp.where(chip == s // 2, s % 2, 2 + source[s]),
                    value,
                )
            chosen.append(value)
        sides.append(chosen)
    return [keep] + sides[0] + sides[1]


def pick(number, candidates):
    result = candidates[0]
    for i in range(1, len(candidates)):
        result = jnp.where(number == i, candidates[i], result)
    return result


def gather_kernel(parts, chips, width, sub, *refs):
    if parts == 4:
        ow, ow_all, w_send, w_recv, share_send, share_recv = refs[3], refs[6], *refs[-4:]
        refs = refs[:3] + refs[4:6] + refs[7:-4]
    (
    slot_ref, tokens, prefix, segment, kv_out,
    packed, own, held_l, held_r, stage_r, stage_l, ag,
    ag_send, ag_recv, a2a_send, a2a_recv, own_send, own_recv,
    r_send, r_recv, l_send, l_recv, rf_send, rf_recv, lf_send, lf_recv,
    ) = refs
    me = lax.axis_index("tensor")
    group = lax.axis_index("dp")
    chip, core = group // 2, group % 2
    other = 1 - core
    sibling = chip * 2 + other
    groups = 2 * chips
    chunks = parts * sub
    chunk_rows = prefix.shape[0] // sub

    for ref in (held_l, held_r):
        ref[...] = jnp.zeros_like(ref)
    barrier = pltpu.get_barrier_semaphore()
    for d in range(1, parts):
        pl.semaphore_signal(
            barrier, inc=1, device_id={"tensor": lax.rem(me + d, parts)}, device_id_type=MESH
        )
    near = (sibling, lax.rem(group + 2, groups), lax.rem(group + groups - 2, groups))
    for to in near:
        pl.semaphore_signal(barrier, inc=1, device_id={"dp": to}, device_id_type=MESH)

    choice = route_choice(slot_ref, group, chips, width)
    rows_i = lax.broadcasted_iota(jnp.int32, (2 * KVH * HD, LANES), 0)
    cols_i = lax.broadcasted_iota(jnp.int32, (2 * KVH * HD, LANES), 1)
    source = cols_i + jnp.where(cols_i >= HD, KVH * HD - HD, 0)
    for h in range(KVH):
        take = (rows_i == source + h * HD).astype(F32).astype(BF16)
        packed[h] = (
            jnp.dot(prefix[...], take, preferred_element_type=F32)
            .astype(BF16)
            .reshape(sub, chunk_rows, LANES)
        )
    pl.semaphore_wait(barrier, parts - 1 + 3)

    copies = []
    for d in range(parts - 1, 0, -1):
        to = lax.rem(me + d, parts)
        copy = pltpu.make_async_remote_copy(
            src_ref=packed.at[to * KVH // parts],
            dst_ref=own.at[core, pl.ds((parts - d) * sub, sub)],
            send_sem=a2a_send.at[parts - d],
            recv_sem=a2a_recv.at[parts - d],
            device_id={"tensor": to},
            device_id_type=MESH,
        )
        copy.start()
        copies.append(copy)
    own[core, 0:sub] = packed[me * KVH // parts]

    ag[0] = norm_rows(tokens[...])
    def ag_copy(d):
        return pltpu.make_async_remote_copy(
            src_ref=ag.at[0],
            dst_ref=ag.at[d],
            send_sem=ag_send.at[d],
            recv_sem=ag_recv.at[d],
            device_id={"tensor": lax.rem(me + d, parts)},
            device_id_type=MESH,
        )

    def half_copy(slot, place, half, to):
        rows = tokens.shape[0] // 2
        at = pl.ds(half * rows, rows)
        return pltpu.make_async_remote_copy(
            src_ref=ag.at[slot, at],
            dst_ref=ag.at[place, at],
            send_sem=ag_send.at[2 * place + half - 2],
            recv_sem=ag_recv.at[2 * place + half - 2],
            device_id={"tensor": to},
            device_id_type=MESH,
        )

    near_x, near_y = me + 1 - 2 * (me % 2), lax.rem(me + 2, parts)

    def ag_start():
        if parts == 4:
            half_copy(0, 1, 0, near_x).start()
            half_copy(0, 2, 1, near_y).start()
            half_copy(0, 1, 1, near_x).start()
            half_copy(0, 2, 0, near_y).start()
        else:
            for d in range(1, parts):
                ag_copy(d).start()

    def ag_forward():
        if parts == 4:
            half_copy(0, 1, 0, near_x).wait_recv()
            half_copy(1, 3, 0, near_y).start()
            half_copy(0, 2, 1, near_y).wait_recv()
            half_copy(2, 3, 1, near_x).start()

    def ag_finish():
        segment[pl.ds(me, 1)] = ag[0:1]
        if parts == 4:
            half_copy(0, 1, 1, near_x).wait_recv()
            segment[pl.ds(near_x, 1)] = ag[1:2]
            half_copy(0, 2, 0, near_y).wait_recv()
            segment[pl.ds(near_y, 1)] = ag[2:3]
            half_copy(1, 3, 0, near_y).wait_recv()
            half_copy(2, 3, 1, near_x).wait_recv()
            segment[pl.ds(parts - 1 - me, 1)] = ag[3:4]
            for place, half in ((1, 0), (1, 1), (2, 0), (2, 1), (3, 0), (3, 1)):
                half_copy(0, place, half, near_x).wait_send()
        else:
            for d in range(1, parts):
                ag_copy(d).wait_recv()
                segment[pl.ds(lax.rem(me + parts - d, parts), 1)] = ag[d : d + 1]
            for d in range(1, parts):
                ag_copy(d).wait_send()

    def weight_piece(src, place, half, to):
        quarter, moved = ow.shape[0] // 4, ow_all.shape[2]
        at = pl.ds((2 * core + half) * quarter, quarter)
        return pltpu.make_async_remote_copy(
            src_ref=ow.at[at, 0:moved] if src == 0 else ow_all.at[src, at],
            dst_ref=ow_all.at[place, at],
            send_sem=w_send.at[2 * place + half - 2],
            recv_sem=w_recv.at[2 * place + half - 2],
            device_id={"tensor": to},
            device_id_type=MESH,
        )

    def share(place):
        quarter = ow.shape[0] // 4
        ref = ow_all.at[place, pl.ds(2 * core * quarter, 2 * quarter)]
        return pltpu.make_async_remote_copy(
            src_ref=ref, dst_ref=ref, send_sem=share_send.at[place - 1],
            recv_sem=share_recv.at[place - 1], device_id={"dp": sibling}, device_id_type=MESH,
        )

    def weight_start():
        weight_piece(0, 1, 0, near_x).start()
        weight_piece(0, 2, 1, near_y).start()
        weight_piece(0, 1, 1, near_x).start()
        weight_piece(0, 2, 0, near_y).start()
        ow_all[0] = ow[:, 0 : ow_all.shape[2]]

    def weight_forward():
        weight_piece(0, 1, 0, near_x).wait_recv()
        weight_piece(1, 3, 0, near_y).start()
        weight_piece(0, 2, 1, near_y).wait_recv()
        weight_piece(2, 3, 1, near_x).start()

    def weight_share():
        weight_piece(0, 1, 1, near_x).wait_recv()
        share(1).start()
        weight_piece(0, 2, 0, near_y).wait_recv()
        share(2).start()

    def weight_finish():
        weight_piece(1, 3, 0, near_y).wait_recv()
        weight_piece(2, 3, 1, near_x).wait_recv()
        share(3).start()

    def weight_end():
        for place in (1, 2, 3):
            share(place).wait_recv()
        for place in (1, 2, 3):
            share(place).wait_send()
            for half in range(2):
                weight_piece(0, place, half, near_x).wait_send()

    def lane_copy(src, dst, send_sem, recv_sem, to):
        return pltpu.make_async_remote_copy(
            src_ref=src, dst_ref=dst, send_sem=send_sem, recv_sem=recv_sem,
            device_id={"dp": to}, device_id_type=MESH,
        )

    def own_copy(m):
        block = own.at[core, pl.ds(m * sub, sub)]
        return lane_copy(block, block, own_send.at[m], own_recv.at[m], sibling)

    last = chips - 1

    def flow(place, to, base, held, stage, send, recv, f_send, f_recv):
        def hop(w, k):
            return lane_copy(
                stage.at[w, k], held.at[w * 2 + core, k], send.at[w, k], recv.at[w, k], to
            )

        def forward(w, k):
            ref = held.at[w * 2 + core, k]
            return lane_copy(ref, ref, f_send.at[w, k], f_recv.at[w, k], sibling)

        def comes(w):
            return (place > w) & (place <= last - w)

        def goes(w):
            return (place >= w) & (place < last - w)

        def receive(s):
            k = s - SKEW * place
            for w in range(width):
                @pl.when((k >= 0) & (k < chunks) & comes(w))
                def _(w=w):
                    hop(w, k).wait_recv()
                    forward(w, k).start()

        def pass_on(s):
            k = s - 1 - SKEW * place
            for w in range(width):
                @pl.when((k >= 0) & (k < chunks) & comes(w))
                def _(w=w):
                    forward(w, k).wait_recv()
            for w in range(width):
                @pl.when((k >= 0) & (k < chunks) & goes(w))
                def _(w=w):
                    stage[w, k] = pick(
                        choice[base + w],
                        [own[0, k], own[1, k]] + [held[i, k] for i in range(2 * width)],
                    )
                    hop(w, k).start()

        def drain(k):
            for w in range(width):
                @pl.when(goes(w))
                def _(w=w):
                    hop(w, k).wait_send()
                @pl.when(comes(w))
                def _(w=w):
                    forward(w, k).wait_send()

        return receive, pass_on, drain

    flows = (
        flow(chip, lax.rem(group + 2, groups), 1,
             held_l, stage_r, r_send, r_recv, rf_send, rf_recv),
        flow(last - chip, lax.rem(group + groups - 2, groups), 1 + width,
             held_r, stage_l, l_send, l_recv, lf_send, lf_recv),
    )

    def step(s, carry):
        m = s // sub

        @pl.when((m < parts) & (s % sub == 0))
        def _():
            @pl.when(m > 0)
            def _():
                pltpu.make_async_remote_copy(
                    src_ref=packed.at[0],
                    dst_ref=own.at[core, pl.ds(m * sub, sub)],
                    send_sem=a2a_send.at[m],
                    recv_sem=a2a_recv.at[m],
                    device_id={"tensor": lax.rem(me + 1, parts)},
                    device_id_type=MESH,
                ).wait_recv()

            own_copy(m).start()
            pl.when(m == 1)(ag_start)

        for receive, _, _ in flows:
            receive(s)
        before = s - 1

        @pl.when((before >= 0) & (before // sub < parts) & (before % sub == 0))
        def _():
            own_copy(before // sub).wait_recv()

        for _, pass_on, _ in flows:
            pass_on(s)
        if parts == 4:
            pl.when(s == 10)(ag_forward)
            pl.when(s == 10)(weight_start)
            pl.when(s == 19)(weight_forward)
            pl.when(s == 23)(weight_share)
        return carry

    lax.fori_loop(0, chunks + SKEW * last + 1, step, 0)

    if parts == 4:
        weight_finish()

    def finish(k, carry):
        kv_out[k] = pick(
            choice[0],
            [own[0, k], own[1, k]]
            + [held_l[i, k] for i in range(2 * width)]
            + [held_r[i, k] for i in range(2 * width)],
        )
        return carry

    lax.fori_loop(0, chunks, finish, 0)

    def drain(k, carry):
        for _, _, end in flows:
            end(k)
        return carry

    lax.fori_loop(0, chunks, drain, 0)
    for m in range(parts):
        own_copy(m).wait_send()
    for copy in copies:
        copy.wait_send()
    ag_finish()
    if parts == 4:
        weight_end()


def gather(slots, tokens, prefix, out_w, parts, chips, width, identity):
    rows, model = tokens.shape
    shard = prefix.shape[0]
    sub = 4 if shard >= 1024 else 2
    chunks = parts * sub
    piece = (chunks, shard // sub, LANES)
    dma = pltpu.SemaphoreType.DMA
    lane = [dma((width, chunks))] * 8
    shapes = [
        jax.ShapeDtypeStruct((parts, rows, model), BF16),
        jax.ShapeDtypeStruct(piece, BF16),
    ]
    operands = [slots, tokens, prefix]
    extra = []
    if parts == 4:
        operands.append(out_w)
        shapes.append(jax.ShapeDtypeStruct((parts, out_w.shape[0], model // 2), BF16))
        extra = [dma((6,))] * 2 + [dma((3,))] * 2
    segment, kv, *weight = pl.pallas_call(
        functools.partial(gather_kernel, parts, chips, width, sub),
        out_shape=shapes,
        in_specs=[SMEM] + [VMEM] * (len(operands) - 1),
        out_specs=[VMEM] * len(shapes),
        scratch_shapes=[
            pltpu.VMEM((KVH, sub, shard // sub, LANES), BF16),
            pltpu.VMEM((2,) + piece, BF16),
            pltpu.VMEM((2 * width,) + piece, BF16),
            pltpu.VMEM((2 * width,) + piece, BF16),
            pltpu.VMEM((width,) + piece, BF16),
            pltpu.VMEM((width,) + piece, BF16),
            pltpu.VMEM((parts, rows, model), BF16),
        ]
        + [dma((max(parts, 6),))] * 2
        + [dma((parts,))] * 4
        + lane
        + extra,
        compiler_params=pltpu.CompilerParams(
            collective_id=identity, has_side_effects=True, vmem_limit_bytes=52 * MIB
        ),
        name="gather",
    )(*operands)
    return [segment.reshape(parts * rows, model), kv.reshape(PLEN, LANES)] + weight


def table_kernel(lengths, cos_ref, sin_ref, begin_ref):
    rows = begin_ref.shape[0]
    lane = lax.broadcasted_iota(jnp.int32, (1, LANES), 1)
    index = lax.broadcasted_iota(jnp.int32, (rows, LANES), 0)
    begins = jnp.zeros((rows, LANES), jnp.int32)
    start = jnp.int32(0)
    for r in range(lengths.shape[1]):
        begins = jnp.where(index >= start, start, begins)
        start = start + lengths[0, r]
    begin_ref[...] = begins
    steps_float = (lane % (HD // 2)).astype(F32)
    inverse = jnp.exp(steps_float * (-2.0 * math.log(10000.0) / HD))
    angles = (PLEN + index - begins).astype(F32) * inverse
    cos_ref[...] = jnp.cos(angles)
    sin_ref[...] = jnp.sin(angles)


def attention_kernel(heads, parts, *refs):
    (x_ref, wq_ref, wk_ref, wv_ref, cos_ref, sin_ref, begin_ref, kv_ref) = refs[:8]
    if parts == 4:
        ow, out_ref, ow_all, queries, keys, values, scores, w_send, w_recv, s_send, s_recv = refs[8:]
        me = lax.axis_index("tensor")
        group = lax.axis_index("dp")
        core = group % 2
        sibling = group + 1 - 2 * core
        near_x, near_y = me + 1 - 2 * (me % 2), lax.rem(me + 2, parts)
        quarter, moved = ow.shape[0] // 4, ow_all.shape[2]

        def piece(src, place, half, to):
            at = pl.ds((2 * core + half) * quarter, quarter)
            return pltpu.make_async_remote_copy(
                src_ref=ow.at[at, pl.ds(moved, moved)] if src == 0 else ow_all.at[src, at],
                dst_ref=ow_all.at[place, at],
                send_sem=w_send.at[2 * place + half - 2],
                recv_sem=w_recv.at[2 * place + half - 2],
                device_id={"tensor": to},
                device_id_type=MESH,
            )

        def share(place):
            ref = ow_all.at[place, pl.ds(2 * core * quarter, 2 * quarter)]
            return pltpu.make_async_remote_copy(
                src_ref=ref, dst_ref=ref, send_sem=s_send.at[place - 1],
                recv_sem=s_recv.at[place - 1], device_id={"dp": sibling}, device_id_type=MESH,
            )

        barrier = pltpu.get_barrier_semaphore()
        for to in ({"tensor": near_x}, {"tensor": near_y}, {"dp": sibling}):
            pl.semaphore_signal(barrier, inc=1, device_id=to, device_id_type=MESH)
        pl.semaphore_wait(barrier, 3)
        piece(0, 1, 0, near_x).start()
        piece(0, 2, 1, near_y).start()
        piece(0, 1, 1, near_x).start()
        piece(0, 2, 0, near_y).start()
        ow_all[0] = ow[:, moved:]
    else:
        out_ref, queries, keys, values, scores = refs[8:]
    rows = x_ref.shape[0]
    lane = lax.broadcasted_iota(jnp.int32, (1, LANES), 1)
    former = (lane % HD) < HD // 2
    low = lane < HD

    def rotated(tile, cos_table, sin_table):
        swapped = jnp.where(
            former, -pltpu.roll(tile, LANES - HD // 2, 1), pltpu.roll(tile, HD // 2, 1)
        )
        return tile * cos_table + swapped * sin_table

    cos_table, sin_table = cos_ref[...], sin_ref[...]
    x = x_ref[...]
    mapped = jnp.dot(x, wq_ref[...], preferred_element_type=F32)
    for h in range(heads):
        if h % 2 == 0:
            tile = mapped[:, (h // 2) * LANES : (h // 2 + 1) * LANES]
            tile = rotated(tile, cos_table, sin_table).astype(BF16).astype(F32) * 0.125
            head = tile
        else:
            head = pltpu.roll(tile, HD, 1)
        queries[h] = jnp.where(low, head, 0.0).astype(BF16)
    is_odd = (lax.axis_index("tensor") * heads // (QH // KVH)) % 2 == 1
    new_k = jnp.dot(x, wk_ref[...], preferred_element_type=F32)
    new_v = jnp.dot(x, wv_ref[...], preferred_element_type=F32)
    new_k = rotated(new_k, cos_table, sin_table)
    new_k = jnp.where(is_odd, pltpu.roll(new_k, HD, 1), new_k)
    new_v = jnp.where(is_odd, new_v, pltpu.roll(new_v, HD, 1))
    pair = jnp.where(low, new_k, new_v)
    keys[0:PLEN, :] = kv_ref[...]
    keys[PLEN:, :] = pair.astype(BF16)
    values[...] = jnp.where(low, 1.0, keys[...].astype(F32)).astype(BF16)

    block = 256 if rows % 256 == 0 else rows
    step = 512
    total = PLEN + rows
    per_head = rows // block
    pairs = (heads + 1) // 2

    def one_head(h, start, slot):
        query = queries[h, pl.ds(start, block), :]
        top = jnp.full((block, LANES), NEG_FILL, F32)
        for n in range(total // step):
            part = lax.dot_general(
                query, keys[n * step : (n + 1) * step, :], (((1,), (1,)), ((), ())),
                preferred_element_type=F32,
            )
            if n * step >= PLEN:
                place = lax.broadcasted_iota(jnp.int32, (block, step), 1) + (n * step - PLEN)
                row = lax.broadcasted_iota(jnp.int32, (block, step), 0) + start
                seen = (place >= begin_ref[pl.ds(start, block), 0:1]) & (place <= row)
                part = jnp.where(seen, part, NEG_FILL)
            scores[slot, :, n * step : (n + 1) * step] = part
            for q in range(step // LANES):
                top = jnp.maximum(top, part[:, q * LANES : (q + 1) * LANES])
        top = jnp.max(top, axis=1, keepdims=True)
        blended = jnp.zeros((block, LANES), F32)
        for n in range(total // step):
            weight = jnp.exp(scores[slot, :, n * step : (n + 1) * step] - top).astype(BF16)
            blended += jnp.dot(
                weight, values[n * step : (n + 1) * step, :], preferred_element_type=F32
            )
        return blended

    def one(i, carry):
        if parts == 4:
            @pl.when(i == 1)
            def _():
                piece(0, 1, 0, near_x).wait_recv()
                piece(1, 3, 0, near_y).start()
                piece(0, 2, 1, near_y).wait_recv()
                piece(2, 3, 1, near_x).start()

            @pl.when(i == 2)
            def _():
                piece(0, 1, 1, near_x).wait_recv()
                share(1).start()
                piece(0, 2, 0, near_y).wait_recv()
                share(2).start()

            @pl.when(i == pairs * per_head - 1)
            def _():
                piece(1, 3, 0, near_y).wait_recv()
                piece(2, 3, 1, near_x).wait_recv()
                share(3).start()

        p, b = i // per_head, i % per_head
        start = pl.multiple_of(b * block, block)
        even = one_head(2 * p, start, 0)
        even = pltpu.roll(even, HD, 1) / even
        if heads > 1:
            odd = one_head(2 * p + 1, start, 1)
            odd = odd / pltpu.roll(odd, HD, 1)
        else:
            odd = jnp.zeros_like(even)
        at = pl.ds(pl.multiple_of(p * LANES, LANES), LANES)
        out_ref[pl.ds(start, block), at] = jnp.where(low, even, odd).astype(BF16)
        return carry

    lax.fori_loop(0, pairs * per_head, one, 0)
    if parts == 4:
        for place in (1, 2, 3):
            share(place).wait_recv()
        for place in (1, 2, 3):
            share(place).wait_send()
            for half in range(2):
                piece(0, place, half, near_x).wait_send()


def attention(x, wq, key_weight, value_weight, lengths, kv, out_w, heads, tile, parts, identity):
    rows = x.shape[0]
    total = PLEN + rows
    block = 256 if rows % 256 == 0 else rows
    table = jax.ShapeDtypeStruct((rows, LANES), F32)
    tables = pl.pallas_call(
        table_kernel,
        out_shape=[table, table, jax.ShapeDtypeStruct((rows, LANES), jnp.int32)],
        in_specs=[SMEM],
        out_specs=[VMEM] * 3,
        name="tables",
    )(lengths)
    columns = pl.BlockSpec((wq.shape[0], LANES), lambda i: (0, tile()))
    whole = lambda shape: pl.BlockSpec(shape, lambda i: (0,) * len(shape))
    shapes = [jax.ShapeDtypeStruct((rows, (heads + 1) // 2 * LANES), BF16)]
    operands = [x, wq, key_weight, value_weight, *tables, kv]
    specs = [whole(x.shape), whole(wq.shape), columns, columns]
    specs += [whole(t.shape) for t in tables] + [whole(kv.shape)]
    scratch = [
        pltpu.VMEM((heads, rows, LANES), BF16),
        pltpu.VMEM((total, LANES), BF16),
        pltpu.VMEM((total, LANES), BF16),
        pltpu.VMEM((2, block, total), F32),
    ]
    params = dict(vmem_limit_bytes=52 * MIB)
    out_specs = [whole(shapes[0].shape)]
    if parts == 4:
        operands.append(out_w)
        specs.append(VMEM)
        shapes.append(jax.ShapeDtypeStruct((parts, out_w.shape[0], out_w.shape[1] // 2), BF16))
        out_specs.append(VMEM)
        scratch += [pltpu.SemaphoreType.DMA((6,))] * 2 + [pltpu.SemaphoreType.DMA((3,))] * 2
        params.update(collective_id=identity, has_side_effects=True)
    return pl.pallas_call(
        functools.partial(attention_kernel, heads, parts),
        grid=(1,),
        out_shape=shapes,
        in_specs=specs,
        out_specs=out_specs,
        scratch_shapes=scratch,
        compiler_params=pltpu.CompilerParams(**params),
        name="attention",
    )(*operands)


def mlp_kernel(
    parts, att, out_w, tokens, gate_up, down, result,
    gu_v, dn_v, a_send, a_recv, rows_v, f_send, f_recv, hidden,
    w_sem, as_sem, ar_sem, gs_sem, gr_sem, fs_sem, fr_sem,
):
    me = lax.axis_index("tensor")
    rows = tokens.shape[0]
    model = tokens.shape[1]
    units = hidden.shape[1]
    loads = [
        pltpu.make_async_copy(gate_up, gu_v, w_sem.at[0]),
        pltpu.make_async_copy(down, dn_v, w_sem.at[1]),
    ]
    for load in loads:
        load.start()
    barrier = pltpu.get_barrier_semaphore()
    for d in range(1, parts):
        pl.semaphore_signal(
            barrier, inc=1, device_id={"tensor": lax.rem(me + d, parts)}, device_id_type=MESH
        )

    def send(src, dst, send_sem, recv_sem, to):
        return pltpu.make_async_remote_copy(
            src_ref=src, dst_ref=dst, send_sem=send_sem, recv_sem=recv_sem,
            device_id={"tensor": to}, device_id_type=MESH,
        )

    def partial_out(owner):
        start = pl.multiple_of(owner * rows, rows)
        return jnp.dot(
            att[pl.ds(start, rows), :], out_w[...], preferred_element_type=F32
        ).astype(BF16)

    copies = []
    for d in range(1, parts):
        to = lax.rem(me + d, parts)
        a_send[d] = partial_out(to)
        if d == 1:
            pl.semaphore_wait(barrier, parts - 1)
        copy = send(a_send.at[d], a_recv.at[d], as_sem.at[d], ar_sem.at[d], to)
        copy.start()
        copies.append(copy)
    total = partial_out(me).astype(F32)
    for d in range(1, parts):
        copies[d - 1].wait_recv()
        total += a_recv[d].astype(F32)
    middle = (tokens[...].astype(F32) + total).astype(BF16)
    a_send[0] = middle
    rows_v[0] = norm_rows(middle)
    sends = []
    for d in range(1, parts):
        copy = send(
            rows_v.at[0], rows_v.at[d], gs_sem.at[d], gr_sem.at[d], lax.rem(me + d, parts)
        )
        copy.start()
        sends.append(copy)
    for load in loads:
        load.wait()

    tile = 256 if units % 256 == 0 else units
    out_tile = 512
    backs = []
    for d in range(parts):
        if d > 0:
            sends[d - 1].wait_recv()

        def up(i, carry, d=d):
            if tile == units:
                at = slice(None)
            else:
                at = pl.ds(pl.multiple_of(i * tile, tile), tile)
            x = rows_v[d]
            gate = jnp.dot(x, gu_v[0, :, at], preferred_element_type=F32)
            raised = jnp.dot(x, gu_v[1, :, at], preferred_element_type=F32)
            hidden[:, at] = (gate / (1.0 + jnp.exp(-gate)) * raised).astype(BF16)
            return carry

        lax.fori_loop(0, units // tile, up, 0)

        def lower(i, carry, d=d):
            at = pl.ds(pl.multiple_of(i * out_tile, out_tile), out_tile)
            f_send[d, :, at] = jnp.dot(
                hidden[...], dn_v[:, at], preferred_element_type=F32
            ).astype(BF16)
            return carry

        lax.fori_loop(0, model // out_tile, lower, 0)
        if d > 0:
            owner = lax.rem(me + parts - d, parts)
            copy = send(f_send.at[d], f_recv.at[d], fs_sem.at[d], fr_sem.at[d], owner)
            copy.start()
            backs.append(copy)
    total = f_send[0].astype(F32)
    for d in range(1, parts):
        backs[d - 1].wait_recv()
        total += f_recv[d].astype(F32)
    result[...] = (a_send[0].astype(F32) + total).astype(BF16)
    for copy in copies + sends + backs:
        copy.wait_send()


def mlp_square_kernel(
    att, out_l, out_r, tokens, gate_up, down, result,
    gu_v, dn_v, att_v, mid_v, rows_v, f_v, f_in, hidden,
    w_sem, as_sem, ar_sem, gs_sem, gr_sem, fs_sem, fr_sem,
):
    parts = 4
    me = lax.axis_index("tensor")
    near_x, near_y, far = me + 1 - 2 * (me % 2), lax.rem(me + 2, parts), parts - 1 - me
    rows, model = tokens.shape
    half_rows = rows // 2
    units = hidden.shape[1]
    loads = [
        pltpu.make_async_copy(gate_up, gu_v, w_sem.at[0]),
        pltpu.make_async_copy(down, dn_v, w_sem.at[1]),
    ]
    for load in loads:
        load.start()
    barrier = pltpu.get_barrier_semaphore()
    for to in (near_x, near_y, far):
        pl.semaphore_signal(barrier, inc=1, device_id={"tensor": to}, device_id_type=MESH)
    pl.semaphore_wait(barrier, parts - 1)

    def send(src, dst, send_sem, recv_sem, to):
        return pltpu.make_async_remote_copy(
            src_ref=src, dst_ref=dst, send_sem=send_sem, recv_sem=recv_sem,
            device_id={"tensor": to}, device_id_type=MESH,
        )

    def cut(half):
        return pl.ds(half * half_rows, half_rows)

    def block_of(owner):
        return att.at[pl.ds(pl.multiple_of(owner * rows, rows), rows)]

    swaps = [
        send(block_of(to), att_v.at[slot], as_sem.at[slot], ar_sem.at[slot], to)
        for slot, to in ((3, far), (1, near_x), (2, near_y))
    ]
    for copy in swaps:
        copy.start()

    def group_term(block, slot):
        terms = [
            jnp.dot(block, weight[slot], preferred_element_type=F32).astype(BF16).astype(F32)
            for weight in (out_l, out_r)
        ]
        return jnp.concatenate(terms, axis=1)

    total = group_term(att[pl.ds(pl.multiple_of(me * rows, rows), rows), :], 0)
    for copy, slot in zip(swaps[1:] + swaps[:1], (1, 2, 3)):
        copy.wait_recv()
        total += group_term(att_v[slot], slot)
    middle = (tokens[...].astype(F32) + total).astype(BF16)
    mid_v[...] = middle
    rows_v[0] = norm_rows(middle)

    def piece(src, place, half, to):
        at = 2 * place + half - 2
        return send(
            rows_v.at[src, cut(half)], rows_v.at[place, cut(half)],
            gs_sem.at[at], gr_sem.at[at], to,
        )

    piece(0, 1, 0, near_x).start()
    piece(0, 2, 1, near_y).start()
    piece(0, 1, 1, near_x).start()
    piece(0, 2, 0, near_y).start()
    for load in loads:
        load.wait()

    tile = 256 if units % 256 == 0 else units
    out_tile = 512

    def feed(first, count):
        many = count * rows

        def up(i, carry):
            at = pl.ds(pl.multiple_of(i * tile, tile), tile)
            x = rows_v[first : first + count].reshape(many, model)
            gate = jnp.dot(x, gu_v[0, :, at], preferred_element_type=F32)
            raised = jnp.dot(x, gu_v[1, :, at], preferred_element_type=F32)
            hidden[0:many, at] = (gate / (1.0 + jnp.exp(-gate)) * raised).astype(BF16)
            return carry

        lax.fori_loop(0, units // tile, up, 0)

        def lower(i, carry):
            at = pl.ds(pl.multiple_of(i * out_tile, out_tile), out_tile)
            f_v[first : first + count, :, at] = (
                jnp.dot(hidden[0:many, :], dn_v[:, at], preferred_element_type=F32)
                .astype(BF16)
                .reshape(count, rows, out_tile)
            )
            return carry

        lax.fori_loop(0, model // out_tile, lower, 0)

    def back(slot, half, place, to):
        at = 2 * place + half
        return send(
            f_v.at[slot, cut(half)], f_in.at[place, cut(half)], fs_sem.at[at], fr_sem.at[at], to
        )

    feed(0, 1)
    piece(0, 1, 0, near_x).wait_recv()
    piece(1, 3, 0, near_y).start()
    piece(0, 2, 1, near_y).wait_recv()
    piece(2, 3, 1, near_x).start()
    piece(0, 1, 1, near_x).wait_recv()
    piece(0, 2, 0, near_y).wait_recv()
    feed(1, 2)
    back(1, 0, 0, near_x).start()
    back(2, 1, 1, near_y).start()
    piece(1, 3, 0, near_y).wait_recv()
    piece(2, 3, 1, near_x).wait_recv()
    feed(3, 1)
    back(3, 0, 2, near_x).start()
    back(3, 1, 2, near_y).start()
    for half, slot, place, to in ((0, 2, 1, near_y), (1, 1, 0, near_x)):
        back(3, half, 2, to).wait_recv()
        f_v[slot, cut(half)] = (
            f_v[slot, cut(half)].astype(F32) + f_in[2, cut(half)].astype(F32)
        ).astype(BF16)
        back(slot, half, place, to).start()
    order = ((1, 0, 0, near_x), (2, 1, 1, near_y), (2, 0, 1, near_y), (1, 1, 0, near_x))
    for slot, half, place, to in order:
        back(slot, half, place, to).wait_recv()
    total = f_v[0].astype(F32) + f_in[0].astype(F32) + f_in[1].astype(F32)
    result[...] = (mid_v[...].astype(F32) + total).astype(BF16)
    for copy in swaps:
        copy.wait_send()
    for place in (1, 2, 3):
        for half in range(2):
            piece(0, place, half, near_x).wait_send()
            back(1, half, place - 1, near_x).wait_send()


def mlp_square(att, out_l, out_r, tokens, gate_up, down, identity):
    rows, model = tokens.shape
    parts = 4
    dma = pltpu.SemaphoreType.DMA
    full = pltpu.VMEM((parts, rows, model), BF16)
    return pl.pallas_call(
        mlp_square_kernel,
        out_shape=jax.ShapeDtypeStruct((rows, model), BF16),
        in_specs=[VMEM, VMEM, VMEM, VMEM, ANY, ANY],
        out_specs=VMEM,
        scratch_shapes=[
            pltpu.VMEM(gate_up.shape, BF16),
            pltpu.VMEM(down.shape, BF16),
            pltpu.VMEM((parts, rows, att.shape[1]), BF16),
            pltpu.VMEM((rows, model), BF16),
            full, full,
            pltpu.VMEM((3, rows, model), BF16),
            pltpu.VMEM((2 * rows, down.shape[0]), BF16),
            dma((2,)), dma((parts,)), dma((parts,)),
        ]
        + [dma((6,))] * 4,
        compiler_params=pltpu.CompilerParams(
            collective_id=identity, has_side_effects=True, vmem_limit_bytes=52 * MIB
        ),
        name="mlp",
    )(att, out_l, out_r, tokens, gate_up, down)


def mlp(att, out_w, tokens, gate_up, down, parts, identity):
    rows, model = tokens.shape
    dma = pltpu.SemaphoreType.DMA
    full = pltpu.VMEM((parts, rows, model), BF16)
    return pl.pallas_call(
        functools.partial(mlp_kernel, parts),
        out_shape=jax.ShapeDtypeStruct((rows, model), BF16),
        in_specs=[VMEM, VMEM, VMEM, ANY, ANY],
        out_specs=VMEM,
        scratch_shapes=[
            pltpu.VMEM(gate_up.shape, BF16),
            pltpu.VMEM(down.shape, BF16),
            full, full, full, full, full,
            pltpu.VMEM((rows, down.shape[0]), BF16),
            dma((2,)),
        ]
        + [dma((parts,))] * 6,
        compiler_params=pltpu.CompilerParams(
            collective_id=identity, has_side_effects=True, vmem_limit_bytes=52 * MIB
        ),
        name="mlp",
    )(att, out_w, tokens, gate_up, down)


def on_device(
    tokens,
    lengths,
    group_prefix,
    prefix_cache,
    query_weight,
    key_weight,
    value_weight,
    out_weight,
    gate_up_weight,
    down_weight,
):
    parts = lax.axis_size("tensor")
    chips = lax.axis_size("dp") // 2
    heads = query_weight.shape[1] // HD

    most = most_crossing(group_prefix, chips)

    def routed(width, identity):
        def run(prefix, rows_in):
            return gather(
                group_prefix, rows_in, prefix, out_weight, parts, chips, width, identity
            )
        return run

    segment, kv, *gathered = lax.cond(
        most <= 2, routed(1, 0), routed(chips // 2, 1), prefix_cache, tokens
    )

    wq = query_weight
    if heads % 2:
        wq = jnp.pad(wq, ((0, 0), (0, HD)))

    def tile():
        return lax.axis_index("tensor") * heads // (QH // KVH) // 2

    att, *rest = attention(
        segment, wq, key_weight, value_weight, lengths, kv, out_weight, heads, tile, parts, 3
    )
    if parts == 4:
        return mlp_square(att, *gathered, *rest, tokens, gate_up_weight, down_weight, 2)
    out_w = out_weight
    if heads % 2:
        out_w = jnp.pad(out_w, ((0, HD), (0, 0)))
    return mlp(att, out_w, tokens, gate_up_weight, down_weight, parts, 2)


def solution(mesh):
    return jax.shard_map(
        on_device,
        mesh=mesh,
        in_specs=(
            P(("dp", "tensor"), None),
            P("dp", None),
            P(),
            P(("dp", "tensor"), None),
            P(None, "tensor"),
            P(),
            P(),
            P("tensor", None),
            P(None, None, "tensor"),
            P("tensor", None),
        ),
        out_specs=P(("dp", "tensor"), None),
        check_vma=False,
    )
```

```python
import functools
import math

import jax
import jax.numpy as jnp
from jax import lax
from jax.experimental import pallas as pl
from jax.experimental.pallas import tpu as pltpu
from jax.sharding import PartitionSpec as P

QH = 16
KVH = 4
HD = 64
PLEN = 4096
LANES = 128
SKEW = 3
NEG_FILL = -1e30
VMEM = pl.BlockSpec(memory_space=pltpu.VMEM)
SMEM = pl.BlockSpec(memory_space=pltpu.SMEM)
ANY = pl.BlockSpec(memory_space=pl.ANY)
MESH = pl.DeviceIdType.MESH
BF16 = jnp.bfloat16
F32 = jnp.float32
MIB = 1 << 20


def norm_rows(inputs):
    floats = inputs.astype(F32)
    mean = jnp.mean(floats * floats, axis=-1, keepdims=True)
    return (floats * lax.rsqrt(mean + 1e-05)).astype(BF16)


def most_crossing(group_prefix, chips):
    slots = jnp.arange(2 * chips, dtype=jnp.int32)
    wanted = group_prefix[None, :] == slots[:, None]
    final = jnp.max(jnp.where(wanted, slots[None, :], -1), axis=1)
    first = jnp.min(jnp.where(wanted, slots[None, :], 2 * chips), axis=1)
    edge = 2 * jnp.arange(1, chips, dtype=jnp.int32)[:, None]
    right = (slots[None, :] < edge) & (final[None, :] >= edge)
    left = (slots[None, :] >= edge) & (first[None, :] < edge)
    counts = jnp.sum(jnp.stack([right, left]).astype(jnp.int32), axis=2)
    return jnp.max(counts)


def route_choice(slot_ref, group, chips, width):
    number = 2 * chips
    chip, core = group // 2, group % 2
    held = [slot_ref[g] for g in range(number)]
    final, first = [], []
    for s in range(number):
        top, low = jnp.int32(-1), jnp.int32(number)
        for g in range(number):
            top = jnp.where(held[g] == s, g, top)
        for g in reversed(range(number)):
            low = jnp.where(held[g] == s, g, low)
        final.append(top)
        first.append(low)

    def ranks(needs):
        result, count = [], jnp.int32(0)
        for need in needs:
            result.append(count)
            count = count + need.astype(jnp.int32)
        return result

    def right(z):
        return [(s // 2 <= z) & (final[s] >= 2 * (z + 1)) for s in range(number)]

    def left(z):
        return [(s // 2 >= z) & (first[s] < 2 * z) for s in range(number)]

    from_left, from_right = ranks(right(chip - 1)), ranks(left(chip + 1))
    mine = slot_ref[group]
    keep = jnp.int32(0)
    sides = []
    for s in range(number):
        own = chip == s // 2
        value = jnp.where(
            own, s % 2, jnp.where(chip > s // 2, 2 + from_left[s], 2 + 2 * width + from_right[s])
        )
        keep = jnp.where(mine == s, value, keep)
    for needs, source in ((right(chip), from_left), (left(chip), from_right)):
        rank = ranks(needs)
        chosen = []
        for w in range(width):
            place = 2 * w + core
            value = jnp.int32(0)
            for s in range(number):
                value = jnp.where(
                    needs[s] & (rank[s] == place),
                    jnp.where(chip == s // 2, s % 2, 2 + source[s]),
                    value,
                )
            chosen.append(value)
        sides.append(chosen)
    return [keep] + sides[0] + sides[1]


def pick(number, candidates):
    result = candidates[0]
    for i in range(1, len(candidates)):
        result = jnp.where(number == i, candidates[i], result)
    return result


def gather_kernel(parts, chips, width, sub, *refs):
    if parts == 4:
        ow, ow_all, w_send, w_recv, share_send, share_recv = refs[3], refs[6], *refs[-4:]
        refs = refs[:3] + refs[4:6] + refs[7:-4]
    (
    slot_ref, tokens, prefix, segment, kv_out,
    packed, own, held_l, held_r, stage_r, stage_l, ag,
    ag_send, ag_recv, a2a_send, a2a_recv, own_send, own_recv,
    r_send, r_recv, l_send, l_recv, rf_send, rf_recv, lf_send, lf_recv,
    ) = refs
    me = lax.axis_index("tensor")
    group = lax.axis_index("dp")
    chip, core = group // 2, group % 2
    other = 1 - core
    sibling = chip * 2 + other
    groups = 2 * chips
    chunks = parts * sub
    chunk_rows = prefix.shape[0] // sub

    for ref in (held_l, held_r):
        ref[...] = jnp.zeros_like(ref)
    barrier = pltpu.get_barrier_semaphore()
    for d in range(1, parts):
        pl.semaphore_signal(
            barrier, inc=1, device_id={"tensor": lax.rem(me + d, parts)}, device_id_type=MESH
        )
    near = (sibling, lax.rem(group + 2, groups), lax.rem(group + groups - 2, groups))
    for to in near:
        pl.semaphore_signal(barrier, inc=1, device_id={"dp": to}, device_id_type=MESH)

    choice = route_choice(slot_ref, group, chips, width)
    rows_i = lax.broadcasted_iota(jnp.int32, (2 * KVH * HD, LANES), 0)
    cols_i = lax.broadcasted_iota(jnp.int32, (2 * KVH * HD, LANES), 1)
    source = cols_i + jnp.where(cols_i >= HD, KVH * HD - HD, 0)
    for h in range(KVH):
        take = (rows_i == source + h * HD).astype(F32).astype(BF16)
        packed[h] = (
            jnp.dot(prefix[...], take, preferred_element_type=F32)
            .astype(BF16)
            .reshape(sub, chunk_rows, LANES)
        )
    pl.semaphore_wait(barrier, parts - 1 + 3)

    copies = []
    for d in range(parts - 1, 0, -1):
        to = lax.rem(me + d, parts)
        copy = pltpu.make_async_remote_copy(
            src_ref=packed.at[to * KVH // parts],
            dst_ref=own.at[core, pl.ds((parts - d) * sub, sub)],
            send_sem=a2a_send.at[parts - d],
            recv_sem=a2a_recv.at[parts - d],
            device_id={"tensor": to},
            device_id_type=MESH,
        )
        copy.start()
        copies.append(copy)
    own[core, 0:sub] = packed[me * KVH // parts]

    ag[0] = norm_rows(tokens[...])
    def ag_copy(d):
        return pltpu.make_async_remote_copy(
            src_ref=ag.at[0],
            dst_ref=ag.at[d],
            send_sem=ag_send.at[d],
            recv_sem=ag_recv.at[d],
            device_id={"tensor": lax.rem(me + d, parts)},
            device_id_type=MESH,
        )

    def half_copy(slot, place, half, to):
        rows = tokens.shape[0] // 2
        at = pl.ds(half * rows, rows)
        return pltpu.make_async_remote_copy(
            src_ref=ag.at[slot, at],
            dst_ref=ag.at[place, at],
            send_sem=ag_send.at[2 * place + half - 2],
            recv_sem=ag_recv.at[2 * place + half - 2],
            device_id={"tensor": to},
            device_id_type=MESH,
        )

    near_x, near_y = me + 1 - 2 * (me % 2), lax.rem(me + 2, parts)

    def ag_start():
        if parts == 4:
            half_copy(0, 1, 0, near_x).start()
            half_copy(0, 2, 1, near_y).start()
            half_copy(0, 1, 1, near_x).start()
            half_copy(0, 2, 0, near_y).start()
        else:
            for d in range(1, parts):
                ag_copy(d).start()

    def ag_forward():
        if parts == 4:
            half_copy(0, 1, 0, near_x).wait_recv()
            half_copy(1, 3, 0, near_y).start()
            half_copy(0, 2, 1, near_y).wait_recv()
            half_copy(2, 3, 1, near_x).start()

    def ag_finish():
        segment[pl.ds(me, 1)] = ag[0:1]
        if parts == 4:
            half_copy(0, 1, 1, near_x).wait_recv()
            segment[pl.ds(near_x, 1)] = ag[1:2]
            half_copy(0, 2, 0, near_y).wait_recv()
            segment[pl.ds(near_y, 1)] = ag[2:3]
            half_copy(1, 3, 0, near_y).wait_recv()
            half_copy(2, 3, 1, near_x).wait_recv()
            segment[pl.ds(parts - 1 - me, 1)] = ag[3:4]
            for place, half in ((1, 0), (1, 1), (2, 0), (2, 1), (3, 0), (3, 1)):
                half_copy(0, place, half, near_x).wait_send()
        else:
            for d in range(1, parts):
                ag_copy(d).wait_recv()
                segment[pl.ds(lax.rem(me + parts - d, parts), 1)] = ag[d : d + 1]
            for d in range(1, parts):
                ag_copy(d).wait_send()

    def weight_piece(src, place, half, to):
        quarter, moved = ow.shape[0] // 4, ow_all.shape[2]
        at = pl.ds((2 * core + half) * quarter, quarter)
        return pltpu.make_async_remote_copy(
            src_ref=ow.at[at, 0:moved] if src == 0 else ow_all.at[src, at],
            dst_ref=ow_all.at[place, at],
            send_sem=w_send.at[2 * place + half - 2],
            recv_sem=w_recv.at[2 * place + half - 2],
            device_id={"tensor": to},
            device_id_type=MESH,
        )

    def share(place):
        quarter = ow.shape[0] // 4
        ref = ow_all.at[place, pl.ds(2 * core * quarter, 2 * quarter)]
        return pltpu.make_async_remote_copy(
            src_ref=ref, dst_ref=ref, send_sem=share_send.at[place - 1],
            recv_sem=share_recv.at[place - 1], device_id={"dp": sibling}, device_id_type=MESH,
        )

    def weight_start():
        weight_piece(0, 1, 0, near_x).start()
        weight_piece(0, 2, 1, near_y).start()
        weight_piece(0, 1, 1, near_x).start()
        weight_piece(0, 2, 0, near_y).start()
        ow_all[0] = ow[:, 0 : ow_all.shape[2]]

    def weight_forward():
        weight_piece(0, 1, 0, near_x).wait_recv()
        weight_piece(1, 3, 0, near_y).start()
        weight_piece(0, 2, 1, near_y).wait_recv()
        weight_piece(2, 3, 1, near_x).start()

    def weight_share():
        weight_piece(0, 1, 1, near_x).wait_recv()
        share(1).start()
        weight_piece(0, 2, 0, near_y).wait_recv()
        share(2).start()

    def weight_finish():
        weight_piece(1, 3, 0, near_y).wait_recv()
        weight_piece(2, 3, 1, near_x).wait_recv()
        share(3).start()

    def weight_end():
        for place in (1, 2, 3):
            share(place).wait_recv()
        for place in (1, 2, 3):
            share(place).wait_send()
            for half in range(2):
                weight_piece(0, place, half, near_x).wait_send()

    def lane_copy(src, dst, send_sem, recv_sem, to):
        return pltpu.make_async_remote_copy(
            src_ref=src, dst_ref=dst, send_sem=send_sem, recv_sem=recv_sem,
            device_id={"dp": to}, device_id_type=MESH,
        )

    def own_copy(m):
        block = own.at[core, pl.ds(m * sub, sub)]
        return lane_copy(block, block, own_send.at[m], own_recv.at[m], sibling)

    last = chips - 1

    def flow(place, to, base, held, stage, send, recv, f_send, f_recv):
        def hop(w, k):
            return lane_copy(
                stage.at[w, k], held.at[w * 2 + core, k], send.at[w, k], recv.at[w, k], to
            )

        def forward(w, k):
            ref = held.at[w * 2 + core, k]
            return lane_copy(ref, ref, f_send.at[w, k], f_recv.at[w, k], sibling)

        def comes(w):
            return (place > w) & (place <= last - w)

        def goes(w):
            return (place >= w) & (place < last - w)

        def receive(s):
            k = s - SKEW * place
            for w in range(width):
                @pl.when((k >= 0) & (k < chunks) & comes(w))
                def _(w=w):
                    hop(w, k).wait_recv()
                    forward(w, k).start()

        def pass_on(s):
            k = s - 1 - SKEW * place
            for w in range(width):
                @pl.when((k >= 0) & (k < chunks) & comes(w))
                def _(w=w):
                    forward(w, k).wait_recv()
            for w in range(width):
                @pl.when((k >= 0) & (k < chunks) & goes(w))
                def _(w=w):
                    stage[w, k] = pick(
                        choice[base + w],
                        [own[0, k], own[1, k]] + [held[i, k] for i in range(2 * width)],
                    )
                    hop(w, k).start()

        def drain(k):
            for w in range(width):
                @pl.when(goes(w))
                def _(w=w):
                    hop(w, k).wait_send()
                @pl.when(comes(w))
                def _(w=w):
                    forward(w, k).wait_send()

        return receive, pass_on, drain

    flows = (
        flow(chip, lax.rem(group + 2, groups), 1,
             held_l, stage_r, r_send, r_recv, rf_send, rf_recv),
        flow(last - chip, lax.rem(group + groups - 2, groups), 1 + width,
             held_r, stage_l, l_send, l_recv, lf_send, lf_recv),
    )

    def step(s, carry):
        m = s // sub

        @pl.when((m < parts) & (s % sub == 0))
        def _():
            @pl.when(m > 0)
            def _():
                pltpu.make_async_remote_copy(
                    src_ref=packed.at[0],
                    dst_ref=own.at[core, pl.ds(m * sub, sub)],
                    send_sem=a2a_send.at[m],
                    recv_sem=a2a_recv.at[m],
                    device_id={"tensor": lax.rem(me + 1, parts)},
                    device_id_type=MESH,
                ).wait_recv()

            own_copy(m).start()
            pl.when(m == 1)(ag_start)

        for receive, _, _ in flows:
            receive(s)
        before = s - 1

        @pl.when((before >= 0) & (before // sub < parts) & (before % sub == 0))
        def _():
            own_copy(before // sub).wait_recv()

        for _, pass_on, _ in flows:
            pass_on(s)
        if parts == 4:
            pl.when(s == 10)(ag_forward)
            pl.when(s == 10)(weight_start)
            pl.when(s == 19)(weight_forward)
            pl.when(s == 23)(weight_share)
        return carry

    lax.fori_loop(0, chunks + SKEW * last + 1, step, 0)

    if parts == 4:
        weight_finish()

    def finish(k, carry):
        kv_out[k] = pick(
            choice[0],
            [own[0, k], own[1, k]]
            + [held_l[i, k] for i in range(2 * width)]
            + [held_r[i, k] for i in range(2 * width)],
        )
        return carry

    lax.fori_loop(0, chunks, finish, 0)

    def drain(k, carry):
        for _, _, end in flows:
            end(k)
        return carry

    lax.fori_loop(0, chunks, drain, 0)
    for m in range(parts):
        own_copy(m).wait_send()
    for copy in copies:
        copy.wait_send()
    ag_finish()
    if parts == 4:
        weight_end()


def gather(slots, tokens, prefix, out_w, parts, chips, width, identity):
    rows, model = tokens.shape
    shard = prefix.shape[0]
    sub = 4 if shard >= 1024 else 2
    chunks = parts * sub
    piece = (chunks, shard // sub, LANES)
    dma = pltpu.SemaphoreType.DMA
    lane = [dma((width, chunks))] * 8
    shapes = [
        jax.ShapeDtypeStruct((parts, rows, model), BF16),
        jax.ShapeDtypeStruct(piece, BF16),
    ]
    operands = [slots, tokens, prefix]
    extra = []
    if parts == 4:
        operands.append(out_w)
        shapes.append(jax.ShapeDtypeStruct((parts, out_w.shape[0], model // 2), BF16))
        extra = [dma((6,))] * 2 + [dma((3,))] * 2
    segment, kv, *weight = pl.pallas_call(
        functools.partial(gather_kernel, parts, chips, width, sub),
        out_shape=shapes,
        in_specs=[SMEM] + [VMEM] * (len(operands) - 1),
        out_specs=[VMEM] * len(shapes),
        scratch_shapes=[
            pltpu.VMEM((KVH, sub, shard // sub, LANES), BF16),
            pltpu.VMEM((2,) + piece, BF16),
            pltpu.VMEM((2 * width,) + piece, BF16),
            pltpu.VMEM((2 * width,) + piece, BF16),
            pltpu.VMEM((width,) + piece, BF16),
            pltpu.VMEM((width,) + piece, BF16),
            pltpu.VMEM((parts, rows, model), BF16),
        ]
        + [dma((max(parts, 6),))] * 2
        + [dma((parts,))] * 4
        + lane
        + extra,
        compiler_params=pltpu.CompilerParams(
            collective_id=identity, has_side_effects=True, vmem_limit_bytes=52 * MIB
        ),
        name="gather",
    )(*operands)
    return [segment.reshape(parts * rows, model), kv.reshape(PLEN, LANES)] + weight


def attention_kernel(heads, parts, *refs):
    (x_ref, wq_ref, wk_ref, wv_ref, lengths, kv_ref) = refs[:6]
    if parts == 4:
        (ow, out_ref, ow_all, queries, keys, values, scores, begin_ref,
         w_send, w_recv, s_send, s_recv) = refs[6:]
        me = lax.axis_index("tensor")
        group = lax.axis_index("dp")
        core = group % 2
        sibling = group + 1 - 2 * core
        near_x, near_y = me + 1 - 2 * (me % 2), lax.rem(me + 2, parts)
        quarter, moved = ow.shape[0] // 4, ow_all.shape[2]

        def piece(src, place, half, to):
            at = pl.ds((2 * core + half) * quarter, quarter)
            return pltpu.make_async_remote_copy(
                src_ref=ow.at[at, pl.ds(moved, moved)] if src == 0 else ow_all.at[src, at],
                dst_ref=ow_all.at[place, at],
                send_sem=w_send.at[2 * place + half - 2],
                recv_sem=w_recv.at[2 * place + half - 2],
                device_id={"tensor": to},
                device_id_type=MESH,
            )

        def share(place):
            ref = ow_all.at[place, pl.ds(2 * core * quarter, 2 * quarter)]
            return pltpu.make_async_remote_copy(
                src_ref=ref, dst_ref=ref, send_sem=s_send.at[place - 1],
                recv_sem=s_recv.at[place - 1], device_id={"dp": sibling}, device_id_type=MESH,
            )

        barrier = pltpu.get_barrier_semaphore()
        for to in ({"tensor": near_x}, {"tensor": near_y}, {"dp": sibling}):
            pl.semaphore_signal(barrier, inc=1, device_id=to, device_id_type=MESH)
        pl.semaphore_wait(barrier, 3)
        piece(0, 1, 0, near_x).start()
        piece(0, 2, 1, near_y).start()
        piece(0, 1, 1, near_x).start()
        piece(0, 2, 0, near_y).start()
        ow_all[0] = ow[:, moved:]
    else:
        out_ref, queries, keys, values, scores, begin_ref = refs[6:]
    rows = x_ref.shape[0]
    lane = lax.broadcasted_iota(jnp.int32, (1, LANES), 1)
    former = (lane % HD) < HD // 2
    low = lane < HD

    def rotated(tile, cos_table, sin_table):
        swapped = jnp.where(
            former, -pltpu.roll(tile, LANES - HD // 2, 1), pltpu.roll(tile, HD // 2, 1)
        )
        return tile * cos_table + swapped * sin_table

    index = lax.broadcasted_iota(jnp.int32, (rows, LANES), 0)
    begins = jnp.zeros((rows, LANES), jnp.int32)
    start = jnp.int32(0)
    for r in range(lengths.shape[1]):
        begins = jnp.where(index >= start, start, begins)
        start = start + lengths[0, r]
    begin_ref[...] = begins
    steps_float = (lane % (HD // 2)).astype(F32)
    inverse = jnp.exp(steps_float * (-2.0 * math.log(10000.0) / HD))
    angles = (PLEN + index - begins).astype(F32) * inverse
    cos_table, sin_table = jnp.cos(angles), jnp.sin(angles)

    x = x_ref[...]
    mapped = jnp.dot(x, wq_ref[...], preferred_element_type=F32)
    for h in range(heads):
        if h % 2 == 0:
            tile = mapped[:, (h // 2) * LANES : (h // 2 + 1) * LANES]
            tile = rotated(tile, cos_table, sin_table).astype(BF16).astype(F32) * 0.125
            head = tile
        else:
            head = pltpu.roll(tile, HD, 1)
        queries[h] = jnp.where(low, head, 0.0).astype(BF16)
    is_odd = (lax.axis_index("tensor") * heads // (QH // KVH)) % 2 == 1
    new_k = jnp.dot(x, wk_ref[...], preferred_element_type=F32)
    new_v = jnp.dot(x, wv_ref[...], preferred_element_type=F32)
    new_k = rotated(new_k, cos_table, sin_table)
    new_k = jnp.where(is_odd, pltpu.roll(new_k, HD, 1), new_k)
    new_v = jnp.where(is_odd, new_v, pltpu.roll(new_v, HD, 1))
    pair = jnp.where(low, new_k, new_v)
    keys[0:PLEN, :] = kv_ref[...]
    keys[PLEN:, :] = pair.astype(BF16)
    values[...] = jnp.where(low, 1.0, keys[...].astype(F32)).astype(BF16)

    block = 256 if rows % 256 == 0 else rows
    step = 512
    total = PLEN + rows
    per_head = rows // block
    pairs = (heads + 1) // 2

    def one_head(h, start, slot):
        query = queries[h, pl.ds(start, block), :]
        top = jnp.full((block, LANES), NEG_FILL, F32)
        for n in range(total // step):
            part = lax.dot_general(
                query, keys[n * step : (n + 1) * step, :], (((1,), (1,)), ((), ())),
                preferred_element_type=F32,
            )
            if n * step >= PLEN:
                place = lax.broadcasted_iota(jnp.int32, (block, step), 1) + (n * step - PLEN)
                row = lax.broadcasted_iota(jnp.int32, (block, step), 0) + start
                seen = (place >= begin_ref[pl.ds(start, block), 0:1]) & (place <= row)
                part = jnp.where(seen, part, NEG_FILL)
            scores[slot, :, n * step : (n + 1) * step] = part
            for q in range(step // LANES):
                top = jnp.maximum(top, part[:, q * LANES : (q + 1) * LANES])
        top = jnp.max(top, axis=1, keepdims=True)
        blended = jnp.zeros((block, LANES), F32)
        for n in range(total // step):
            weight = jnp.exp(scores[slot, :, n * step : (n + 1) * step] - top).astype(BF16)
            blended += jnp.dot(
                weight, values[n * step : (n + 1) * step, :], preferred_element_type=F32
            )
        return blended

    def one(i, carry):
        if parts == 4:
            @pl.when(i == 1)
            def _():
                piece(0, 1, 0, near_x).wait_recv()
                piece(1, 3, 0, near_y).start()
                piece(0, 2, 1, near_y).wait_recv()
                piece(2, 3, 1, near_x).start()

            @pl.when(i == 2)
            def _():
                piece(0, 1, 1, near_x).wait_recv()
                share(1).start()
                piece(0, 2, 0, near_y).wait_recv()
                share(2).start()

            @pl.when(i == pairs * per_head - 1)
            def _():
                piece(1, 3, 0, near_y).wait_recv()
                piece(2, 3, 1, near_x).wait_recv()
                share(3).start()

        p, b = i // per_head, i % per_head
        start = pl.multiple_of(b * block, block)
        even = one_head(2 * p, start, 0)
        even = pltpu.roll(even, HD, 1) / even
        if heads > 1:
            odd = one_head(2 * p + 1, start, 1)
            odd = odd / pltpu.roll(odd, HD, 1)
        else:
            odd = jnp.zeros_like(even)
        at = pl.ds(pl.multiple_of(p * LANES, LANES), LANES)
        out_ref[pl.ds(start, block), at] = jnp.where(low, even, odd).astype(BF16)
        return carry

    lax.fori_loop(0, pairs * per_head, one, 0)
    if parts == 4:
        for place in (1, 2, 3):
            share(place).wait_recv()
        for place in (1, 2, 3):
            share(place).wait_send()
            for half in range(2):
                piece(0, place, half, near_x).wait_send()


def attention(x, wq, key_weight, value_weight, lengths, kv, out_w, heads, tile, parts, identity):
    rows = x.shape[0]
    total = PLEN + rows
    block = 256 if rows % 256 == 0 else rows
    columns = pl.BlockSpec((wq.shape[0], LANES), lambda i: (0, tile()))
    whole = lambda shape: pl.BlockSpec(shape, lambda i: (0,) * len(shape))
    shapes = [jax.ShapeDtypeStruct((rows, (heads + 1) // 2 * LANES), BF16)]
    operands = [x, wq, key_weight, value_weight, lengths, kv]
    specs = [whole(x.shape), whole(wq.shape), columns, columns]
    specs += [SMEM, whole(kv.shape)]
    scratch = [
        pltpu.VMEM((heads, rows, LANES), BF16),
        pltpu.VMEM((total, LANES), BF16),
        pltpu.VMEM((total, LANES), BF16),
        pltpu.VMEM((2, block, total), F32),
        pltpu.VMEM((rows, LANES), jnp.int32),
    ]
    params = dict(vmem_limit_bytes=52 * MIB)
    out_specs = [whole(shapes[0].shape)]
    if parts == 4:
        operands.append(out_w)
        specs.append(VMEM)
        shapes.append(jax.ShapeDtypeStruct((parts, out_w.shape[0], out_w.shape[1] // 2), BF16))
        out_specs.append(VMEM)
        scratch += [pltpu.SemaphoreType.DMA((6,))] * 2 + [pltpu.SemaphoreType.DMA((3,))] * 2
        params.update(collective_id=identity, has_side_effects=True)
    return pl.pallas_call(
        functools.partial(attention_kernel, heads, parts),
        grid=(1,),
        out_shape=shapes,
        in_specs=specs,
        out_specs=out_specs,
        scratch_shapes=scratch,
        compiler_params=pltpu.CompilerParams(**params),
        name="attention",
    )(*operands)


def mlp_kernel(
    parts, att, out_w, tokens, gate_up, down, result,
    gu_v, dn_v, a_send, a_recv, rows_v, f_send, f_recv, hidden,
    w_sem, as_sem, ar_sem, gs_sem, gr_sem, fs_sem, fr_sem,
):
    me = lax.axis_index("tensor")
    rows = tokens.shape[0]
    model = tokens.shape[1]
    units = hidden.shape[1]
    loads = [
        pltpu.make_async_copy(gate_up, gu_v, w_sem.at[0]),
        pltpu.make_async_copy(down, dn_v, w_sem.at[1]),
    ]
    for load in loads:
        load.start()
    barrier = pltpu.get_barrier_semaphore()
    for d in range(1, parts):
        pl.semaphore_signal(
            barrier, inc=1, device_id={"tensor": lax.rem(me + d, parts)}, device_id_type=MESH
        )

    def send(src, dst, send_sem, recv_sem, to):
        return pltpu.make_async_remote_copy(
            src_ref=src, dst_ref=dst, send_sem=send_sem, recv_sem=recv_sem,
            device_id={"tensor": to}, device_id_type=MESH,
        )

    def partial_out(owner):
        start = pl.multiple_of(owner * rows, rows)
        return jnp.dot(
            att[pl.ds(start, rows), :], out_w[...], preferred_element_type=F32
        ).astype(BF16)

    copies = []
    for d in range(1, parts):
        to = lax.rem(me + d, parts)
        a_send[d] = partial_out(to)
        if d == 1:
            pl.semaphore_wait(barrier, parts - 1)
        copy = send(a_send.at[d], a_recv.at[d], as_sem.at[d], ar_sem.at[d], to)
        copy.start()
        copies.append(copy)
    total = partial_out(me).astype(F32)
    for d in range(1, parts):
        copies[d - 1].wait_recv()
        total += a_recv[d].astype(F32)
    middle = (tokens[...].astype(F32) + total).astype(BF16)
    a_send[0] = middle
    rows_v[0] = norm_rows(middle)
    sends = []
    for d in range(1, parts):
        copy = send(
            rows_v.at[0], rows_v.at[d], gs_sem.at[d], gr_sem.at[d], lax.rem(me + d, parts)
        )
        copy.start()
        sends.append(copy)
    for load in loads:
        load.wait()

    tile = 256 if units % 256 == 0 else units
    out_tile = 512
    backs = []
    for d in range(parts):
        if d > 0:
            sends[d - 1].wait_recv()

        def up(i, carry, d=d):
            if tile == units:
                at = slice(None)
            else:
                at = pl.ds(pl.multiple_of(i * tile, tile), tile)
            x = rows_v[d]
            gate = jnp.dot(x, gu_v[0, :, at], preferred_element_type=F32)
            raised = jnp.dot(x, gu_v[1, :, at], preferred_element_type=F32)
            hidden[:, at] = (gate / (1.0 + jnp.exp(-gate)) * raised).astype(BF16)
            return carry

        lax.fori_loop(0, units // tile, up, 0)

        def lower(i, carry, d=d):
            at = pl.ds(pl.multiple_of(i * out_tile, out_tile), out_tile)
            f_send[d, :, at] = jnp.dot(
                hidden[...], dn_v[:, at], preferred_element_type=F32
            ).astype(BF16)
            return carry

        lax.fori_loop(0, model // out_tile, lower, 0)
        if d > 0:
            owner = lax.rem(me + parts - d, parts)
            copy = send(f_send.at[d], f_recv.at[d], fs_sem.at[d], fr_sem.at[d], owner)
            copy.start()
            backs.append(copy)
    total = f_send[0].astype(F32)
    for d in range(1, parts):
        backs[d - 1].wait_recv()
        total += f_recv[d].astype(F32)
    result[...] = (a_send[0].astype(F32) + total).astype(BF16)
    for copy in copies + sends + backs:
        copy.wait_send()


def mlp_square_kernel(
    att, out_l, out_r, tokens, gate_up, down, result,
    gu_v, dn_v, att_v, mid_v, rows_v, f_v, f_in, hidden,
    w_sem, as_sem, ar_sem, gs_sem, gr_sem, fs_sem, fr_sem,
):
    parts = 4
    me = lax.axis_index("tensor")
    near_x, near_y, far = me + 1 - 2 * (me % 2), lax.rem(me + 2, parts), parts - 1 - me
    rows, model = tokens.shape
    half_rows = rows // 2
    units = hidden.shape[1]
    loads = [
        pltpu.make_async_copy(gate_up, gu_v, w_sem.at[0]),
        pltpu.make_async_copy(down, dn_v, w_sem.at[1]),
    ]
    for load in loads:
        load.start()
    barrier = pltpu.get_barrier_semaphore()
    for to in (near_x, near_y, far):
        pl.semaphore_signal(barrier, inc=1, device_id={"tensor": to}, device_id_type=MESH)
    pl.semaphore_wait(barrier, parts - 1)

    def send(src, dst, send_sem, recv_sem, to):
        return pltpu.make_async_remote_copy(
            src_ref=src, dst_ref=dst, send_sem=send_sem, recv_sem=recv_sem,
            device_id={"tensor": to}, device_id_type=MESH,
        )

    def cut(half):
        return pl.ds(half * half_rows, half_rows)

    def block_of(owner):
        return att.at[pl.ds(pl.multiple_of(owner * rows, rows), rows)]

    swaps = [
        send(block_of(to), att_v.at[slot], as_sem.at[slot], ar_sem.at[slot], to)
        for slot, to in ((3, far), (1, near_x), (2, near_y))
    ]
    for copy in swaps:
        copy.start()

    def group_term(block, slot):
        terms = [
            jnp.dot(block, weight[slot], preferred_element_type=F32).astype(BF16).astype(F32)
            for weight in (out_l, out_r)
        ]
        return jnp.concatenate(terms, axis=1)

    total = group_term(att[pl.ds(pl.multiple_of(me * rows, rows), rows), :], 0)
    for copy, slot in zip(swaps[1:] + swaps[:1], (1, 2, 3)):
        copy.wait_recv()
        total += group_term(att_v[slot], slot)
    middle = (tokens[...].astype(F32) + total).astype(BF16)
    mid_v[...] = middle
    rows_v[0] = norm_rows(middle)

    def piece(src, place, half, to):
        at = 2 * place + half - 2
        return send(
            rows_v.at[src, cut(half)], rows_v.at[place, cut(half)],
            gs_sem.at[at], gr_sem.at[at], to,
        )

    piece(0, 1, 0, near_x).start()
    piece(0, 2, 1, near_y).start()
    piece(0, 1, 1, near_x).start()
    piece(0, 2, 0, near_y).start()
    for load in loads:
        load.wait()

    tile = 256 if units % 256 == 0 else units
    out_tile = 512

    def feed(first, count):
        many = count * rows

        def up(i, carry):
            at = pl.ds(pl.multiple_of(i * tile, tile), tile)
            x = rows_v[first : first + count].reshape(many, model)
            gate = jnp.dot(x, gu_v[0, :, at], preferred_element_type=F32)
            raised = jnp.dot(x, gu_v[1, :, at], preferred_element_type=F32)
            hidden[0:many, at] = (gate / (1.0 + jnp.exp(-gate)) * raised).astype(BF16)
            return carry

        lax.fori_loop(0, units // tile, up, 0)

        def lower(i, carry):
            at = pl.ds(pl.multiple_of(i * out_tile, out_tile), out_tile)
            f_v[first : first + count, :, at] = (
                jnp.dot(hidden[0:many, :], dn_v[:, at], preferred_element_type=F32)
                .astype(BF16)
                .reshape(count, rows, out_tile)
            )
            return carry

        lax.fori_loop(0, model // out_tile, lower, 0)

    def back(slot, half, place, to):
        at = 2 * place + half
        return send(
            f_v.at[slot, cut(half)], f_in.at[place, cut(half)], fs_sem.at[at], fr_sem.at[at], to
        )

    feed(0, 1)
    piece(0, 1, 0, near_x).wait_recv()
    piece(1, 3, 0, near_y).start()
    piece(0, 2, 1, near_y).wait_recv()
    piece(2, 3, 1, near_x).start()
    piece(0, 1, 1, near_x).wait_recv()
    piece(0, 2, 0, near_y).wait_recv()
    feed(1, 2)
    back(1, 0, 0, near_x).start()
    back(2, 1, 1, near_y).start()
    piece(1, 3, 0, near_y).wait_recv()
    piece(2, 3, 1, near_x).wait_recv()
    feed(3, 1)
    back(3, 0, 2, near_x).start()
    back(3, 1, 2, near_y).start()
    for half, slot, place, to in ((0, 2, 1, near_y), (1, 1, 0, near_x)):
        back(3, half, 2, to).wait_recv()
        f_v[slot, cut(half)] = (
            f_v[slot, cut(half)].astype(F32) + f_in[2, cut(half)].astype(F32)
        ).astype(BF16)
        back(slot, half, place, to).start()
    order = ((1, 0, 0, near_x), (2, 1, 1, near_y), (2, 0, 1, near_y), (1, 1, 0, near_x))
    for slot, half, place, to in order:
        back(slot, half, place, to).wait_recv()
    total = f_v[0].astype(F32) + f_in[0].astype(F32) + f_in[1].astype(F32)
    result[...] = (mid_v[...].astype(F32) + total).astype(BF16)
    for copy in swaps:
        copy.wait_send()
    for place in (1, 2, 3):
        for half in range(2):
            piece(0, place, half, near_x).wait_send()
            back(1, half, place - 1, near_x).wait_send()


def mlp_square(att, out_l, out_r, tokens, gate_up, down, identity):
    rows, model = tokens.shape
    parts = 4
    dma = pltpu.SemaphoreType.DMA
    full = pltpu.VMEM((parts, rows, model), BF16)
    return pl.pallas_call(
        mlp_square_kernel,
        out_shape=jax.ShapeDtypeStruct((rows, model), BF16),
        in_specs=[VMEM, VMEM, VMEM, VMEM, ANY, ANY],
        out_specs=VMEM,
        scratch_shapes=[
            pltpu.VMEM(gate_up.shape, BF16),
            pltpu.VMEM(down.shape, BF16),
            pltpu.VMEM((parts, rows, att.shape[1]), BF16),
            pltpu.VMEM((rows, model), BF16),
            full, full,
            pltpu.VMEM((3, rows, model), BF16),
            pltpu.VMEM((2 * rows, down.shape[0]), BF16),
            dma((2,)), dma((parts,)), dma((parts,)),
        ]
        + [dma((6,))] * 4,
        compiler_params=pltpu.CompilerParams(
            collective_id=identity, has_side_effects=True, vmem_limit_bytes=52 * MIB
        ),
        name="mlp",
    )(att, out_l, out_r, tokens, gate_up, down)


def mlp(att, out_w, tokens, gate_up, down, parts, identity):
    rows, model = tokens.shape
    dma = pltpu.SemaphoreType.DMA
    full = pltpu.VMEM((parts, rows, model), BF16)
    return pl.pallas_call(
        functools.partial(mlp_kernel, parts),
        out_shape=jax.ShapeDtypeStruct((rows, model), BF16),
        in_specs=[VMEM, VMEM, VMEM, ANY, ANY],
        out_specs=VMEM,
        scratch_shapes=[
            pltpu.VMEM(gate_up.shape, BF16),
            pltpu.VMEM(down.shape, BF16),
            full, full, full, full, full,
            pltpu.VMEM((rows, down.shape[0]), BF16),
            dma((2,)),
        ]
        + [dma((parts,))] * 6,
        compiler_params=pltpu.CompilerParams(
            collective_id=identity, has_side_effects=True, vmem_limit_bytes=52 * MIB
        ),
        name="mlp",
    )(att, out_w, tokens, gate_up, down)


def on_device(
    tokens,
    lengths,
    group_prefix,
    prefix_cache,
    query_weight,
    key_weight,
    value_weight,
    out_weight,
    gate_up_weight,
    down_weight,
):
    parts = lax.axis_size("tensor")
    chips = lax.axis_size("dp") // 2
    heads = query_weight.shape[1] // HD

    most = most_crossing(group_prefix, chips)

    def routed(width, identity):
        def run(prefix, rows_in):
            return gather(
                group_prefix, rows_in, prefix, out_weight, parts, chips, width, identity
            )
        return run

    segment, kv, *gathered = lax.cond(
        most <= 2, routed(1, 0), routed(chips // 2, 1), prefix_cache, tokens
    )

    wq = query_weight
    if heads % 2:
        wq = jnp.pad(wq, ((0, 0), (0, HD)))

    def tile():
        return lax.axis_index("tensor") * heads // (QH // KVH) // 2

    att, *rest = attention(
        segment, wq, key_weight, value_weight, lengths, kv, out_weight, heads, tile, parts, 3
    )
    if parts == 4:
        return mlp_square(att, *gathered, *rest, tokens, gate_up_weight, down_weight, 2)
    out_w = out_weight
    if heads % 2:
        out_w = jnp.pad(out_w, ((0, HD), (0, 0)))
    return mlp(att, out_w, tokens, gate_up_weight, down_weight, parts, 2)


def solution(mesh):
    return jax.shard_map(
        on_device,
        mesh=mesh,
        in_specs=(
            P(("dp", "tensor"), None),
            P("dp", None),
            P(),
            P(("dp", "tensor"), None),
            P(None, "tensor"),
            P(),
            P(),
            P("tensor", None),
            P(None, None, "tensor"),
            P("tensor", None),
        ),
        out_specs=P(("dp", "tensor"), None),
        check_vma=False,
    )
```
